32 devices in a mesh: dp: 16 (over z, y, x), ramp: 2 (over core).
Axes of the slice: x: 2, y: 2, z: 4, core: 2. Of those that a mesh axis runs over, the one named last changes fastest.
Arguments:
- hidden_in: bfloat16 [16384, 768], P(('dp', 'ramp')), may hold values from -10 to 10
- cotangent: bfloat16 [16384, 768], P(('dp', 'ramp')), may hold values from -6 to 6
- qkv_weight: bfloat16 [768, 2304], replicated, may hold values from -0.15625 to 0.15625
- query_bias: float32 [768], replicated, may hold values from -1.75 to 1.75
- value_bias: float32 [768], replicated, may hold values from -1.75 to 1.75
- output_weight: bfloat16 [768, 768], replicated, may hold values from -0.4375 to 0.4375
- output_bias: float32 [768], replicated, may hold values from -1.75 to 1.75
- first_scale: float32 [768], replicated, may hold values from 0.5 to 1.5
- first_shift: float32 [768], replicated, may hold values from -1.75 to 1.75
- inner_weight: bfloat16 [768, 3072], replicated, may hold values from -0.21875 to 0.21875
- inner_bias: float32 [3072], replicated, may hold values from -1.75 to 1.75
- outer_weight: bfloat16 [3072, 768], replicated, may hold values from -0.109375 to 0.109375
- outer_bias: float32 [768], replicated, may hold values from -1.75 to 1.75
- second_scale: float32 [768], replicated, may hold values from 0.5 to 1.5
- second_shift: float32 [768], replicated, may hold values from -1.75 to 1.75
- pool_weight: bfloat16 [2, 768, 768], P('ramp'), may hold values from -0.21875 to 0.21875
- pool_bias: float32 [2, 768], P('ramp'), may hold values from -1.75 to 1.75
- class_weight: bfloat16 [2, 768, 3], P('ramp'), may hold values from -0.4375 to 0.4375
- class_bias: float32 [2, 3], P('ramp'), may hold values from -3 to 3
- labels: int32 [128], P(('dp', 'ramp')), may hold values from 0 to 2
- ramp_index: int32 [128], P(('dp', 'ramp')), may hold values from 0 to 1, as said below
Outputs:
- output: bfloat16 [16384, 768], P(('dp', 'ramp'))
- logits: float32 [128, 3], P(('dp', 'ramp'))
- rms_values: float32 [3], replicated
- input_grad: bfloat16 [16384, 768], P(('dp', 'ramp'))
- qkv_weight_grad: float32 [768, 2304], P('dp', 'ramp')
- query_bias_grad: float32 [768], replicated
- value_bias_grad: float32 [768], replicated
- output_weight_grad: float32 [768, 768], P('dp', 'ramp')
- output_bias_grad: float32 [768], replicated
- first_scale_grad: float32 [768], replicated
- first_shift_grad: float32 [768], replicated
- inner_weight_grad: float32 [768, 3072], P('dp', 'ramp')
- inner_bias_grad: float32 [3072], replicated
- outer_weight_grad: float32 [3072, 768], P('dp', 'ramp')
- outer_bias_grad: float32 [768], replicated
- second_scale_grad: float32 [768], replicated
- second_shift_grad: float32 [768], replicated
- pool_weight_grad: float32 [2, 768, 768], P('ramp', 'dp')
- pool_bias_grad: float32 [2, 768], P('ramp')
- class_weight_grad: float32 [2, 768, 3], P('ramp')
- class_bias_grad: float32 [2, 3], P('ramp')
The draws below stay inside these ranges and needn't reach their ends.
Inputs may be any that keep to these rules, and one draw needn't show every extreme that they name: `ramp_index`: in every aligned block of 4 sequences (the sequences of one device) each off-ramp is named exactly 4 // 2 times.
All inputs are finite; a program needn't handle non-finite values.
Results may differ from the reference program's by a relative error of at most 0.015.
Values may be sent and summed in bfloat16 or wider, within the bound.
No kernel may reach another device: no remote copies, remote signals or barrier semaphores. Data moves between devices by JAX's collectives and lax.ppermute only.
A program may use at most 192 MiB of HBM per device.

```python
import math
import jax
import jax.numpy as jnp
from jax import lax

D = 768
FF = 3072
HEADS = 12
HEAD_DIM = 64
CLASSES = 3
LENGTH = 128
SEQ_DEV = 4
RAMPS = 2
SEQS = 128
TOKENS = 16384


def draw_hidden_in(key, part):
    key = jax.random.fold_in(key, 11)
    first_key = jax.random.fold_in(key, 0)
    position = jnp.arange(TOKENS, dtype=jnp.float32) / TOKENS
    row_scale = 0.8 + 1.6 * position
    base = jnp.clip(jax.random.normal(first_key, (TOKENS, D), jnp.float32), -4.0, 4.0)
    return (base * row_scale[:, None]).astype(jnp.bfloat16)


def draw_ramp_index(key, part):
    key = jax.random.fold_in(key, 7)
    noise = jax.random.randint(key, (SEQS // SEQ_DEV, SEQ_DEV), 0, 1 << 20)
    within = jnp.arange(SEQ_DEV, dtype=jnp.int32)[None, :]
    ranked = jnp.argsort(noise * SEQ_DEV + within, axis=1, stable=True).astype(jnp.int32)
    return (ranked % RAMPS).reshape(SEQS).astype(jnp.int32)


def place_ends(entries, key, least, high):
    spot = [jax.random.randint(jax.random.fold_in(key, axis), (), 0, length) for axis, length in enumerate(entries.shape)]
    longest = entries.shape.index(max(entries.shape))
    beside = spot[:longest] + [(spot[longest] + 1) % entries.shape[longest]] + spot[longest + 1:]
    return entries.at[tuple(spot)].set(least).at[tuple(beside)].set(high)


def block_levels(rng, dims, cuts, smallest, top_value):
    level = 1.0
    for dim, parts in cuts:
        draws = jax.random.uniform(jax.random.fold_in(jax.random.fold_in(rng, 6), dim), (parts,), jnp.float32, smallest / len(cuts), top_value / len(cuts))
        level = level * jnp.repeat(jnp.exp(draws), dims[dim] // parts).reshape((-1,) + (1,) * (len(dims) - 1 - dim))
    return level


def bell_draw(stream_key, dims, width, most, pieces=(), kind=jnp.bfloat16):
    array = jax.random.normal(stream_key, dims, jnp.float32) * width
    if len(pieces) > 0:
        array = block_levels(stream_key, dims, pieces, -0.22, 0.18) * array
    return jnp.clip(array, min=-most, max=most).astype(kind)


def setup_inputs(seed: int = 0) -> dict:
    splits = jax.random.split(jax.random.key(seed), 22)
    return {
        "hidden_in": draw_hidden_in(jax.random.fold_in(splits[21], 71), 0),
        "cotangent": bell_draw(splits[1], (TOKENS, D), 1.0, 6.0, ((0, 32),)),
        "qkv_weight": bell_draw(splits[2], (D, 3 * D), (2 * D) ** -0.5, 0.15625),
        "query_bias": bell_draw(splits[3], (D,), 0.3, 1.75, (), jnp.float32),
        "value_bias": bell_draw(splits[4], (D,), 0.3, 1.75, (), jnp.float32),
        "output_weight": bell_draw(splits[5], (D, D), (D // 4) ** -0.5, 0.4375),
        "output_bias": bell_draw(splits[6], (D,), 0.3, 1.75, (), jnp.float32),
        "first_scale": jnp.clip(1.0 + 0.1 * jax.random.normal(splits[7], (D,), jnp.float32), 0.5, 1.5),
        "first_shift": bell_draw(splits[8], (D,), 0.3, 1.75, (), jnp.float32),
        "inner_weight": bell_draw(splits[9], (D, FF), D ** -0.5, 0.21875),
        "inner_bias": bell_draw(splits[10], (FF,), 0.3, 1.75, (), jnp.float32),
        "outer_weight": bell_draw(splits[11], (FF, D), FF ** -0.5, 0.109375),
        "outer_bias": bell_draw(splits[12], (D,), 0.3, 1.75, (), jnp.float32),
        "second_scale": jnp.clip(1.0 + 0.1 * jax.random.normal(splits[13], (D,), jnp.float32), 0.5, 1.5),
        "second_shift": bell_draw(splits[14], (D,), 0.3, 1.75, (), jnp.float32),
        "pool_weight": bell_draw(splits[15], (RAMPS, D, D), D ** -0.5, 0.21875, ((0, 2),)),
        "pool_bias": bell_draw(splits[16], (RAMPS, D), 0.3, 1.75, ((0, 2),), jnp.float32),
        "class_weight": bell_draw(splits[17], (RAMPS, D, CLASSES), (D // 4) ** -0.5, 0.4375, ((0, 2),)),
        "class_bias": bell_draw(splits[18], (RAMPS, CLASSES), 0.5, 3.0, ((0, 2),), jnp.float32),
        "labels": place_ends(jax.random.randint(splits[19], (SEQS,), 0, CLASSES), jax.random.fold_in(splits[19], 1), 0, CLASSES - 1).astype(jnp.int32),
        "ramp_index": draw_ramp_index(jax.random.fold_in(splits[21], 71), 0),
    }


@jax.custom_vjp
def low(v):
    return lax.optimization_barrier(v.astype(jnp.bfloat16)).astype(jnp.float32)

@jax.custom_vjp
def low_back(v):
    return v

def low_keep(v):
    return (low(v), None)

def low_pass(kept, grad):
    return (grad,)

def back_keep(v):
    return (v, None)

def back_low(kept, grad):
    return (low(grad),)
low.defvjp(low_keep, low_pass)
low_back.defvjp(back_keep, back_low)
EPS = 1e-06
HIGH = lax.Precision.HIGHEST

def layer_norm(residual, scales, offset):
    centred = residual - lax.optimization_barrier(jnp.mean(residual, axis=-1, keepdims=True))
    spread = lax.optimization_barrier(jnp.mean(centred * centred, axis=-1, keepdims=True))
    return centred * lax.rsqrt(spread + EPS) * scales + offset

def block_forward(hidden, cot_rows, label_rows, ramp_rows, weights):
    qkv_weight, query_bias, value_bias, output_weight, output_bias, first_scale, first_shift, inner_weight, inner_bias, outer_weight, outer_bias, second_scale, second_shift, pool_weight, pool_bias, class_weight, class_bias = weights
    row_count = hidden.shape[0]
    seq_count = row_count // LENGTH
    mixed = jnp.dot(low(hidden), qkv_weight, precision=HIGH)
    queries = low(low_back(mixed[:, :D] + query_bias))
    key_rows = low(low_back(mixed[:, D:2 * D]))
    values = low(low_back(mixed[:, 2 * D:] + value_bias))
    split_shape = (seq_count, LENGTH, HEADS, HEAD_DIM)
    scores = jnp.einsum('bqhd,bkhd->bhqk', queries.reshape(split_shape), key_rows.reshape(split_shape), precision=HIGH) * HEAD_DIM ** (-0.5)
    scores = low_back(scores)
    probs = low(jax.nn.softmax(scores, axis=-1))
    context = jnp.einsum('bhqk,bkhd->bqhd', probs, values.reshape(split_shape), precision=HIGH).reshape(row_count, D)
    context = low(low_back(context))
    attended = low_back(jnp.dot(context, output_weight, precision=HIGH) + output_bias)
    first = layer_norm(hidden + attended, first_scale, first_shift)
    inner = low_back(jnp.dot(low(first), inner_weight, precision=HIGH) + inner_bias)
    acted = low(jax.nn.gelu(inner, approximate=False))
    outer = low_back(jnp.dot(acted, outer_weight, precision=HIGH) + outer_bias)
    final = layer_norm(first + outer, second_scale, second_shift)
    leading = low(final.reshape(seq_count, LENGTH, D)[:, 0])
    chosen = (ramp_rows[:, None] == jnp.arange(RAMPS)[None, :]).astype(jnp.float32)
    pre_all = jnp.einsum('gd,rde->gre', leading, pool_weight, precision=HIGH) + pool_bias[None]
    pre = low_back(lax.optimization_barrier(jnp.sum(chosen[:, :, None] * pre_all, axis=1)))
    pooled = low(jnp.tanh(pre))
    logit_all = jnp.einsum('gd,rdc->grc', pooled, class_weight, precision=HIGH) + class_bias[None]
    logits = lax.optimization_barrier(jnp.sum(chosen[:, :, None] * logit_all, axis=1))
    target = (label_rows[:, None] == jnp.arange(CLASSES)[None, :]).astype(jnp.float32)
    losses = jax.nn.logsumexp(logits, axis=-1) - lax.optimization_barrier(jnp.sum(target * logits, axis=-1))
    objective = jnp.sum(final * cot_rows) + jnp.sum(losses)
    squares = jnp.stack([jnp.sum(hidden * hidden), jnp.sum(attended * attended), jnp.sum(outer * outer)])
    return (objective, (final, logits, squares))

def reference(hidden_in, cotangent, qkv_weight, query_bias, value_bias, output_weight, output_bias, first_scale, first_shift, inner_weight, inner_bias, outer_weight, outer_bias, second_scale, second_shift, pool_weight, pool_bias, class_weight, class_bias, labels, ramp_index):
    params = tuple((weight_arg.astype(jnp.float32) for weight_arg in (qkv_weight, query_bias, value_bias, output_weight, output_bias, first_scale, first_shift, inner_weight, inner_bias, outer_weight, outer_bias, second_scale, second_shift, pool_weight, pool_bias, class_weight, class_bias)))
    group = math.gcd(SEQS, 32)
    turns = SEQS // group
    hidden_all = hidden_in.astype(jnp.float32).reshape(turns, group * LENGTH, D)
    cot_all = cotangent.astype(jnp.float32).reshape(turns, group * LENGTH, D)
    label_groups = labels.reshape(turns, group)
    ramp_groups = ramp_index.reshape(turns, group)

    def total(hidden_stack, weights):

        def one_turn(carry, slices):
            value, extra = block_forward(slices[0], slices[1], slices[2], slices[3], weights)
            return (carry + value, extra)
        return lax.scan(jax.checkpoint(one_turn), jnp.zeros((), jnp.float32), (hidden_stack, cot_all, label_groups, ramp_groups))
    objective, pullback, extras = jax.vjp(total, hidden_all, params, has_aux=True)
    input_grad, grads = pullback(jnp.ones_like(objective))
    final, logit_stack, square_stack = extras
    output = final.reshape(TOKENS, D).astype(jnp.bfloat16)
    logits = logit_stack.reshape(SEQS, CLASSES)
    rms_values = jnp.sqrt(lax.optimization_barrier(jnp.sum(square_stack, axis=0)) / (TOKENS * D))
    input_grad = input_grad.reshape(TOKENS, D).astype(jnp.bfloat16)
    return (output, logits, rms_values, input_grad, grads[0], grads[1], grads[2], grads[3], grads[4], grads[5], grads[6], grads[7], grads[8], grads[9], grads[10], grads[11], grads[12], grads[13], grads[14], grads[15], grads[16])
```

```python
from functools import partial

import jax
import jax.numpy as jnp
from jax import lax
from jax.experimental import pallas as pl
from jax.experimental.pallas import tpu as pltpu
from jax.sharding import PartitionSpec as P

HEADS = 12
CLASSES = 3
LANES = 128
EPS = 1e-06
F32 = jnp.float32
LOW = jnp.bfloat16
VMEM = pl.BlockSpec(memory_space=pltpu.VMEM)
SMEM = pl.BlockSpec(memory_space=pltpu.SMEM)
VMEM_BYTES = 56 * 1024 * 1024


def times(left, right):
    return lax.dot_general(left, right, (((1,), (0,)), ((), ())), preferred_element_type=F32)


def times_transposed(left, right):
    return lax.dot_general(left, right, (((1,), (1,)), ((), ())), preferred_element_type=F32)


def row_sum(values):
    return jnp.sum(values, axis=-1, keepdims=True)


def column_sum(values):
    return jnp.sum(values, axis=0, keepdims=True)


def call(body, outs, args, scratch=(), flops=0, specs=None, nbytes=0, transcendentals=0):
    return pl.pallas_call(
        body,
        out_shape=tuple(jax.ShapeDtypeStruct(shape, kind) for shape, kind in outs),
        in_specs=[VMEM] * len(args) if specs is None else specs,
        out_specs=tuple([VMEM] * len(outs)),
        scratch_shapes=list(scratch),
        compiler_params=pltpu.CompilerParams(vmem_limit_bytes=VMEM_BYTES),
        cost_estimate=pl.CostEstimate(
            flops=flops, bytes_accessed=nbytes, transcendentals=transcendentals
        ),
    )(*args)


class Place:
    def __init__(self, dp, rows):
        self.dp = dp
        self.planes = dp // 4
        self.fast = self.planes == 4 and rows % (16 * dp) == 0

    def position(self, block, index):
        if not self.fast:
            return block
        diff = block ^ index
        near = self.planes // 2
        far = ((diff >> 2) - 1) & (self.planes - 1)
        same_x = 1 - (diff & 1)
        same_y = 1 - ((diff >> 1) & 1)
        first = jnp.where(far < near, same_x * 2 + same_y, same_y * 2 + same_x)
        channel = jnp.where(far < near, 0, 1)
        return (channel * 4 + first) * near + (far & (near - 1))

    def store(self, ref, value, index, start, total):
        if not self.fast:
            ref[start : start + value.shape[0], :] = value
            return
        size = total // self.dp
        for step in range(value.shape[0] // size):
            block = start // size + step
            offset = pl.multiple_of(self.position(block, index) * size, 16)
            ref[pl.ds(offset, size), :] = value[step * size : (step + 1) * size, :]


def head_masks(rows):
    lane = lax.broadcasted_iota(jnp.int32, (rows, LANES), 1)
    left = (lane < LANES // 2).astype(F32).astype(LOW)
    right = (lane >= LANES // 2).astype(F32).astype(LOW)
    return left, right


def attention_forward(
    place, length,
    x_ref, qkv_ref, query_bias_ref, value_bias_ref, output_ref, output_bias_ref,
    mixed_ref, probs_ref, hidden_t_ref, context_t_ref, normal_ref, spread_ref, square_ref,
    context_ref, transposed_ref, sum_ref,
):
    rows, features = x_ref.shape
    index = lax.axis_index("dp")
    pairs = features // LANES
    factor = (features // HEADS) ** (-0.5)
    for part in range(3):
        columns = slice(part * features, (part + 1) * features)
        mixed = times(x_ref[...], qkv_ref[:, columns])
        if part == 0:
            mixed = mixed + query_bias_ref[...][None, :]
        if part == 2:
            mixed = mixed + value_bias_ref[...][None, :]
        mixed_ref[:, columns] = mixed.astype(LOW)
    place.store(hidden_t_ref, x_ref[...].T, index, 0, features)
    left, right = head_masks(length)
    left_t, right_t = left.T, right.T

    def one_sequence(seq, carry):
        here = pl.ds(pl.multiple_of(seq * length, length), length)
        for pair in range(pairs):
            start = pair * LANES
            query = mixed_ref[here, start : start + LANES]
            key = mixed_ref[here, features + start : features + start + LANES]
            value = mixed_ref[here, 2 * features + start : 2 * features + start + LANES]
            stacked = jnp.concatenate([query * left, query * right], axis=0)
            scores = times_transposed(key, stacked)
            top = jnp.max(scores, axis=0, keepdims=True)
            raised = jnp.exp((scores - top) * factor)
            probs = (raised * (1.0 / column_sum(raised))).astype(LOW)
            probs_ref[pl.ds(seq * pairs + pair, 1)] = probs[None]
            value_t = value.T
            both = jnp.concatenate([value_t * left_t, value_t * right_t], axis=1)
            tall = jnp.concatenate([probs[:, :length], probs[:, length:]], axis=0)
            context_t = times(both, tall).astype(LOW)
            transposed_ref[start : start + LANES, here] = context_t
            context_ref[here, start : start + LANES] = context_t.T
        return carry

    lax.fori_loop(0, rows // length, one_sequence, 0)
    place.store(context_t_ref, transposed_ref[...], index, 0, features)
    sum_ref[...] = times(context_ref[...], output_ref[...]) + output_bias_ref[...][None, :]

    def one_chunk(seq, carry):
        here = pl.ds(pl.multiple_of(seq * length, length), length)
        hidden = x_ref[here, :].astype(F32)
        attended = sum_ref[here, :]
        residual = hidden + attended
        centred = residual - row_sum(residual) * (1.0 / features)
        spread = lax.rsqrt(row_sum(centred * centred) * (1.0 / features) + EPS)
        normal_ref[here, :] = centred * spread
        spread_ref[here, :] = spread
        return (
            carry[0] + column_sum(hidden * hidden),
            carry[1] + column_sum(attended * attended),
        )

    zero = jnp.zeros((1, features), F32)
    hidden_square, attended_square = lax.fori_loop(0, rows // length, one_chunk, (zero, zero))
    square_ref[0:1, :] = hidden_square
    square_ref[1:2, :] = attended_square


def gelu_both(inner):
    density = jnp.exp(inner * inner * (-0.5)) * 0.3989422804014327
    below = 0.5 + 0.5 * lax.erf(inner * 0.7071067811865476)
    return inner * below, below + inner * density


def feed_forward(
    place, length, ramp_count,
    normal_ref, first_scale_ref, first_shift_ref, inner_ref, inner_bias_ref, outer_ref,
    outer_bias_ref, second_scale_ref, second_shift_ref, cot_ref, pool_own_ref, pool_other_ref,
    small_own_ref, small_other_ref, labels_ref, ramps_ref,
    output_ref, logits_ref, first_t_ref, acted_t_ref, slope_ref, resid_ref, outer_full_ref,
    outer_send_ref, outer_keep_ref, vector_ref, pair_own_ref, pair_send_ref,
    low_ref, sum_ref, spread_ref,
):
    rows, features = normal_ref.shape
    hidden_units = inner_ref.shape[1]
    seqs = rows // length
    index = lax.axis_index("dp")
    core = lax.axis_index("ramp")
    first = normal_ref[...] * first_scale_ref[...][None, :] + first_shift_ref[...][None, :]
    low_ref[...] = first.astype(LOW)
    sum_ref[...] = first + outer_bias_ref[...][None, :]
    place.store(first_t_ref, low_ref[...].T, index, 0, features)
    width = features
    for step in range(hidden_units // width):
        columns = slice(step * width, (step + 1) * width)
        inner = times(low_ref[...], inner_ref[:, columns])
        inner = inner + inner_bias_ref[columns][None, :]
        acted, slope = gelu_both(inner)
        acted = acted.astype(LOW)
        slope_ref[:, columns] = slope.astype(LOW)
        place.store(acted_t_ref, acted.T, index, step * width, hidden_units)
        sum_ref[...] += times(acted, outer_ref[columns, :])

    scale = second_scale_ref[...][None, :]
    shift = second_shift_ref[...][None, :]
    outer_bias = outer_bias_ref[...][None, :]
    square = jnp.zeros((1, features), F32)
    leading = []
    for seq in range(seqs):
        here = slice(seq * length, (seq + 1) * length)
        residual = sum_ref[here, :]
        first = normal_ref[here, :] * first_scale_ref[...][None, :] + first_shift_ref[...][None, :]
        outer = residual - first
        square = square + column_sum(outer * outer)
        centred = residual - row_sum(residual) * (1.0 / features)
        spread = lax.rsqrt(row_sum(centred * centred) * (1.0 / features) + EPS)
        normal = centred * spread
        sum_ref[here, :] = normal
        spread_ref[here, :] = spread
        final = (normal * scale + shift).astype(LOW)
        output_ref[here, :] = final
        leading.append(final[0:1, :].astype(F32))

    blank = 8 - seqs
    leading = jnp.concatenate(leading + [jnp.zeros((blank, features), F32)], axis=0)
    states = leading.astype(LOW)
    row = lax.broadcasted_iota(jnp.int32, (8, 1), 0)
    ramp_of = jnp.full((8, 1), -1, jnp.int32)
    label_of = jnp.full((8, 1), -1, jnp.int32)
    for seq in range(seqs):
        ramp_of = jnp.where(row == seq, ramps_ref[seq], ramp_of)
        label_of = jnp.where(row == seq, labels_ref[seq], label_of)
    own = ramp_of == core
    pre_own = times(states, pool_own_ref[0]) + small_own_ref[0:1, :]
    pre_other = times(states, pool_other_ref[0]) + small_other_ref[0:1, :]
    pooled = jnp.tanh(jnp.where(own, pre_own, pre_other))
    pooled_low = pooled.astype(LOW).astype(F32)
    chosen, logits = [], []
    for kind in range(CLASSES):
        chosen.append(
            jnp.where(own, small_own_ref[2 + kind : 3 + kind, :], small_other_ref[2 + kind : 3 + kind, :])
        )
        bias = jnp.where(own, small_own_ref[1:2, kind : kind + 1], small_other_ref[1:2, kind : kind + 1])
        logits.append(row_sum(pooled_low * chosen[kind]) + bias)
    top = jnp.maximum(jnp.maximum(logits[0], logits[1]), logits[2])
    raised = [jnp.exp(one - top) for one in logits]
    whole = raised[0] + raised[1] + raised[2]
    kind_at = lax.broadcasted_iota(jnp.int32, (8, LANES), 1)
    shown = jnp.zeros((8, LANES), F32)
    grads = []
    for kind in range(CLASSES):
        grads.append(raised[kind] / whole - (label_of == kind).astype(F32))
        shown = jnp.where(kind_at == kind, logits[kind], shown)
    logits_ref[...] = shown[:seqs, :CLASSES]
    pooled_grad = grads[0] * chosen[0] + grads[1] * chosen[1] + grads[2] * chosen[2]
    pre_low = (pooled_grad * (1.0 - pooled * pooled)).astype(LOW).astype(F32)
    pre_own_low = jnp.where(own, pre_low, 0.0).astype(LOW)
    pre_other_low = jnp.where(own, 0.0, pre_low).astype(LOW)
    state_grad = times_transposed(pre_own_low, pool_own_ref[0])
    state_grad = state_grad + times_transposed(pre_other_low, pool_other_ref[0])
    pair_own_ref[0:8, :] = states
    pair_own_ref[8:16, :] = pre_own_low
    pair_send_ref[0:8, :] = states
    pair_send_ref[8:16, :] = pre_other_low

    vector_ref[...] = jnp.zeros(vector_ref.shape, F32)
    wide_at = lax.broadcasted_iota(jnp.int32, (1, features), 1)
    for ramp in range(ramp_count):
        mask = (ramp_of == ramp).astype(F32)
        base = 8 * (ramp + 1)
        vector_ref[base : base + 1, :] = column_sum(pre_low * mask)
        bias_row = jnp.zeros((1, features), F32)
        for kind in range(CLASSES):
            vector_ref[base + 1 + kind : base + 2 + kind, :] = column_sum(
                pooled_low * (grads[kind] * mask)
            )
            bias_row = jnp.where(wide_at == kind, column_sum(grads[kind] * mask), bias_row)
        vector_ref[base + 4 : base + 5, :] = bias_row

    scale_grad = jnp.zeros((1, features), F32)
    shift_grad = jnp.zeros((1, features), F32)
    bias_grad = jnp.zeros((1, features), F32)
    at_first = lax.broadcasted_iota(jnp.int32, (length, 1), 0) == 0
    for seq in range(seqs):
        here = slice(seq * length, (seq + 1) * length)
        final_grad = cot_ref[here, :].astype(F32)
        final_grad = final_grad + jnp.where(at_first, state_grad[seq : seq + 1, :], 0.0)
        normal = sum_ref[here, :]
        scale_grad = scale_grad + column_sum(final_grad * normal)
        shift_grad = shift_grad + column_sum(final_grad)
        scaled = final_grad * scale
        resid = spread_ref[here, :] * (
            scaled
            - row_sum(scaled) * (1.0 / features)
            - normal * (row_sum(scaled * normal) * (1.0 / features))
        )
        resid_ref[here, :] = resid
        low = resid.astype(LOW)
        outer_full_ref[here, :] = low
        bias_grad = bias_grad + column_sum(low.astype(F32))
    vector_ref[0:1, :] = bias_grad
    vector_ref[1:2, :] = scale_grad
    vector_ref[2:3, :] = shift_grad
    vector_ref[3:4, :] = square
    half = features // 2
    outer_send_ref[...] = outer_full_ref[:, pl.ds(pl.multiple_of((1 - core) * half, LANES), half)]
    outer_keep_ref[...] = outer_full_ref[:, pl.ds(pl.multiple_of(core * half, LANES), half)]


def feed_backward(
    length,
    outer_full_ref, slope_ref, outer_ref, inner_ref, resid_ref, normal_ref, spread_ref,
    first_scale_ref, output_ref,
    inner_send_ref, inner_keep_ref, attended_send_ref, attended_keep_ref, context_grad_ref,
    first_resid_ref, vector_ref,
    sum_ref, low_ref,
):
    rows, features = resid_ref.shape
    core = lax.axis_index("ramp")
    width = features
    parts = slope_ref.shape[1] // width // 2
    sum_ref[...] = resid_ref[...]
    vector_ref[...] = jnp.zeros(vector_ref.shape, F32)
    for kept in (False, True):
        target = inner_keep_ref if kept else inner_send_ref
        which = core if kept else 1 - core
        for part in range(parts):
            number = which * parts + part
            columns = pl.ds(pl.multiple_of(number * width, LANES), width)
            acted_grad = times_transposed(outer_full_ref[...], outer_ref[columns, :])
            inner_grad = (slope_ref[:, columns].astype(F32) * acted_grad).astype(LOW)
            target[:, part * width : (part + 1) * width] = inner_grad
            vector_ref[pl.ds(number + 3, 1), :] = column_sum(inner_grad.astype(F32))
            sum_ref[...] += times_transposed(inner_grad, inner_ref[:, columns])
    scale = first_scale_ref[...][None, :]

    def one_chunk(seq, carry):
        here = pl.ds(pl.multiple_of(seq * length, length), length)
        first_grad = sum_ref[here, :]
        normal = normal_ref[here, :]
        scaled = first_grad * scale
        resid = spread_ref[here, :] * (
            scaled
            - row_sum(scaled) * (1.0 / features)
            - normal * (row_sum(scaled * normal) * (1.0 / features))
        )
        first_resid_ref[here, :] = resid
        low = resid.astype(LOW)
        low_ref[here, :] = low
        return (
            carry[0] + column_sum(low.astype(F32)),
            carry[1] + column_sum(first_grad * normal),
            carry[2] + column_sum(first_grad),
        )

    zero = jnp.zeros((1, features), F32)
    sums = lax.fori_loop(0, rows // length, one_chunk, (zero, zero, zero))
    for place, one in enumerate(sums):
        vector_ref[place : place + 1, :] = one
    context_grad_ref[...] = times_transposed(low_ref[...], output_ref[...]).astype(LOW)
    half = features // 2
    attended_send_ref[...] = low_ref[:, pl.ds(pl.multiple_of((1 - core) * half, LANES), half)]
    attended_keep_ref[...] = low_ref[:, pl.ds(pl.multiple_of(core * half, LANES), half)]


def attention_backward(
    length,
    mixed_ref, probs_ref, context_grad_ref,
    grad_ref, send_ref, keep_ref, vector_ref,
):
    rows, features = context_grad_ref.shape
    core = lax.axis_index("ramp")
    pairs = features // LANES
    factor = (features // HEADS) ** (-0.5)
    left, right = head_masks(length)

    def one_sequence(seq, carry):
        here = pl.ds(pl.multiple_of(seq * length, length), length)
        for pair in range(pairs):
            start = pair * LANES
            query = mixed_ref[here, start : start + LANES]
            key = mixed_ref[here, features + start : features + start + LANES]
            value = mixed_ref[here, 2 * features + start : 2 * features + start + LANES]
            context_grad = context_grad_ref[here, start : start + LANES]
            queries = jnp.concatenate([query * left, query * right], axis=0)
            keys = jnp.concatenate([key * left, key * right], axis=0)
            grads = jnp.concatenate([context_grad * left, context_grad * right], axis=0)
            probs = probs_ref[pl.ds(seq * pairs + pair, 1)][0]
            probs_grad = times_transposed(value, grads)
            wide = probs.astype(F32)
            score_grad = wide * (probs_grad - column_sum(wide * probs_grad))
            score_grad = score_grad.astype(LOW)
            value_grad = times(probs, grads).astype(LOW)
            key_grad = (times(score_grad, queries) * factor).astype(LOW)
            turned = jnp.concatenate(
                [score_grad[:, :length].T, score_grad[:, length:].T], axis=1
            )
            query_grad = (times(turned, keys) * factor).astype(LOW)
            grad_ref[here, start : start + LANES] = query_grad
            grad_ref[here, features + start : features + start + LANES] = key_grad
            grad_ref[here, 2 * features + start : 2 * features + start + LANES] = value_grad
        return carry

    lax.fori_loop(0, rows // length, one_sequence, 0)
    vector_ref[...] = jnp.zeros(vector_ref.shape, F32)
    vector_ref[0:1, :] = column_sum(grad_ref[:, :features].astype(F32))
    vector_ref[1:2, :] = column_sum(grad_ref[:, 2 * features :].astype(F32))
    half = grad_ref.shape[1] // 2
    send_ref[...] = grad_ref[:, pl.ds(pl.multiple_of((1 - core) * half, LANES), half)]
    keep_ref[...] = grad_ref[:, pl.ds(pl.multiple_of(core * half, LANES), half)]


def weight_gradient(count, *refs):
    operands, results = refs[: 4 * count], refs[4 * count :]
    start = 0
    for number in range(count):
        own_ref, other_ref, keep_ref, got_ref = operands[4 * number : 4 * number + 4]
        height = own_ref.shape[0]
        width = keep_ref.shape[1]
        quarter = height // len(results)
        tall = 768
        across = 384
        for top in range(0, height, tall):
            for column in range(0, width, across):
                columns = slice(column, column + across)
                total = times(own_ref[top : top + tall, :], keep_ref[:, columns])
                total = total + times(other_ref[top : top + tall, :], got_ref[:, columns])
                total = total.astype(LOW)
                for row in range(top, top + tall, min(quarter, tall)):
                    size = min(quarter, tall)
                    inside = row % quarter
                    results[row // quarter][
                        inside : inside + size, start + column : start + column + across
                    ] = total[row - top : row - top + size, :]
        start += width


def add_halves(got_x_ref, keep_x_ref, got_y_ref, keep_y_ref, *results):
    for got_ref, keep_ref, first_ref, second_ref in (
        (got_x_ref, keep_x_ref, results[0], results[1]),
        (got_y_ref, keep_y_ref, results[2], results[3]),
    ):
        half = got_ref.shape[0] // 2
        total = got_ref[...].astype(F32) + keep_ref[...].astype(F32)
        total = total.astype(LOW)
        first_ref[...] = total[:half, :]
        second_ref[...] = total[half:, :]


def add_last(widths, one_ref, two_ref, three_ref, own_ref, *results):
    total = one_ref[...].astype(F32) + two_ref[...].astype(F32)
    total = total + (three_ref[...].astype(F32) + own_ref[...].astype(F32))
    start = 0
    for width, result in zip(widths, results):
        result[...] = total[:, start : start + width]
        start += width


def input_gradient(grad_ref, qkv_ref, resid_ref, result_ref):
    result_ref[...] = (
        resid_ref[...] + times_transposed(grad_ref[...], qkv_ref[...])
    ).astype(LOW)


def shift(values, mask):
    dp = lax.axis_size("dp")
    return lax.ppermute(values, "dp", [(one, one ^ mask) for one in range(dp)])


def swap_core(values):
    return lax.ppermute(values, "ramp", [(0, 1), (1, 0)])


def reduce_scatter(place, quarters, widths):
    dp = place.dp
    if not place.fast:
        rows = lax.psum_scatter(quarters[0], "dp", scatter_dimension=0, tiled=True).astype(F32)
        ends = [sum(widths[: one + 1]) for one in range(len(widths))]
        return [rows[:, end - width : end] for width, end in zip(widths, ends)]
    send_x, keep_x, send_y, keep_y = quarters
    height, width = send_x.shape
    got_x = shift(send_x, 1)
    got_y = shift(send_y, 2)
    half = ((height // 2, width), LOW)
    send_x, keep_x, send_y, keep_y = call(
        add_halves, [half] * 4, (got_x, keep_x, got_y, keep_y), nbytes=12 * height * width
    )
    got_x = shift(send_x, 2)
    got_y = shift(send_y, 1)
    block = ((height // 4, width), LOW)
    one, two, three, own = call(
        add_halves, [block] * 4, (got_x, keep_x, got_y, keep_y), nbytes=6 * height * width
    )
    one = shift(one, 1 << 2)
    two = shift(two, 2 << 2)
    three = shift(three, 3 << 2)
    return call(
        partial(add_last, widths),
        [((height // 4, one_width), F32) for one_width in widths],
        (one, two, three, own),
        nbytes=3 * height * width,
    )


def on_device(
    hidden_in, cotangent, qkv_weight, query_bias, value_bias, output_weight, output_bias,
    first_scale, first_shift, inner_weight, inner_bias, outer_weight, outer_bias,
    second_scale, second_shift, pool_weight, pool_bias, class_weight, class_bias,
    labels, ramp_index,
):
    rows, features = hidden_in.shape
    seqs = labels.shape[0]
    length = rows // seqs
    units = inner_weight.shape[1]
    dp = lax.axis_size("dp")
    ramps = lax.axis_size("ramp")
    pairs = features // LANES
    place = Place(dp, features)
    half = features // 2

    pool_other = swap_core(pool_weight)
    small = jnp.concatenate(
        [
            pool_bias,
            jnp.pad(class_bias, ((0, 0), (0, features - CLASSES))),
            class_weight[0].astype(F32).T,
            jnp.zeros((3, features), F32),
        ]
    )
    small_other = swap_core(small)

    mixed, probs, hidden_t, context_t, normal, spread, squares = call(
        partial(attention_forward, place, length),
        [
            ((rows, 3 * features), LOW),
            ((seqs * pairs, length, 2 * length), LOW),
            ((features, rows), LOW),
            ((features, rows), LOW),
            ((rows, features), F32),
            ((rows, 1), F32),
            ((2, features), F32),
        ],
        (hidden_in, qkv_weight, query_bias, value_bias, output_weight, output_bias),
        scratch=[
            pltpu.VMEM((rows, features), LOW),
            pltpu.VMEM((features, rows), LOW),
            pltpu.VMEM((rows, features), F32),
        ],
        flops=2 * rows * features * 4 * features + 8 * rows * features * length,
        nbytes=16 << 20,
    )
    hidden_t_other = swap_core(hidden_t)
    context_t_other = swap_core(context_t)

    (
        output, logits, first_t, acted_t, slope, second_resid, outer_full,
        outer_send, outer_keep, second_vector, pair_own, pair_send,
    ) = call(
        partial(feed_forward, place, length, ramps),
        [
            ((rows, features), LOW),
            ((seqs, CLASSES), F32),
            ((features, rows), LOW),
            ((units, rows), LOW),
            ((rows, units), LOW),
            ((rows, features), F32),
            ((rows, features), LOW),
            ((rows, half), LOW),
            ((rows, half), LOW),
            ((8 * (ramps + 1), features), F32),
            ((16, features), LOW),
            ((16, features), LOW),
        ],
        (
            normal, first_scale, first_shift, inner_weight, inner_bias, outer_weight, outer_bias,
            second_scale, second_shift, cotangent, pool_weight, pool_other, small, small_other,
            labels, ramp_index,
        ),
        specs=[VMEM] * 14 + [SMEM] * 2,
        scratch=[
            pltpu.VMEM((rows, features), LOW),
            pltpu.VMEM((rows, features), F32),
            pltpu.VMEM((rows, 1), F32),
        ],
        flops=4 * rows * features * units,
        nbytes=30 << 20,
    )
    acted_t_other = swap_core(acted_t)
    outer_got = swap_core(outer_send)
    first_t_other = swap_core(first_t)
    pair_other = swap_core(pair_send)

    (
        inner_send, inner_keep, attended_send, attended_keep, context_grad, first_resid, first_vector,
    ) = call(
        partial(feed_backward, length),
        [
            ((rows, units // 2), LOW),
            ((rows, units // 2), LOW),
            ((rows, half), LOW),
            ((rows, half), LOW),
            ((rows, features), LOW),
            ((rows, features), F32),
            ((8, features), F32),
        ],
        (
            outer_full, slope, outer_weight, inner_weight, second_resid, normal, spread,
            first_scale, output_weight,
        ),
        scratch=[pltpu.VMEM((rows, features), F32), pltpu.VMEM((rows, features), LOW)],
        flops=4 * rows * features * units + 2 * rows * features * features,
        nbytes=25 << 20,
    )
    inner_got = swap_core(inner_send)
    attended_got = swap_core(attended_send)

    splits = 4 if place.fast else 1

    def gradient(parts, height):
        width = sum(part[2].shape[1] for part in parts)
        return call(
            partial(weight_gradient, len(parts)),
            [((height // splits, width), LOW)] * splits,
            [one for part in parts for one in part],
            flops=4 * rows * height * width,
            nbytes=12 << 20,
        )

    outer_quarters = gradient([(acted_t, acted_t_other, outer_keep, outer_got)], units)
    (outer_sum,) = reduce_scatter(place, outer_quarters, [half])

    inner_quarters = gradient(
        [
            (first_t, first_t_other, inner_keep, inner_got),
            (context_t, context_t_other, attended_keep, attended_got),
        ],
        features,
    )
    inner_sum, output_sum = reduce_scatter(place, inner_quarters, [units // 2, half])

    mixed_grad, mixed_send, mixed_keep, mixed_vector = call(
        partial(attention_backward, length),
        [
            ((rows, 3 * features), LOW),
            ((rows, 3 * half), LOW),
            ((rows, 3 * half), LOW),
            ((8, features), F32),
        ],
        (mixed, probs, context_grad),
        flops=20 * rows * features * length,
        nbytes=12 << 20,
    )
    mixed_got = swap_core(mixed_send)
    qkv_quarters = gradient([(hidden_t, hidden_t_other, mixed_keep, mixed_got)], features)
    (qkv_sum,) = reduce_scatter(place, qkv_quarters, [3 * half])
    (input_grad,) = call(
        input_gradient,
        [((rows, features), LOW)],
        (mixed_grad, qkv_weight, first_resid),
        flops=6 * rows * features * features,
        nbytes=10 << 20,
    )

    pair = jnp.stack([pair_own, pair_other]).reshape(1, 4, 8, features)
    pair = lax.all_to_all(
        jnp.broadcast_to(pair, (dp, 4, 8, features)), "dp", split_axis=0, concat_axis=0, tiled=True
    )
    index = lax.axis_index("dp")
    states = pair[:, 0::2].reshape(dp * 16, features)
    pre_grads = pair[:, 1::2].reshape(dp * 16, features)
    own_rows = features // dp
    states = lax.dynamic_slice_in_dim(states, index * own_rows, own_rows, axis=1)
    pool_sum = lax.dot_general(
        states, pre_grads, (((0,), (0,)), ((), ())), preferred_element_type=F32
    )

    vectors = jnp.concatenate(
        [mixed_vector, first_vector, second_vector, jnp.pad(squares, ((0, 6), (0, 0)))]
    )
    vectors = vectors + swap_core(vectors)
    count = vectors.shape[0]
    piece = lax.all_to_all(
        vectors.reshape(dp, -1), "dp", split_axis=0, concat_axis=0, tiled=True
    ).sum(axis=0)
    vectors = lax.all_to_all(
        jnp.broadcast_to(piece[None], (dp, piece.shape[0])),
        "dp", split_axis=0, concat_axis=0, tiled=True,
    ).reshape(count, features)
    entries = rows * features * dp * ramps
    rms = jnp.sqrt(
        jnp.sum(jnp.stack([vectors[count - 8], vectors[count - 7], vectors[19]]), axis=1) / entries
    )
    mine = lax.dynamic_slice_in_dim(vectors, 24 + 8 * lax.axis_index("ramp"), 8, axis=0)
    return (
        output,
        logits,
        rms,
        input_grad,
        qkv_sum,
        vectors[0],
        vectors[1],
        output_sum,
        vectors[8],
        vectors[9],
        vectors[10],
        inner_sum,
        vectors[11 : 11 + units // features].reshape(units),
        outer_sum,
        vectors[16],
        vectors[17],
        vectors[18],
        pool_sum[None],
        mine[0:1],
        mine[1:4].T[None],
        mine[4:5, :CLASSES],
    )


def solution(mesh):
    whole = P(("dp", "ramp"), None)
    return jax.shard_map(
        on_device,
        mesh=mesh,
        in_specs=(whole, whole)
        + (P(),) * 13
        + (
            P("ramp", None, None),
            P("ramp", None),
            P("ramp", None, None),
            P("ramp", None),
            P(("dp", "ramp")),
            P(("dp", "ramp")),
        ),
        out_specs=(
            whole,
            whole,
            P(),
            whole,
            P("dp", "ramp"),
            P(),
            P(),
            P("dp", "ramp"),
            P(),
            P(),
            P(),
            P("dp", "ramp"),
            P(),
            P("dp", "ramp"),
            P(),
            P(),
            P(),
            P("ramp", "dp", None),
            P("ramp", None),
            P("ramp", None, None),
            P("ramp", None),
        ),
        check_vma=False,
    )
```

```python
from functools import partial

import jax
import jax.numpy as jnp
from jax import lax
from jax.experimental import pallas as pl
from jax.experimental.pallas import tpu as pltpu
from jax.sharding import PartitionSpec as P

HEADS = 12
CLASSES = 3
LANES = 128
EPS = 1e-06
F32 = jnp.float32
LOW = jnp.bfloat16
NEAR = pl.BlockSpec(memory_space=pltpu.VMEM)
VMEM = pltpu.VMEM
SMEM = pltpu.SMEM
FAR = pl.BlockSpec(memory_space=pl.ANY)
VMEM_BYTES = 60 * 1024 * 1024
SMALL_BYTES = 16 * 1024 * 1024


def times(left, right):
    return lax.dot_general(left, right, (((1,), (0,)), ((), ())), preferred_element_type=F32)


def times_transposed(left, right):
    return lax.dot_general(left, right, (((1,), (1,)), ((), ())), preferred_element_type=F32)


def first_times(left, right):
    return lax.dot_general(left, right, (((0,), (0,)), ((), ())), preferred_element_type=F32)


def row_sum(values):
    return jnp.sum(values, axis=-1, keepdims=True)


def column_sum(values):
    return jnp.sum(values, axis=0, keepdims=True)


def call(body, outs, args, scratch=(), flops=0, nbytes=0, limit=VMEM_BYTES):
    near_in = [number for number, (_, spec) in enumerate(args) if spec in (VMEM, SMEM)]
    near_out = [number for number, (_, _, spec) in enumerate(outs) if spec in (VMEM, SMEM)]
    copies = [args[number][1](args[number][0].shape, args[number][0].dtype) for number in near_in]
    copies += [outs[number][2](outs[number][0], outs[number][1]) for number in near_out]

    def kernel(*refs):
        ins, refs = list(refs[: len(args)]), refs[len(args) :]
        results, refs = list(refs[: len(outs)]), refs[len(outs) :]
        own, refs = refs[: len(scratch)], refs[len(scratch) :]
        held, sems = refs[:-1], refs[-1]
        moving = []
        for place, number in enumerate(near_in):
            moving.append(pltpu.make_async_copy(ins[number], held[place], sems.at[place]))
            ins[number] = held[place]
        for copy in moving:
            copy.start()

        def ready():
            while moving:
                moving.pop(0).wait()

        far = {}
        for place, number in enumerate(near_out, len(near_in)):
            far[place] = results[number]
            results[number] = held[place]
        mover = body(ready, *ins, *results, *own)
        ready()
        leaving = [
            pltpu.make_async_copy(held[place], target, sems.at[place]) for place, target in far.items()
        ]
        for copy in leaving:
            copy.start()
        if mover is not None:
            mover.finish()
        for copy in leaving:
            copy.wait()

    return pl.pallas_call(
        kernel,
        out_shape=tuple(jax.ShapeDtypeStruct(shape, kind) for shape, kind, _ in outs),
        in_specs=[NEAR if spec is NEAR else FAR for _, spec in args],
        out_specs=tuple([NEAR if spec is NEAR else FAR for _, _, spec in outs]),
        scratch_shapes=list(scratch)
        + copies
        + [pltpu.SemaphoreType.DMA((max(1, len(near_in) + len(near_out)),))],
        compiler_params=pltpu.CompilerParams(vmem_limit_bytes=limit),
        cost_estimate=pl.CostEstimate(flops=flops, bytes_accessed=nbytes, transcendentals=0),
    )(*[array for array, _ in args])


class Mover:
    def __init__(self, sems):
        self.sems = sems
        self.used = 0
        self.open = []

    def start(self, source, target):
        copy = pltpu.make_async_copy(source, target, self.sems.at[self.used])
        self.used += 1
        copy.start()
        return copy

    def out(self, source, target):
        self.open.append(self.start(source, target))

    def finish(self):
        for copy in self.open:
            copy.wait()


class Feed:
    def __init__(self, mover, pairs, depth):
        self.mover = mover
        self.pairs = pairs
        self.running = []
        self.done = 0
        for _ in range(depth):
            self.more()

    def more(self):
        if len(self.running) < len(self.pairs):
            self.running.append(self.mover.start(*self.pairs[len(self.running)]))

    def ahead(self):
        while len(self.running) < len(self.pairs):
            self.more()

    def need(self, count):
        while self.done < count:
            self.running[self.done].wait()
            self.done += 1
            self.more()


class Place:
    def __init__(self, dp, rows):
        self.dp = dp
        self.planes = dp // 4
        self.fast = self.planes == 4 and rows % (16 * dp) == 0
        self.count = 4 if self.fast else 1

    def out(self, mover, source, columns, fars, core, first, size, start=0):
        width = columns.size if isinstance(columns, pl.Slice) else columns.stop - columns.start
        target = slice(start, start + width)
        if not self.fast:
            rows = slice(first * size, first * size + source.shape[0])
            mover.out(source.at[:, columns], fars[0].at[rows, target])
            return
        index = lax.axis_index("dp")
        for plane in range(source.shape[0] // size // 4):
            far = (((first // 4 + plane) ^ (index >> 2)) - 1) & (self.planes - 1)
            for near in range(4):
                upper, lower = 1 - near // 2, 1 - near % 2
                flip = jnp.where(core == 0, upper + 2 * lower, lower + 2 * upper)
                block = plane * 4 + ((index & 3) ^ flip)
                mover.out(
                    source.at[pl.ds(pl.multiple_of(block * size, 16), size), columns],
                    fars[near].at[pl.ds(pl.multiple_of(far * size, 16), size), target],
                )


def half_of(which, half):
    return pl.ds(pl.multiple_of(which * half, LANES), half)


def head_masks(rows):
    lane = lax.broadcasted_iota(jnp.int32, (rows, LANES), 1)
    left = (lane < LANES // 2).astype(F32).astype(LOW)
    right = (lane >= LANES // 2).astype(F32).astype(LOW)
    return left, right


def gelu_both(inner):
    density = jnp.exp(inner * inner * (-0.5)) * 0.3989422804014327
    below = 0.5 + 0.5 * lax.erf(inner * 0.7071067811865476)
    return inner * below, below + inner * density


def forward(
    place, length, ramp_count, ready,
    x_far, qkv_far, query_bias_ref, value_bias_ref, output_far, output_bias_ref,
    first_scale_ref, first_shift_ref, inner_far, inner_bias_ref, outer_far,
    outer_bias_ref, second_scale_ref, second_shift_ref, cot_far, pool_own_far, pool_other_far,
    pool_bias_own_ref, pool_bias_other_ref, class_own_ref, class_other_ref,
    class_bias_own_ref, class_bias_other_ref, labels_ref, ramps_ref,
    mixed_far, probs_far, context_far, normal_far, spread_ref,
    final_far, logits_ref, slope_far, resid_far, full_far, vector_ref, pair_own_ref, pair_send_ref,
    *refs,
):
    sends, owns, refs = refs[: place.count], refs[place.count : 2 * place.count], refs[2 * place.count :]
    (
    x_ref, qkv_ref, output_ref, mixed_ref, probs_ref, context_ref, normal_ref,
    inner_ref, outer_ref, cot_ref, pool_own_ref, pool_other_ref,
    final_ref, acted_ref, slope_ref, resid_ref, full_ref,
    low_ref, sum_ref, second_spread_ref, sems,
    ) = refs
    rows, features = x_ref.shape
    hidden_units = inner_ref.shape[1]
    seqs = rows // length
    pairs = features // LANES
    factor = (features // HEADS) ** (-0.5)
    core = lax.axis_index("ramp")
    mover = Mover(sems)
    parts = [slice(part * features, (part + 1) * features) for part in range(3)]
    steps = [
        slice(one * features, (one + 1) * features) for one in range(hidden_units // features)
    ]
    wanted = [(x_far, x_ref)]
    wanted += [(qkv_far.at[:, one], qkv_ref.at[:, one]) for one in parts]
    wanted += [(output_far, output_ref)]
    for one in steps:
        wanted += [(inner_far.at[:, one], inner_ref.at[:, one])]
        wanted += [(outer_far.at[one], outer_ref.at[one])]
    wanted += [(pool_own_far, pool_own_ref), (pool_other_far, pool_other_ref), (cot_far, cot_ref)]
    feed = Feed(mover, wanted, 3)
    ready()
    for part, columns in enumerate(parts):
        feed.need(2 + part)
        mixed = times(x_ref[...], qkv_ref[:, columns])
        if part == 0:
            mixed = mixed + query_bias_ref[...][None, :]
        if part == 2:
            mixed = mixed + value_bias_ref[...][None, :]
        mixed_ref[:, columns] = mixed.astype(LOW)
    feed.ahead()
    left, right = head_masks(length)
    left_t, right_t = left.T, right.T

    def one_sequence(seq, carry):
        here = pl.ds(pl.multiple_of(seq * length, length), length)
        for pair in range(pairs):
            start = pair * LANES
            query = mixed_ref[here, start : start + LANES]
            key = mixed_ref[here, features + start : features + start + LANES]
            value = mixed_ref[here, 2 * features + start : 2 * features + start + LANES]
            stacked = jnp.concatenate([query * left, query * right], axis=0)
            scores = times_transposed(key, stacked)
            top = jnp.max(scores, axis=0, keepdims=True)
            raised = jnp.exp((scores - top) * factor)
            probs = (raised * (1.0 / column_sum(raised))).astype(LOW)
            probs_ref[pl.ds(seq * pairs + pair, 1)] = probs[None]
            value_t = value.T
            both = jnp.concatenate([value_t * left_t, value_t * right_t], axis=1)
            tall = jnp.concatenate([probs[:, :length], probs[:, length:]], axis=0)
            context_t = times(both, tall).astype(LOW)
            context_ref[here, start : start + LANES] = context_t.T
        return carry

    lax.fori_loop(0, seqs, one_sequence, 0)
    feed.need(5)
    mover.out(mixed_ref, mixed_far)
    mover.out(probs_ref, probs_far)
    mover.out(context_ref, context_far)
    normal_ref[...] = times(context_ref[...], output_ref[...]) + output_bias_ref[...][None, :]
    hidden_square = jnp.zeros((1, features), F32)
    attended_square = jnp.zeros((1, features), F32)
    first_scale = first_scale_ref[...][None, :]
    first_shift = first_shift_ref[...][None, :]
    outer_bias = outer_bias_ref[...][None, :]
    for seq in range(seqs):
        here = slice(seq * length, (seq + 1) * length)
        hidden = x_ref[here, :].astype(F32)
        attended = normal_ref[here, :]
        residual = hidden + attended
        centred = residual - row_sum(residual) * (1.0 / features)
        spread = lax.rsqrt(row_sum(centred * centred) * (1.0 / features) + EPS)
        normal = centred * spread
        normal_ref[here, :] = normal
        spread_ref[here, :] = spread
        first = normal * first_scale + first_shift
        low_ref[here, :] = first.astype(LOW)
        sum_ref[here, :] = first + outer_bias
        hidden_square = hidden_square + column_sum(hidden * hidden)
        attended_square = attended_square + column_sum(attended * attended)
    mover.out(normal_ref, normal_far)

    feed.need(5 + 2 * len(steps))

    def inner_of(columns):
        return times(low_ref[...], inner_ref[:, columns]) + inner_bias_ref[columns][None, :]

    inner = inner_of(steps[0])
    for step, columns in enumerate(steps):
        following = inner_of(steps[step + 1]) if step + 1 < len(steps) else None
        acted, slope = gelu_both(inner)
        acted = acted.astype(LOW)
        acted_ref[:, columns] = acted
        slope_ref[:, columns] = slope.astype(LOW)
        sum_ref[...] += times(acted, outer_ref[columns, :])
        inner = following
    mover.out(slope_ref, slope_far)

    scale = second_scale_ref[...][None, :]
    shift = second_shift_ref[...][None, :]
    square = jnp.zeros((1, features), F32)
    leading = []
    for seq in range(seqs):
        here = slice(seq * length, (seq + 1) * length)
        residual = sum_ref[here, :]
        outer = residual - (normal_ref[here, :] * first_scale + first_shift)
        square = square + column_sum(outer * outer)
        centred = residual - row_sum(residual) * (1.0 / features)
        spread = lax.rsqrt(row_sum(centred * centred) * (1.0 / features) + EPS)
        normal = centred * spread
        sum_ref[here, :] = normal
        second_spread_ref[here, :] = spread
        final = (normal * scale + shift).astype(LOW)
        final_ref[here, :] = final
        leading.append(final[0:1, :].astype(F32))
    mover.out(final_ref, final_far)

    feed.need(len(wanted) - 1)
    leading = jnp.concatenate(leading + [jnp.zeros((8 - seqs, features), F32)], axis=0)
    states = leading.astype(LOW)
    row = lax.broadcasted_iota(jnp.int32, (8, 1), 0)
    ramp_of = jnp.full((8, 1), -1, jnp.int32)
    label_of = jnp.full((8, 1), -1, jnp.int32)
    for seq in range(seqs):
        ramp_of = jnp.where(row == seq, ramps_ref[seq], ramp_of)
        label_of = jnp.where(row == seq, labels_ref[seq], label_of)
    own = ramp_of == core
    pre_own = times(states, pool_own_ref[0]) + pool_bias_own_ref[...]
    pre_other = times(states, pool_other_ref[0]) + pool_bias_other_ref[...]
    pooled = jnp.tanh(jnp.where(own, pre_own, pre_other))
    pooled_low = pooled.astype(LOW)
    logits = jnp.where(
        own,
        times(pooled_low, class_own_ref[0]) + class_bias_own_ref[...],
        times(pooled_low, class_other_ref[0]) + class_bias_other_ref[...],
    )
    logits_ref[...] = logits[:seqs, :]
    raised = jnp.exp(logits - jnp.max(logits, axis=-1, keepdims=True))
    kind = lax.broadcasted_iota(jnp.int32, (8, CLASSES), 1)
    grads = raised / row_sum(raised) - (kind == label_of).astype(F32)
    grads = jnp.where(ramp_of >= 0, grads, 0.0)
    grads_high = grads.astype(LOW)
    grads_rest = (grads - grads_high.astype(F32)).astype(LOW)

    def from_logits(weight):
        return times_transposed(grads_high, weight) + times_transposed(grads_rest, weight)

    pooled_grad = jnp.where(own, from_logits(class_own_ref[0]), from_logits(class_other_ref[0]))
    pre_low = (pooled_grad * (1.0 - pooled * pooled)).astype(LOW).astype(F32)
    pre_own_low = jnp.where(own, pre_low, 0.0).astype(LOW)
    pre_other_low = jnp.where(own, 0.0, pre_low).astype(LOW)
    state_grad = times_transposed(pre_own_low, pool_own_ref[0])
    state_grad = state_grad + times_transposed(pre_other_low, pool_other_ref[0])
    pair_own_ref[0:8, :] = states
    pair_own_ref[8:16, :] = pre_own_low
    pair_send_ref[0:8, :] = states
    pair_send_ref[8:16, :] = pre_other_low

    vector_ref[...] = jnp.zeros(vector_ref.shape, F32)
    for ramp in range(ramp_count):
        mask = ramp_of == ramp
        base = 8 * (ramp + 1)
        vector_ref[base : base + 1, :] = column_sum(jnp.where(mask, pre_low, 0.0))
        high = jnp.where(mask, grads_high.astype(F32), 0.0).astype(LOW)
        rest = jnp.where(mask, grads_rest.astype(F32), 0.0).astype(LOW)
        vector_ref[base + 1 : base + 1 + CLASSES, :] = first_times(high, pooled_low) + first_times(
            rest, pooled_low
        )
        vector_ref[base + 4 : base + 5, 0:CLASSES] = column_sum(jnp.where(mask, grads, 0.0))

    feed.need(len(wanted))
    scale_grad = jnp.zeros((1, features), F32)
    shift_grad = jnp.zeros((1, features), F32)
    bias_grad = jnp.zeros((1, features), F32)
    at_first = lax.broadcasted_iota(jnp.int32, (length, 1), 0) == 0
    for seq in range(seqs):
        here = slice(seq * length, (seq + 1) * length)
        final_grad = cot_ref[here, :].astype(F32)
        final_grad = final_grad + jnp.where(at_first, state_grad[seq : seq + 1, :], 0.0)
        normal = sum_ref[here, :]
        scale_grad = scale_grad + column_sum(final_grad * normal)
        shift_grad = shift_grad + column_sum(final_grad)
        scaled = final_grad * scale
        resid = second_spread_ref[here, :] * (
            scaled
            - row_sum(scaled) * (1.0 / features)
            - normal * (row_sum(scaled * normal) * (1.0 / features))
        )
        resid_ref[here, :] = resid
        low = resid.astype(LOW)
        full_ref[here, :] = low
        bias_grad = bias_grad + column_sum(low.astype(F32))
    mover.out(full_ref, full_far)
    mover.out(resid_ref, resid_far)
    size = hidden_units // place.dp
    half = features // 2
    def leave(step):
        first = step * features // size
        source = outer_ref.at[steps[step]]
        place.out(mover, source, half_of(1 - core, half), sends, 1 - core, first, size)
        place.out(mover, source, half_of(core, half), owns, core, first, size)

    middle = len(steps) // 2
    for step, columns in enumerate(steps):
        outer_ref[columns, :] = first_times(acted_ref[:, columns], full_ref[...]).astype(LOW)
        if step + 1 == middle:
            for one in range(middle):
                leave(one)
    for one in range(middle, len(steps)):
        leave(one)
    vector_ref[0:1, :] = bias_grad
    vector_ref[1:2, :] = scale_grad
    vector_ref[2:3, :] = shift_grad
    vector_ref[3:4, 0:1] = row_sum(hidden_square)
    vector_ref[3:4, 1:2] = row_sum(attended_square)
    vector_ref[3:4, 2:3] = row_sum(square)
    return mover


def feed_backward(
    place, length, ready,
    full_far, slope_far, outer_far, inner_far, resid_far, normal_far, spread_ref,
    first_scale_ref, first_shift_ref, output_far, context_far, after_far,
    context_grad_far, first_resid_far, vector_ref, *refs,
):
    sends, owns, refs = refs[: place.count], refs[place.count : 2 * place.count], refs[2 * place.count :]
    (
    full_ref, slope_ref, outer_ref, inner_ref, sum_ref, normal_ref, output_ref, context_ref,
    weight_ref, output_grad_ref, first_ref, context_grad_ref, first_resid_ref,
    low_ref, first_grad_ref, sems,
    ) = refs
    rows, features = normal_ref.shape
    core = lax.axis_index("ramp")
    hidden_units = slope_ref.shape[1]
    half = hidden_units // 2
    mover = Mover(sems)
    order = []
    for far, who in ((sends, 1 - core), (owns, core)):
        for start in range(0, half, features):
            number = who * (half // features) + start // features
            columns = pl.ds(pl.multiple_of(number * features, LANES), features)
            order.append((far, who, start, number, columns))
    wanted = [(full_far, full_ref)]
    for _, _, _, _, columns in order:
        wanted.append((outer_far.at[columns], outer_ref.at[columns]))
        wanted.append((slope_far.at[:, columns], slope_ref.at[:, columns]))
        if len(wanted) == 3:
            wanted.append((normal_far, normal_ref))
        wanted.append((inner_far.at[:, columns], inner_ref.at[:, columns]))
    wanted += [(resid_far, sum_ref), (output_far, output_ref), (context_far, context_ref)]
    feed = Feed(mover, wanted, 7)
    ready()
    scale = first_scale_ref[...][None, :]
    vector_ref[...] = jnp.zeros(vector_ref.shape, F32)
    size = features // place.dp
    def acted_grad_of(step):
        return times_transposed(full_ref[...], outer_ref[order[step][4], :])

    feed.need(2)
    acted_grad = acted_grad_of(0)
    feed.need(4)
    first_ref[...] = (normal_ref[...] * scale + first_shift_ref[...][None, :]).astype(LOW)
    for step, (far, who, start, number, columns) in enumerate(order):
        feed.need(min(5 + 3 * step + 1, 2 + 3 * len(order)))
        following = acted_grad_of(step + 1) if step + 1 < len(order) else None
        inner_grad = (slope_ref[:, columns].astype(F32) * acted_grad).astype(LOW)
        vector_ref[pl.ds(3 + number, 1), :] = column_sum(inner_grad.astype(F32))
        product = times_transposed(inner_grad, inner_ref[:, columns])
        if step == 0:
            first_grad_ref[...] = product
        else:
            first_grad_ref[...] += product
        here = slice(step * features, (step + 1) * features)
        weight_ref[:, here] = first_times(first_ref[...], inner_grad).astype(LOW)
        place.out(mover, weight_ref, here, far, who, 0, size, start)
        acted_grad = following
    feed.need(len(wanted))
    zero = jnp.zeros((1, features), F32)
    sums = [zero, zero, zero]
    for seq in range(rows // length):
        here = slice(seq * length, (seq + 1) * length)
        first_grad = sum_ref[here, :] + first_grad_ref[here, :]
        normal = normal_ref[here, :]
        scaled = first_grad * scale
        resid = spread_ref[here, :] * (
            scaled
            - row_sum(scaled) * (1.0 / features)
            - normal * (row_sum(scaled * normal) * (1.0 / features))
        )
        first_resid_ref[here, :] = resid
        low = resid.astype(LOW)
        low_ref[here, :] = low
        sums[0] = sums[0] + column_sum(low.astype(F32))
        sums[1] = sums[1] + column_sum(first_grad * normal)
        sums[2] = sums[2] + column_sum(first_grad)
    mover.out(first_resid_ref, first_resid_far)
    for number, one in enumerate(sums):
        vector_ref[number : number + 1, :] = one
    output_grad_ref[...] = first_times(context_ref[...], low_ref[...]).astype(LOW)
    for far, who in ((sends, 1 - core), (owns, core)):
        place.out(mover, output_grad_ref, half_of(who, features // 2), far, who, 0, size, half)
    context_grad_ref[...] = times_transposed(low_ref[...], output_ref[...]).astype(LOW)
    mover.out(context_grad_ref, context_grad_far)
    return mover


def attention_backward(
    place, length, ready,
    mixed_far, probs_far, context_grad_far, x_far, after_far,
    grad_far, vector_ref, *refs,
):
    sends, owns, refs = refs[: place.count], refs[place.count : 2 * place.count], refs[2 * place.count :]
    mixed_ref, probs_ref, context_grad_ref, x_ref, grad_ref, weight_ref, sems, out_sems = refs
    rows, features = context_grad_ref.shape
    seqs = rows // length
    core = lax.axis_index("ramp")
    pairs = features // LANES
    factor = (features // HEADS) ** (-0.5)
    left, right = head_masks(length)

    def copies(seq):
        here = pl.ds(pl.multiple_of(seq * length, length), length)
        heads = pl.ds(seq * pairs, pairs)
        return (
            pltpu.make_async_copy(mixed_far.at[here], mixed_ref.at[here], sems.at[0, seq]),
            pltpu.make_async_copy(probs_far.at[heads], probs_ref.at[heads], sems.at[1, seq]),
            pltpu.make_async_copy(
                context_grad_far.at[here], context_grad_ref.at[here], sems.at[2, seq]
            ),
        )

    for seq in range(seqs):
        for copy in copies(seq):
            copy.start()
    mover = Mover(out_sems)
    got_x = mover.start(x_far, x_ref)

    def one_sequence(seq, carry):
        here = pl.ds(pl.multiple_of(seq * length, length), length)
        for copy in copies(seq):
            copy.wait()
        for pair in range(pairs):
            start = pair * LANES
            query = mixed_ref[here, start : start + LANES]
            key = mixed_ref[here, features + start : features + start + LANES]
            value = mixed_ref[here, 2 * features + start : 2 * features + start + LANES]
            context_grad = context_grad_ref[here, start : start + LANES]
            queries = jnp.concatenate([query * left, query * right], axis=0)
            keys = jnp.concatenate([key * left, key * right], axis=0)
            grads = jnp.concatenate([context_grad * left, context_grad * right], axis=0)
            probs = probs_ref[pl.ds(seq * pairs + pair, 1)][0]
            probs_grad = times_transposed(value, grads)
            wide = probs.astype(F32)
            score_grad = wide * (probs_grad - column_sum(wide * probs_grad))
            score_grad = score_grad.astype(LOW)
            value_grad = times(probs, grads).astype(LOW)
            key_grad = (times(score_grad, queries) * factor).astype(LOW)
            turned = jnp.concatenate(
                [score_grad[:, :length].T, score_grad[:, length:].T], axis=1
            )
            query_grad = (times(turned, keys) * factor).astype(LOW)
            grad_ref[here, start : start + LANES] = query_grad
            grad_ref[here, features + start : features + start + LANES] = key_grad
            grad_ref[here, 2 * features + start : 2 * features + start + LANES] = value_grad
        return carry

    lax.fori_loop(0, seqs, one_sequence, 0)
    mover.out(grad_ref, grad_far)
    got_x.wait()
    half = 3 * features // 2
    size = features // place.dp
    for far, who in ((sends, 1 - core), (owns, core)):
        for start, width in ((0, features), (features, half - features)):
            columns = pl.ds(pl.multiple_of(who * half + start, LANES), width)
            weight_ref[:, columns] = first_times(x_ref[...], grad_ref[:, columns]).astype(LOW)
            place.out(mover, weight_ref, columns, far, who, 0, size, start)
    vector_ref[...] = jnp.zeros(vector_ref.shape, F32)
    vector_ref[0:1, :] = column_sum(grad_ref[:, :features].astype(F32))
    vector_ref[1:2, :] = column_sum(grad_ref[:, 2 * features :].astype(F32))
    return mover


def input_gradient(
    ready,
    grad_far, qkv_far, resid_far, after_far,
    result_far,
    grad_ref, qkv_ref, resid_ref, result_ref, sems,
):
    mover = Mover(sems)
    features = resid_ref.shape[1]
    parts = [slice(part * features, (part + 1) * features) for part in range(3)]
    got = []
    for one in parts:
        got.append(
            (
                mover.start(grad_far.at[:, one], grad_ref.at[:, one]),
                mover.start(qkv_far.at[:, one], qkv_ref.at[:, one]),
            )
        )
    got_resid = mover.start(resid_far, resid_ref)
    total = None
    for columns, copies in zip(parts, got):
        for copy in copies:
            copy.wait()
        product = times_transposed(grad_ref[:, columns], qkv_ref[:, columns])
        total = product if total is None else total + product
    got_resid.wait()
    result_ref[...] = (resid_ref[...] + total).astype(LOW)
    mover.out(result_ref, result_far)
    return mover


def swap_core(values):
    return lax.ppermute(values, "ramp", [(0, 1), (1, 0)])


def shift(values, even, odd):
    dp = lax.axis_size("dp")
    pairs = []
    for one in range(dp):
        pairs.append((2 * one, 2 * (one ^ even)))
        pairs.append((2 * one + 1, 2 * (one ^ odd) + 1))
    return lax.ppermute(values, ("dp", "ramp"), pairs)


def combine(plan, count, ready, *refs):
    arrays, results = refs[:count], refs[count:]
    for parts, result in zip(plan, results):
        top = 0
        for rows, width, terms in parts:
            total = None
            for array, row, column in terms:
                term = arrays[array][row : row + rows, column : column + width].astype(F32)
                total = term if total is None else total + term
            result[top : top + rows, :] = total.astype(result.dtype)
            top += rows


def combined(results, after=()):
    arrays = []
    for _, _, parts in results:
        for _, terms in parts:
            for array, _, _ in terms:
                if not any(array is one for one in arrays):
                    arrays.append(array)

    def number(array):
        return [one is array for one in arrays].index(True)

    plan = [
        [(rows, width, [(number(array), row, column) for array, row, column in terms]) for rows, terms in parts]
        for width, _, parts in results
    ]
    shapes = [((sum(part[0] for part in parts), width), kind) for width, kind, parts in results]
    return call(
        partial(combine, plan, len(arrays) + len(after)),
        [(shape, kind, NEAR) for shape, kind in shapes] + [((8, LANES), F32, FAR)],
        [(array, NEAR) for array in arrays] + [(array, FAR) for array in after],
        nbytes=sum(8 * shape[0] * shape[1] for shape, _ in shapes),
        limit=SMALL_BYTES,
    )


class Chain:
    def __init__(self, sends, owns):
        self.own = owns
        self.got = [swap_core(one) for one in sends]
        self.width = owns[0].shape[1]

    def add_first(self):
        rows = self.own[0].shape[0]
        parts = [(rows, [(own, 0, 0), (got, 0, 0)]) for own, got in zip(self.own, self.got)]
        return [(self.width, LOW, parts[:2]), (self.width, LOW, parts[2:])]

    def send_first(self, send, keep):
        self.got, self.own = shift(send, 1, 2), keep

    def add_second(self):
        rows = self.own.shape[0] // 2
        return [
            (self.width, LOW, [(rows, [(self.own, start, 0), (self.got, start, 0)])])
            for start in (0, rows)
        ]

    def send_second(self, send, keep):
        self.got, self.own = shift(send, 2, 1), keep

    def add_third(self):
        rows = self.own.shape[0] // 4
        return [
            (self.width, LOW, [(rows, [(self.own, start * rows, 0), (self.got, start * rows, 0)])])
            for start in range(4)
        ]

    def send_third(self, *arrays):
        self.planes = [
            shift(one, (number + 1) << 2, (number + 1) << 2) for number, one in enumerate(arrays[:3])
        ]
        self.own = arrays[3]

    def add_last(self, widths):
        results = []
        start = 0
        for width in widths:
            terms = [(array, 0, start) for array in [self.own] + self.planes]
            results.append((width, F32, [(self.own.shape[0], terms)]))
            start += width
        return results

    def plain(self, widths):
        total = (self.own[0].astype(F32) + self.got[0].astype(F32)).astype(LOW)
        rows = lax.psum_scatter(total, "dp", scatter_dimension=0, tiled=True).astype(F32)
        ends = [sum(widths[: one + 1]) for one in range(len(widths))]
        return [rows[:, end - width : end] for width, end in zip(widths, ends)]


VECTOR_ROWS = 128


def collect_vectors(features, ready, mixed_ref, first_ref, second_ref, after_far, out_ref):
    ready()
    out_ref[...] = jnp.zeros(out_ref.shape, F32)
    place = 0

    def put(row):
        nonlocal place
        for start in range(0, features, LANES):
            out_ref[place : place + 1, :] = row[:, start : start + LANES]
            place += 1

    for number in range(2):
        put(mixed_ref[number : number + 1, :])
    for number in range(7):
        put(first_ref[number : number + 1, :])
    for number in range(3):
        put(second_ref[number : number + 1, :])
    for base in (8, 16):
        for number in range(1 + CLASSES):
            put(second_ref[base + number : base + number + 1, :])
    for number in (3, 12, 20):
        out_ref[place : place + 1, :] = second_ref[number : number + 1, :LANES]
        place += 1


def add_all(ready, *refs):
    ready()
    *refs, after_far, out_ref = refs
    total = refs[0][...]
    for ref in refs[1:]:
        total = total + ref[...]
    out_ref[...] = total


def add_over(values, masks, after=None):
    got = [shift(values, mask, mask) for mask in masks]
    (total,) = call(
        add_all,
        [(values.shape, values.dtype, VMEM)],
        [(one, VMEM) for one in [values] + got] + [((after or [values])[0], FAR)],
        limit=SMALL_BYTES,
    )
    return total


def hand_out(features, entries, ready, all_ref, after_far, *outs):
    ready()
    core = lax.axis_index("ramp")
    place = 0

    def take(ref, start=0):
        nonlocal place
        for column in range(0, features, LANES):
            ref[pl.ds(start + column, LANES)] = all_ref[place, :]
            place += 1

    rms_ref, query_ref, value_ref, output_ref, scale_ref, shift_ref, inner_ref = outs[:7]
    outer_ref, second_scale_ref, second_shift_ref, pool_ref, class_ref, class_bias_ref = outs[7:]
    for ref in (query_ref, value_ref, output_ref, scale_ref, shift_ref):
        take(ref)
    for start in range(0, inner_ref.shape[0], features):
        take(inner_ref, start)
    for ref in (outer_ref, second_scale_ref, second_shift_ref):
        take(ref)
    step = features // LANES
    size = step * (1 + CLASSES)
    for column in range(step):
        at = column * LANES
        first = all_ref[place + column : place + column + 1, :]
        second = all_ref[place + size + column : place + size + column + 1, :]
        pool_ref[:, at : at + LANES] = jnp.where(core == 0, first, second)
        for kind in range(CLASSES):
            row = place + (1 + kind) * step + column
            first = all_ref[row : row + 1, :]
            second = all_ref[row + size : row + size + 1, :]
            class_ref[kind : kind + 1, at : at + LANES] = jnp.where(core == 0, first, second)
    place += 2 * size
    rms_ref[...] = jnp.sqrt(all_ref[place : place + 1, :] * (1.0 / entries))
    first = all_ref[place + 1 : place + 2, :CLASSES]
    second = all_ref[place + 2 : place + 3, :CLASSES]
    class_bias_ref[...] = jnp.where(core == 0, first, second)


def collect_pairs(ready, own_ref, other_ref, after_far, out_ref):
    ready()
    for device in range(out_ref.shape[0]):
        out_ref[device, 0:8, :] = own_ref[0:8, :]
        out_ref[device, 8:16, :] = other_ref[0:8, :]
        out_ref[device, 16:24, :] = own_ref[8:16, :]
        out_ref[device, 24:32, :] = other_ref[8:16, :]


def pool_gradient(ready, pair_ref, after_far, out_ref, token_far, all_ref):
    ready()
    devices, _, features = pair_ref.shape
    states = pair_ref[:, 0:16, :].reshape(devices * 16, features)
    grads = pair_ref[:, 16:32, :].reshape(devices * 16, features)
    all_ref[...] = first_times(states, grads)
    rows = out_ref.shape[0]
    out_ref[...] = all_ref[pl.ds(pl.multiple_of(lax.axis_index("dp") * rows, 8), rows), :]


def on_device(
    hidden_in, cotangent, qkv_weight, query_bias, value_bias, output_weight, output_bias,
    first_scale, first_shift, inner_weight, inner_bias, outer_weight, outer_bias,
    second_scale, second_shift, pool_weight, pool_bias, class_weight, class_bias,
    labels, ramp_index,
):
    rows, features = hidden_in.shape
    seqs = labels.shape[0]
    length = rows // seqs
    units = inner_weight.shape[1]
    dp = lax.axis_size("dp")
    ramps = lax.axis_size("ramp")
    pairs = features // LANES
    place = Place(dp, features)
    half = features // 2
    halves = units // 2 + half

    pool_other = swap_core(pool_weight)
    pool_bias_other = swap_core(pool_bias)
    class_other = swap_core(class_weight)
    class_bias_other = swap_core(class_bias)
    (
        mixed, probs, context, normal, spread, output, logits, slope, second_resid, outer_full,
        second_vector, pair_own, pair_send, *outer_parts,
    ) = call(
        partial(forward, place, length, ramps),
        [
            ((rows, 3 * features), LOW, FAR),
            ((seqs * pairs, length, 2 * length), LOW, FAR),
            ((rows, features), LOW, FAR),
            ((rows, features), F32, FAR),
            ((rows, 1), F32, VMEM),
            ((rows, features), LOW, FAR),
            ((seqs, CLASSES), F32, VMEM),
            ((rows, units), LOW, FAR),
            ((rows, features), F32, FAR),
            ((rows, features), LOW, FAR),
            ((8 * (ramps + 1), features), F32, VMEM),
            ((16, features), LOW, VMEM),
            ((16, features), LOW, VMEM),
        ]
        + [((units // place.count, half), LOW, FAR)] * (2 * place.count),
        [
            (hidden_in, FAR),
            (qkv_weight, FAR),
            (query_bias, VMEM),
            (value_bias, VMEM),
            (output_weight, FAR),
            (output_bias, VMEM),
            (first_scale, VMEM),
            (first_shift, VMEM),
            (inner_weight, FAR),
            (inner_bias, VMEM),
            (outer_weight, FAR),
            (outer_bias, VMEM),
            (second_scale, VMEM),
            (second_shift, VMEM),
            (cotangent, FAR),
            (pool_weight, FAR),
            (pool_other, FAR),
            (pool_bias, VMEM),
            (pool_bias_other, VMEM),
            (class_weight, VMEM),
            (class_other, VMEM),
            (class_bias, VMEM),
            (class_bias_other, VMEM),
            (labels, SMEM),
            (ramp_index, SMEM),
        ],
        scratch=[
            pltpu.VMEM((rows, features), LOW),
            pltpu.VMEM((features, 3 * features), LOW),
            pltpu.VMEM((features, features), LOW),
            pltpu.VMEM((rows, 3 * features), LOW),
            pltpu.VMEM((seqs * pairs, length, 2 * length), LOW),
            pltpu.VMEM((rows, features), LOW),
            pltpu.VMEM((rows, features), F32),
            pltpu.VMEM((features, units), LOW),
            pltpu.VMEM((units, features), LOW),
            pltpu.VMEM((rows, features), LOW),
            pltpu.VMEM((1, features, features), LOW),
            pltpu.VMEM((1, features, features), LOW),
            pltpu.VMEM((rows, features), LOW),
            pltpu.VMEM((rows, units), LOW),
            pltpu.VMEM((rows, units), LOW),
            pltpu.VMEM((rows, features), F32),
            pltpu.VMEM((rows, features), LOW),
            pltpu.VMEM((rows, features), LOW),
            pltpu.VMEM((rows, features), F32),
            pltpu.VMEM((rows, 1), F32),
            pltpu.SemaphoreType.DMA((16 + 3 * (units // features) + 2 * dp,)),
        ],
        flops=2 * rows * features * (4 * features + 3 * units) + 8 * rows * features * length,
        nbytes=40 << 20,
        limit=VMEM_BYTES,
    )
    outer_chain = Chain(outer_parts[: place.count], outer_parts[place.count :])
    token = second_vector
    if place.fast:
        *sends, token = combined(outer_chain.add_first())
        outer_chain.send_first(*sends)

    context_grad, first_resid, first_vector, *inner_parts = call(
        partial(feed_backward, place, length),
        [
            ((rows, features), LOW, FAR),
            ((rows, features), F32, FAR),
            ((8, features), F32, VMEM),
        ]
        + [((features // place.count, halves), LOW, FAR)] * (2 * place.count),
        [
            (outer_full, FAR),
            (slope, FAR),
            (outer_weight, FAR),
            (inner_weight, FAR),
            (second_resid, FAR),
            (normal, FAR),
            (spread, VMEM),
            (first_scale, VMEM),
            (first_shift, VMEM),
            (output_weight, FAR),
            (context, FAR),
            (token, FAR),
        ],
        scratch=[
            pltpu.VMEM((rows, features), LOW),
            pltpu.VMEM((rows, units), LOW),
            pltpu.VMEM((units, features), LOW),
            pltpu.VMEM((features, units), LOW),
            pltpu.VMEM((rows, features), F32),
            pltpu.VMEM((rows, features), F32),
            pltpu.VMEM((features, features), LOW),
            pltpu.VMEM((rows, features), LOW),
            pltpu.VMEM((features, units), LOW),
            pltpu.VMEM((features, features), LOW),
            pltpu.VMEM((rows, features), LOW),
            pltpu.VMEM((rows, features), LOW),
            pltpu.VMEM((rows, features), F32),
            pltpu.VMEM((rows, features), LOW),
            pltpu.VMEM((rows, features), F32),
            pltpu.SemaphoreType.DMA((8 + (3 + dp) * (units // features) + 2 * dp,)),
        ],
        flops=6 * rows * features * units + 4 * rows * features * features,
        nbytes=25 << 20,
        limit=40 << 20,
    )
    inner_chain = Chain(inner_parts[: place.count], inner_parts[place.count :])
    token = first_vector
    if place.fast:
        *sends, token = combined(outer_chain.add_second(), after=[first_vector])
        outer_chain.send_second(*sends)
    pair_other = swap_core(pair_send)
    (pair,) = call(
        collect_pairs,
        [((dp, 32, features), LOW, VMEM)],
        [(pair_own, VMEM), (pair_other, VMEM), (token, FAR)],
        nbytes=1 << 20,
        limit=SMALL_BYTES,
    )
    token = pair
    if place.fast:
        *sends, token = combined(outer_chain.add_third() + inner_chain.add_first(), after=[pair])
        outer_chain.send_third(*sends[:4])
        inner_chain.send_first(*sends[4:])
    pair_all = lax.all_to_all(pair, "dp", split_axis=0, concat_axis=0, tiled=True)

    mixed_grad, mixed_vector, *qkv_parts = call(
        partial(attention_backward, place, length),
        [
            ((rows, 3 * features), LOW, FAR),
            ((8, features), F32, VMEM),
        ]
        + [((features // place.count, 3 * half), LOW, FAR)] * (2 * place.count),
        [
            (mixed, FAR),
            (probs, FAR),
            (context_grad, FAR),
            (hidden_in, FAR),
            (token, FAR),
        ],
        scratch=[
            pltpu.VMEM((rows, 3 * features), LOW),
            pltpu.VMEM((seqs * pairs, length, 2 * length), LOW),
            pltpu.VMEM((rows, features), LOW),
            pltpu.VMEM((rows, features), LOW),
            pltpu.VMEM((rows, 3 * features), LOW),
            pltpu.VMEM((features, 3 * features), LOW),
            pltpu.SemaphoreType.DMA((3, seqs)),
            pltpu.SemaphoreType.DMA((4 + 4 * dp,)),
        ],
        flops=20 * rows * features * length + 6 * rows * features * features,
        nbytes=12 << 20,
        limit=24 << 20,
    )
    qkv_chain = Chain(qkv_parts[: place.count], qkv_parts[place.count :])
    token = mixed_vector
    if place.fast:
        (pool_sum, pool_token) = call(
            pool_gradient,
            [((features // dp, features), F32, VMEM), ((8, LANES), F32, FAR)],
            [(pair_all, VMEM), (mixed_vector, FAR)],
            scratch=[pltpu.VMEM((features, features), F32)],
            limit=SMALL_BYTES,
        )
        outer_sum, *sends, token = combined(
            outer_chain.add_last([half]) + inner_chain.add_second(),
            after=[mixed_vector, pool_token],
        )
        inner_chain.send_second(*sends)
    (vectors,) = call(
        partial(collect_vectors, features),
        [((VECTOR_ROWS, LANES), F32, VMEM)],
        [
            (mixed_vector, VMEM),
            (first_vector, VMEM),
            (second_vector, VMEM),
            (token, FAR),
        ],
        limit=SMALL_BYTES,
    )
    vectors_other = swap_core(vectors)

    (input_grad,) = call(
        input_gradient,
        [((rows, features), LOW, FAR)],
        [(mixed_grad, FAR), (qkv_weight, FAR), (first_resid, FAR), (vectors, FAR)],
        scratch=[
            pltpu.VMEM((rows, 3 * features), LOW),
            pltpu.VMEM((features, 3 * features), LOW),
            pltpu.VMEM((rows, features), F32),
            pltpu.VMEM((rows, features), LOW),
            pltpu.SemaphoreType.DMA((8,)),
        ],
        flops=6 * rows * features * features,
        nbytes=10 << 20,
        limit=20 << 20,
    )

    token = input_grad
    if place.fast:
        *sends, token = combined(
            inner_chain.add_third() + qkv_chain.add_first(), after=[input_grad]
        )
        inner_chain.send_third(*sends[:4])
        qkv_chain.send_first(*sends[4:])

    (vectors,) = call(
        add_all,
        [((VECTOR_ROWS, LANES), F32, VMEM)],
        [(vectors, VMEM), (vectors_other, VMEM), (token, FAR)],
        limit=SMALL_BYTES,
    )
    vectors = add_over(vectors, [1, 2, 3])
    token = vectors
    if place.fast:
        *sends, inner_sum, output_sum, token = combined(
            qkv_chain.add_second() + inner_chain.add_last([units // 2, half]), after=[vectors]
        )
        qkv_chain.send_second(*sends)
        *sends, token = combined(qkv_chain.add_third())
        qkv_chain.send_third(*sends)
    vectors = add_over(vectors, [one << 2 for one in range(1, dp // 4)], [token])
    (
        rms, query_bias_sum, value_bias_sum, output_bias_sum, first_scale_sum, first_shift_sum,
        inner_bias_sum, outer_bias_sum, second_scale_sum, second_shift_sum,
        pool_bias_sum, class_sum, class_bias_sum,
    ) = call(
        partial(hand_out, features, rows * features * dp * ramps),
        [((1, LANES), F32, VMEM)]
        + [((features,), F32, VMEM)] * 5
        + [((units,), F32, VMEM)]
        + [((features,), F32, VMEM)] * 3
        + [((1, features), F32, VMEM), ((CLASSES, features), F32, VMEM), ((1, CLASSES), F32, VMEM)],
        [(vectors, VMEM), (token, FAR)],
        limit=SMALL_BYTES,
    )
    if place.fast:
        qkv_sum, token = combined(qkv_chain.add_last([3 * half]), after=[rms])
    else:
        states = pair_all[:, 0:16].reshape(dp * 16, features)
        pre_grads = pair_all[:, 16:32].reshape(dp * 16, features)
        own_rows = features // dp
        states = lax.dynamic_slice_in_dim(
            states, lax.axis_index("dp") * own_rows, own_rows, axis=1
        )
        pool_sum = first_times(states, pre_grads)
        (outer_sum,) = outer_chain.plain([half])
        inner_sum, output_sum = inner_chain.plain([units // 2, half])
        (qkv_sum,) = qkv_chain.plain([3 * half])
    return (
        output,
        logits,
        rms[0, :3],
        input_grad,
        qkv_sum,
        query_bias_sum,
        value_bias_sum,
        output_sum,
        output_bias_sum,
        first_scale_sum,
        first_shift_sum,
        inner_sum,
        inner_bias_sum,
        outer_sum,
        outer_bias_sum,
        second_scale_sum,
        second_shift_sum,
        pool_sum[None],
        pool_bias_sum,
        class_sum.T[None],
        class_bias_sum,
    )


def solution(mesh):
    whole = P(("dp", "ramp"), None)
    return jax.shard_map(
        on_device,
        mesh=mesh,
        in_specs=(whole, whole)
        + (P(),) * 13
        + (
            P("ramp", None, None),
            P("ramp", None),
            P("ramp", None, None),
            P("ramp", None),
            P(("dp", "ramp")),
            P(("dp", "ramp")),
        ),
        out_specs=(
            whole,
            whole,
            P(),
            whole,
            P("dp", "ramp"),
            P(),
            P(),
            P("dp", "ramp"),
            P(),
            P(),
            P(),
            P("dp", "ramp"),
            P(),
            P("dp", "ramp"),
            P(),
            P(),
            P(),
            P("ramp", "dp", None),
            P("ramp", None),
            P("ramp", None, None),
            P("ramp", None),
        ),
        check_vma=False,
    )
```

```python
from functools import partial

import jax
import jax.numpy as jnp
from jax import lax
from jax.experimental import pallas as pl
from jax.experimental.pallas import tpu as pltpu
from jax.sharding import PartitionSpec as P

HEADS = 12
CLASSES = 3
LANES = 128
EPS = 1e-06
F32 = jnp.float32
LOW = jnp.bfloat16
NEAR = pl.BlockSpec(memory_space=pltpu.VMEM)
VMEM = pltpu.VMEM
SMEM = pltpu.SMEM
FAR = pl.BlockSpec(memory_space=pl.ANY)
VMEM_BYTES = 60 * 1024 * 1024
SMALL_BYTES = 16 * 1024 * 1024


def times(left, right):
    return lax.dot_general(left, right, (((1,), (0,)), ((), ())), preferred_element_type=F32)


def times_transposed(left, right):
    return lax.dot_general(left, right, (((1,), (1,)), ((), ())), preferred_element_type=F32)


def first_times(left, right):
    return lax.dot_general(left, right, (((0,), (0,)), ((), ())), preferred_element_type=F32)


def row_sum(values):
    return jnp.sum(values, axis=-1, keepdims=True)


def column_sum(values):
    return jnp.sum(values, axis=0, keepdims=True)


def call(body, outs, args, scratch=(), flops=0, nbytes=0, limit=VMEM_BYTES):
    near_in = [number for number, (_, spec) in enumerate(args) if spec in (VMEM, SMEM)]
    near_out = [number for number, (_, _, spec) in enumerate(outs) if spec in (VMEM, SMEM)]
    copies = [args[number][1](args[number][0].shape, args[number][0].dtype) for number in near_in]
    copies += [outs[number][2](outs[number][0], outs[number][1]) for number in near_out]

    def kernel(*refs):
        ins, refs = list(refs[: len(args)]), refs[len(args) :]
        results, refs = list(refs[: len(outs)]), refs[len(outs) :]
        own, refs = refs[: len(scratch)], refs[len(scratch) :]
        held, sems = refs[:-1], refs[-1]
        moving = []
        for place, number in enumerate(near_in):
            moving.append(pltpu.make_async_copy(ins[number], held[place], sems.at[place]))
            ins[number] = held[place]
        for copy in moving:
            copy.start()

        def ready():
            while moving:
                moving.pop(0).wait()

        far = {}
        for place, number in enumerate(near_out, len(near_in)):
            far[place] = results[number]
            results[number] = held[place]
        mover = body(ready, *ins, *results, *own)
        ready()
        leaving = [
            pltpu.make_async_copy(held[place], target, sems.at[place]) for place, target in far.items()
        ]
        for copy in leaving:
            copy.start()
        if mover is not None:
            mover.finish()
        for copy in leaving:
            copy.wait()

    return pl.pallas_call(
        kernel,
        out_shape=tuple(jax.ShapeDtypeStruct(shape, kind) for shape, kind, _ in outs),
        in_specs=[NEAR if spec is NEAR else FAR for _, spec in args],
        out_specs=tuple([NEAR if spec is NEAR else FAR for _, _, spec in outs]),
        scratch_shapes=list(scratch)
        + copies
        + [pltpu.SemaphoreType.DMA((max(1, len(near_in) + len(near_out)),))],
        compiler_params=pltpu.CompilerParams(vmem_limit_bytes=limit),
        cost_estimate=pl.CostEstimate(flops=flops, bytes_accessed=nbytes, transcendentals=0),
    )(*[array for array, _ in args])


class Mover:
    def __init__(self, sems):
        self.sems = sems
        self.used = 0
        self.open = []

    def start(self, source, target):
        copy = pltpu.make_async_copy(source, target, self.sems.at[self.used])
        self.used += 1
        copy.start()
        return copy

    def out(self, source, target):
        self.open.append(self.start(source, target))

    def finish(self):
        for copy in self.open:
            copy.wait()


class Feed:
    def __init__(self, mover, pairs, depth):
        self.mover = mover
        self.pairs = pairs
        self.running = []
        self.done = 0
        for _ in range(depth):
            self.more()

    def more(self):
        if len(self.running) < len(self.pairs):
            self.running.append(self.mover.start(*self.pairs[len(self.running)]))

    def ahead(self):
        while len(self.running) < len(self.pairs):
            self.more()

    def need(self, count):
        while self.done < count:
            self.running[self.done].wait()
            self.done += 1
            self.more()


class Place:
    def __init__(self, dp, rows):
        self.dp = dp
        self.planes = dp // 4
        self.fast = self.planes == 4 and rows % (16 * dp) == 0
        self.count = 4 if self.fast else 1

    def out(self, mover, source, columns, fars, core, first, size, start=0):
        width = columns.size if isinstance(columns, pl.Slice) else columns.stop - columns.start
        target = slice(start, start + width)

        def put(here, far, there):
            if mover is None:
                far[there, target] = source[here, columns]
            else:
                mover.out(source.at[here, columns], far.at[there, target])

        if not self.fast:
            put(slice(0, source.shape[0]), fars[0], slice(first * size, first * size + source.shape[0]))
            return
        index = lax.axis_index("dp")
        for plane in range(source.shape[0] // size // 4):
            far = (((first // 4 + plane) ^ (index >> 2)) - 1) & (self.planes - 1)
            for near in range(4):
                upper, lower = 1 - near // 2, 1 - near % 2
                flip = jnp.where(core == 0, upper + 2 * lower, lower + 2 * upper)
                block = plane * 4 + ((index & 3) ^ flip)
                top = near * self.planes * size if len(fars) == 1 else 0
                put(
                    pl.ds(pl.multiple_of(block * size, 16), size),
                    fars[0 if len(fars) == 1 else near],
                    pl.ds(pl.multiple_of(top + far * size, 16), size),
                )


def half_of(which, half):
    return pl.ds(pl.multiple_of(which * half, LANES), half)


def head_masks(rows):
    lane = lax.broadcasted_iota(jnp.int32, (rows, LANES), 1)
    left = (lane < LANES // 2).astype(F32).astype(LOW)
    right = (lane >= LANES // 2).astype(F32).astype(LOW)
    return left, right


def gelu_both(inner):
    density = jnp.exp(inner * inner * (-0.5)) * 0.3989422804014327
    below = 0.5 + 0.5 * lax.erf(inner * 0.7071067811865476)
    return inner * below, below + inner * density


def forward(
    place, length, ramp_count, ready,
    x_far, qkv_far, query_bias_ref, value_bias_ref, output_far, output_bias_ref,
    first_scale_ref, first_shift_ref, inner_far, inner_bias_ref, outer_far,
    outer_bias_ref, second_scale_ref, second_shift_ref, cot_far, pool_own_far, pool_other_far,
    pool_bias_own_ref, pool_bias_other_ref, class_own_ref, class_other_ref,
    class_bias_own_ref, class_bias_other_ref, labels_ref, ramps_ref,
    mixed_far, probs_far, context_far, normal_far, spread_ref,
    final_far, logits_ref, slope_far, resid_far, full_far, vector_ref, pair_own_ref, pair_send_ref,
    *refs,
):
    sends, owns, refs = refs[: place.count], refs[place.count : place.count + 1], refs[place.count + 1 :]
    (
    x_ref, qkv_ref, output_ref, mixed_ref, probs_ref, context_ref, normal_ref,
    inner_ref, outer_ref, cot_ref, pool_own_ref, pool_other_ref,
    final_ref, acted_ref, slope_ref, resid_ref, full_ref,
    low_ref, sum_ref, second_spread_ref, sems,
    ) = refs
    rows, features = x_ref.shape
    hidden_units = inner_ref.shape[1]
    seqs = rows // length
    pairs = features // LANES
    factor = (features // HEADS) ** (-0.5)
    core = lax.axis_index("ramp")
    mover = Mover(sems)
    parts = [slice(part * features, (part + 1) * features) for part in range(3)]
    steps = [
        slice(one * features, (one + 1) * features) for one in range(hidden_units // features)
    ]
    wanted = [(x_far, x_ref)]
    wanted += [(qkv_far.at[:, one], qkv_ref.at[:, one]) for one in parts]
    wanted += [(output_far, output_ref)]
    for one in steps:
        wanted += [(inner_far.at[:, one], inner_ref.at[:, one])]
        wanted += [(outer_far.at[one], outer_ref.at[one])]
    wanted += [(pool_own_far, pool_own_ref), (pool_other_far, pool_other_ref), (cot_far, cot_ref)]
    feed = Feed(mover, wanted, 3)
    ready()
    for part, columns in enumerate(parts):
        feed.need(2 + part)
        mixed = times(x_ref[...], qkv_ref[:, columns])
        if part == 0:
            mixed = mixed + query_bias_ref[...][None, :]
        if part == 2:
            mixed = mixed + value_bias_ref[...][None, :]
        mixed_ref[:, columns] = mixed.astype(LOW)
    feed.ahead()
    left, right = head_masks(length)
    left_t, right_t = left.T, right.T

    def one_sequence(seq, carry):
        here = pl.ds(pl.multiple_of(seq * length, length), length)
        for pair in range(pairs):
            start = pair * LANES
            query = mixed_ref[here, start : start + LANES]
            key = mixed_ref[here, features + start : features + start + LANES]
            value = mixed_ref[here, 2 * features + start : 2 * features + start + LANES]
            stacked = jnp.concatenate([query * left, query * right], axis=0)
            scores = times_transposed(key, stacked)
            top = jnp.max(scores, axis=0, keepdims=True)
            raised = jnp.exp((scores - top) * factor)
            probs = (raised * (1.0 / column_sum(raised))).astype(LOW)
            probs_ref[pl.ds(seq * pairs + pair, 1)] = probs[None]
            value_t = value.T
            both = jnp.concatenate([value_t * left_t, value_t * right_t], axis=1)
            tall = jnp.concatenate([probs[:, :length], probs[:, length:]], axis=0)
            context_t = times(both, tall).astype(LOW)
            context_ref[here, start : start + LANES] = context_t.T
        return carry

    lax.fori_loop(0, seqs, one_sequence, 0)
    feed.need(5)
    mover.out(mixed_ref, mixed_far)
    mover.out(probs_ref, probs_far)
    mover.out(context_ref, context_far)
    normal_ref[...] = times(context_ref[...], output_ref[...]) + output_bias_ref[...][None, :]
    hidden_square = jnp.zeros((1, features), F32)
    attended_square = jnp.zeros((1, features), F32)
    first_scale = first_scale_ref[...][None, :]
    first_shift = first_shift_ref[...][None, :]
    outer_bias = outer_bias_ref[...][None, :]
    for seq in range(seqs):
        here = slice(seq * length, (seq + 1) * length)
        hidden = x_ref[here, :].astype(F32)
        attended = normal_ref[here, :]
        residual = hidden + attended
        centred = residual - row_sum(residual) * (1.0 / features)
        spread = lax.rsqrt(row_sum(centred * centred) * (1.0 / features) + EPS)
        normal = centred * spread
        normal_ref[here, :] = normal
        spread_ref[here, :] = spread
        first = normal * first_scale + first_shift
        low_ref[here, :] = first.astype(LOW)
        sum_ref[here, :] = first + outer_bias
        hidden_square = hidden_square + column_sum(hidden * hidden)
        attended_square = attended_square + column_sum(attended * attended)
    mover.out(normal_ref, normal_far)

    feed.need(5 + 2 * len(steps))

    def inner_of(columns):
        return times(low_ref[...], inner_ref[:, columns]) + inner_bias_ref[columns][None, :]

    inner = inner_of(steps[0])
    for step, columns in enumerate(steps):
        following = inner_of(steps[step + 1]) if step + 1 < len(steps) else None
        acted, slope = gelu_both(inner)
        acted = acted.astype(LOW)
        acted_ref[:, columns] = acted
        slope_ref[:, columns] = slope.astype(LOW)
        sum_ref[...] += times(acted, outer_ref[columns, :])
        inner = following
    mover.out(slope_ref, slope_far)

    scale = second_scale_ref[...][None, :]
    shift = second_shift_ref[...][None, :]
    square = jnp.zeros((1, features), F32)
    leading = []
    for seq in range(seqs):
        here = slice(seq * length, (seq + 1) * length)
        residual = sum_ref[here, :]
        outer = residual - (normal_ref[here, :] * first_scale + first_shift)
        square = square + column_sum(outer * outer)
        centred = residual - row_sum(residual) * (1.0 / features)
        spread = lax.rsqrt(row_sum(centred * centred) * (1.0 / features) + EPS)
        normal = centred * spread
        sum_ref[here, :] = normal
        second_spread_ref[here, :] = spread
        final = (normal * scale + shift).astype(LOW)
        final_ref[here, :] = final
        leading.append(final[0:1, :].astype(F32))
    mover.out(final_ref, final_far)

    feed.need(len(wanted) - 1)
    leading = jnp.concatenate(leading + [jnp.zeros((8 - seqs, features), F32)], axis=0)
    states = leading.astype(LOW)
    row = lax.broadcasted_iota(jnp.int32, (8, 1), 0)
    ramp_of = jnp.full((8, 1), -1, jnp.int32)
    label_of = jnp.full((8, 1), -1, jnp.int32)
    for seq in range(seqs):
        ramp_of = jnp.where(row == seq, ramps_ref[seq], ramp_of)
        label_of = jnp.where(row == seq, labels_ref[seq], label_of)
    own = ramp_of == core
    pre_own = times(states, pool_own_ref[0]) + pool_bias_own_ref[...]
    pre_other = times(states, pool_other_ref[0]) + pool_bias_other_ref[...]
    pooled = jnp.tanh(jnp.where(own, pre_own, pre_other))
    pooled_low = pooled.astype(LOW)
    logits = jnp.where(
        own,
        times(pooled_low, class_own_ref[0]) + class_bias_own_ref[...],
        times(pooled_low, class_other_ref[0]) + class_bias_other_ref[...],
    )
    logits_ref[...] = logits[:seqs, :]
    raised = jnp.exp(logits - jnp.max(logits, axis=-1, keepdims=True))
    kind = lax.broadcasted_iota(jnp.int32, (8, CLASSES), 1)
    grads = raised / row_sum(raised) - (kind == label_of).astype(F32)
    grads = jnp.where(ramp_of >= 0, grads, 0.0)
    grads_high = grads.astype(LOW)
    grads_rest = (grads - grads_high.astype(F32)).astype(LOW)

    def from_logits(weight):
        return times_transposed(grads_high, weight) + times_transposed(grads_rest, weight)

    pooled_grad = jnp.where(own, from_logits(class_own_ref[0]), from_logits(class_other_ref[0]))
    pre_low = (pooled_grad * (1.0 - pooled * pooled)).astype(LOW).astype(F32)
    pre_own_low = jnp.where(own, pre_low, 0.0).astype(LOW)
    pre_other_low = jnp.where(own, 0.0, pre_low).astype(LOW)
    state_grad = times_transposed(pre_own_low, pool_own_ref[0])
    state_grad = state_grad + times_transposed(pre_other_low, pool_other_ref[0])
    chosen_row = lax.broadcasted_iota(jnp.int32, (8, 8), 0)
    chosen_seq = lax.broadcasted_iota(jnp.int32, (8, 8), 1)
    per_ramp = seqs // ramp_count
    for ref, which, top in ((pair_own_ref, core, 0), (pair_send_ref, 1 - core, 2 * per_ramp)):
        pick_states = jnp.zeros((8, 8), jnp.bool_)
        pick_grads = jnp.zeros((8, 8), jnp.bool_)
        for seq in range(seqs):
            rank = jnp.int32(0)
            for other in range(seq):
                rank = rank + (ramps_ref[other] == which).astype(jnp.int32)
            here = (chosen_seq == seq) & (ramps_ref[seq] == which)
            pick_states = pick_states | (here & (chosen_row == top + rank))
            pick_grads = pick_grads | (here & (chosen_row == top + per_ramp + rank))
        rows_of_pair = times(pick_states.astype(F32).astype(LOW), states)
        rows_of_pair = rows_of_pair + times(pick_grads.astype(F32).astype(LOW), pre_low.astype(LOW))
        folded = jnp.concatenate([rows_of_pair[:, : features // 2], rows_of_pair[:, features // 2 :]], axis=0)
        ref[...] = folded.astype(LOW)

    vector_ref[...] = jnp.zeros(vector_ref.shape, F32)
    for ramp in range(ramp_count):
        mask = ramp_of == ramp
        base = 8 * (ramp + 1)
        vector_ref[base : base + 1, :] = column_sum(jnp.where(mask, pre_low, 0.0))
        high = jnp.where(mask, grads_high.astype(F32), 0.0).astype(LOW)
        rest = jnp.where(mask, grads_rest.astype(F32), 0.0).astype(LOW)
        vector_ref[base + 1 : base + 1 + CLASSES, :] = first_times(high, pooled_low) + first_times(
            rest, pooled_low
        )
        vector_ref[base + 4 : base + 5, 0:CLASSES] = column_sum(jnp.where(mask, grads, 0.0))

    feed.need(len(wanted))
    scale_grad = jnp.zeros((1, features), F32)
    shift_grad = jnp.zeros((1, features), F32)
    bias_grad = jnp.zeros((1, features), F32)
    at_first = lax.broadcasted_iota(jnp.int32, (length, 1), 0) == 0
    for seq in range(seqs):
        here = slice(seq * length, (seq + 1) * length)
        final_grad = cot_ref[here, :].astype(F32)
        final_grad = final_grad + jnp.where(at_first, state_grad[seq : seq + 1, :], 0.0)
        normal = sum_ref[here, :]
        scale_grad = scale_grad + column_sum(final_grad * normal)
        shift_grad = shift_grad + column_sum(final_grad)
        scaled = final_grad * scale
        resid = second_spread_ref[here, :] * (
            scaled
            - row_sum(scaled) * (1.0 / features)
            - normal * (row_sum(scaled * normal) * (1.0 / features))
        )
        resid_ref[here, :] = resid
        low = resid.astype(LOW)
        full_ref[here, :] = low
        bias_grad = bias_grad + column_sum(low.astype(F32))
    mover.out(full_ref, full_far)
    mover.out(resid_ref, resid_far)
    size = hidden_units // place.dp
    half = features // 2
    def leave(step):
        first = step * features // size
        source = outer_ref.at[steps[step]]
        place.out(mover, source, half_of(1 - core, half), sends, 1 - core, first, size)
        place.out(mover, source, half_of(core, half), owns, core, first, size)

    middle = len(steps) // 2
    for step, columns in enumerate(steps):
        outer_ref[columns, :] = first_times(acted_ref[:, columns], full_ref[...]).astype(LOW)
        if step + 1 == middle:
            for one in range(middle):
                leave(one)
    for one in range(middle, len(steps)):
        leave(one)
    vector_ref[0:1, :] = bias_grad
    vector_ref[1:2, :] = scale_grad
    vector_ref[2:3, :] = shift_grad
    vector_ref[3:4, 0:1] = row_sum(hidden_square)
    vector_ref[3:4, 1:2] = row_sum(attended_square)
    vector_ref[3:4, 2:3] = row_sum(square)
    return mover


def feed_backward(
    place, length, ready,
    full_far, slope_far, outer_far, inner_far, resid_far, normal_far,
    first_scale_ref, first_shift_ref, after_far,
    first_grad_far, vector_ref, *refs,
):
    sends, owns, refs = refs[: place.count], refs[place.count : place.count + 1], refs[place.count + 1 :]
    full_ref, slope_ref, outer_ref, inner_ref, sum_ref, normal_ref, weight_ref, first_ref, sems = refs
    rows, features = normal_ref.shape
    core = lax.axis_index("ramp")
    hidden_units = slope_ref.shape[1]
    half = hidden_units // 2
    mover = Mover(sems)
    order = []
    for fars, who in ((sends, 1 - core), (owns, core)):
        for start in range(0, half, features):
            number = who * (half // features) + start // features
            columns = pl.ds(pl.multiple_of(number * features, LANES), features)
            order.append((fars, who, start, number, columns))
    wanted = [(full_far, full_ref)]
    for _, _, _, _, columns in order:
        wanted.append((outer_far.at[columns], outer_ref.at[columns]))
        wanted.append((slope_far.at[:, columns], slope_ref.at[:, columns]))
        if len(wanted) == 3:
            wanted.append((normal_far, normal_ref))
        wanted.append((inner_far.at[:, columns], inner_ref.at[:, columns]))
        if len(wanted) == 5:
            wanted.append((resid_far, sum_ref))
    feed = Feed(mover, wanted, 7)
    ready()
    scale = first_scale_ref[...][None, :]
    vector_ref[...] = jnp.zeros(vector_ref.shape, F32)
    size = features // place.dp

    def acted_grad_of(step):
        return times_transposed(full_ref[...], outer_ref[order[step][4], :])

    feed.need(2)
    acted_grad = acted_grad_of(0)
    feed.need(4)
    first_ref[...] = (normal_ref[...] * scale + first_shift_ref[...][None, :]).astype(LOW)
    for step, (fars, who, start, number, columns) in enumerate(order):
        feed.need(min(6 + 3 * step + 1, len(wanted)))
        following = acted_grad_of(step + 1) if step + 1 < len(order) else None
        inner_grad = (slope_ref[:, columns].astype(F32) * acted_grad).astype(LOW)
        vector_ref[pl.ds(number, 1), :] = column_sum(inner_grad.astype(F32))
        sum_ref[...] += times_transposed(inner_grad, inner_ref[:, columns])
        here = slice(step * features, (step + 1) * features)
        weight_ref[:, here] = first_times(first_ref[...], inner_grad).astype(LOW)
        place.out(None, weight_ref, here, fars, who, 0, size, start)
        acted_grad = following
    mover.out(sum_ref, first_grad_far)
    return mover


def attention_backward(
    place, length, ready,
    first_grad_far, normal_far, spread_ref, first_scale_ref, output_far, context_far,
    mixed_far, probs_far, x_far, after_far,
    grad_far, first_resid_far, vector_ref, *refs,
):
    sends, owns, refs = refs[: place.count], refs[place.count : place.count + 1], refs[place.count + 1 :]
    (
        first_grad_ref, normal_ref, output_ref, context_ref, low_ref, first_resid_ref,
        mixed_ref, probs_ref, context_grad_ref, x_ref, grad_ref, weight_ref, sems, out_sems,
    ) = refs
    rows, features = context_grad_ref.shape
    seqs = rows // length
    core = lax.axis_index("ramp")
    pairs = features // LANES
    factor = (features // HEADS) ** (-0.5)
    half = features // 2
    size = features // place.dp
    left, right = head_masks(length)
    mover = Mover(out_sems)
    wanted = [
        (first_grad_far, first_grad_ref),
        (normal_far, normal_ref),
        (output_far, output_ref),
        (context_far, context_ref),
    ]
    feed = Feed(mover, wanted, len(wanted))

    def copies(seq):
        here = pl.ds(pl.multiple_of(seq * length, length), length)
        heads = pl.ds(seq * pairs, pairs)
        return (
            pltpu.make_async_copy(mixed_far.at[here], mixed_ref.at[here], sems.at[0, seq]),
            pltpu.make_async_copy(probs_far.at[heads], probs_ref.at[heads], sems.at[1, seq]),
        )

    for seq in range(seqs):
        for copy in copies(seq):
            copy.start()
    got_x = mover.start(x_far, x_ref)
    ready()
    feed.need(2)
    scale = first_scale_ref[...][None, :]
    zero = jnp.zeros((1, features), F32)
    sums = [zero, zero, zero]
    for seq in range(seqs):
        here = slice(seq * length, (seq + 1) * length)
        first_grad = first_grad_ref[here, :]
        normal = normal_ref[here, :]
        scaled = first_grad * scale
        resid = spread_ref[here, :] * (
            scaled
            - row_sum(scaled) * (1.0 / features)
            - normal * (row_sum(scaled * normal) * (1.0 / features))
        )
        first_resid_ref[here, :] = resid
        low = resid.astype(LOW)
        low_ref[here, :] = low
        sums[0] = sums[0] + column_sum(low.astype(F32))
        sums[1] = sums[1] + column_sum(first_grad * normal)
        sums[2] = sums[2] + column_sum(first_grad)
    mover.out(first_resid_ref, first_resid_far)
    feed.need(len(wanted))
    context_grad_ref[...] = times_transposed(low_ref[...], output_ref[...]).astype(LOW)
    columns = slice(3 * features, 4 * features)
    weight_ref[:, columns] = first_times(context_ref[...], low_ref[...]).astype(LOW)
    for fars, who in ((sends, 1 - core), (owns, core)):
        columns = pl.ds(pl.multiple_of(3 * features + who * half, LANES), half)
        place.out(None, weight_ref, columns, fars, who, 0, size, 3 * half)

    def one_sequence(seq, carry):
        here = pl.ds(pl.multiple_of(seq * length, length), length)
        for copy in copies(seq):
            copy.wait()
        for pair in range(pairs):
            start = pair * LANES
            query = mixed_ref[here, start : start + LANES]
            key = mixed_ref[here, features + start : features + start + LANES]
            value = mixed_ref[here, 2 * features + start : 2 * features + start + LANES]
            context_grad = context_grad_ref[here, start : start + LANES]
            queries = jnp.concatenate([query * left, query * right], axis=0)
            keys = jnp.concatenate([key * left, key * right], axis=0)
            grads = jnp.concatenate([context_grad * left, context_grad * right], axis=0)
            probs = probs_ref[pl.ds(seq * pairs + pair, 1)][0]
            probs_grad = times_transposed(value, grads)
            wide = probs.astype(F32)
            score_grad = wide * (probs_grad - column_sum(wide * probs_grad))
            score_grad = score_grad.astype(LOW)
            value_grad = times(probs, grads).astype(LOW)
            key_grad = (times(score_grad, queries) * factor).astype(LOW)
            turned = jnp.concatenate(
                [score_grad[:, :length].T, score_grad[:, length:].T], axis=1
            )
            query_grad = (times(turned, keys) * factor).astype(LOW)
            grad_ref[here, start : start + LANES] = query_grad
            grad_ref[here, features + start : features + start + LANES] = key_grad
            grad_ref[here, 2 * features + start : 2 * features + start + LANES] = value_grad
        return carry

    lax.fori_loop(0, seqs, one_sequence, 0)
    mover.out(grad_ref, grad_far)
    got_x.wait()
    for fars, who in ((sends, 1 - core), (owns, core)):
        for start, width in ((0, features), (features, half)):
            columns = pl.ds(pl.multiple_of(who * 3 * half + start, LANES), width)
            weight_ref[:, columns] = first_times(x_ref[...], grad_ref[:, columns]).astype(LOW)
            place.out(None, weight_ref, columns, fars, who, 0, size, start)
    vector_ref[...] = jnp.zeros(vector_ref.shape, F32)
    vector_ref[0:1, :] = column_sum(grad_ref[:, :features].astype(F32))
    vector_ref[1:2, :] = column_sum(grad_ref[:, 2 * features :].astype(F32))
    for number, one in enumerate(sums):
        vector_ref[2 + number : 3 + number, :] = one
    return mover


def input_gradient(
    ready,
    grad_far, qkv_far, resid_far, after_far,
    result_far, token_far,
    grad_ref, qkv_ref, resid_ref, result_ref, sems,
):
    mover = Mover(sems)
    features = resid_ref.shape[1]
    parts = [slice(part * features, (part + 1) * features) for part in range(3)]
    got = []
    for one in parts:
        got.append(
            (
                mover.start(grad_far.at[:, one], grad_ref.at[:, one]),
                mover.start(qkv_far.at[:, one], qkv_ref.at[:, one]),
            )
        )
    got_resid = mover.start(resid_far, resid_ref)
    total = None
    for columns, copies in zip(parts, got):
        for copy in copies:
            copy.wait()
        product = times_transposed(grad_ref[:, columns], qkv_ref[:, columns])
        total = product if total is None else total + product
    got_resid.wait()
    result_ref[...] = (resid_ref[...] + total).astype(LOW)
    mover.out(result_ref, result_far)
    return mover


def swap_core(values):
    return lax.ppermute(values, "ramp", [(0, 1), (1, 0)])


def shift(values, even, odd):
    dp = lax.axis_size("dp")
    pairs = []
    for one in range(dp):
        pairs.append((2 * one, 2 * (one ^ even)))
        pairs.append((2 * one + 1, 2 * (one ^ odd) + 1))
    return lax.ppermute(values, ("dp", "ramp"), pairs)


RIDERS = 16


def pack(ref, total, top, beside):
    high = total.astype(LOW)
    rest = (total - high.astype(F32)).astype(LOW)
    count = total.shape[0] // RIDERS
    if beside is not None:
        spots = rider_spots(ref.shape[0], total.shape[0])
        ref[:, beside:] = jnp.zeros((ref.shape[0], ref.shape[1] - beside), LOW)
        for values, number, row, start in spots:
            part = (high, rest)[values][number * RIDERS : (number + 1) * RIDERS, :]
            ref[row : row + RIDERS, beside + start : beside + start + LANES] = part
        return
    ref[top : top + RIDERS, :] = jnp.zeros((RIDERS, ref.shape[1]), LOW)
    for number in range(count):
        rows = slice(number * RIDERS, (number + 1) * RIDERS)
        for part, values in enumerate((high, rest)):
            start = (part * count + number) * LANES
            ref[top : top + RIDERS, start : start + LANES] = values[rows, :]


def rider_spots(height, rows):
    spots = []
    for number in range(rows // RIDERS):
        below, beside = number % (height // RIDERS), number // (height // RIDERS)
        spots.append((0, number, below * RIDERS, beside * LANES))
    return spots


def rider_width(height, rows):
    return rider_spots(height, rows)[-1][3] + LANES


def unpack(ref, count, top, beside):
    parts = [None] * count
    if beside is not None:
        for _, number, row, start in rider_spots(ref.shape[0], count * RIDERS):
            term = ref[row : row + RIDERS, beside + start : beside + start + LANES].astype(F32)
            parts[number] = term if parts[number] is None else parts[number] + term
    else:
        for number in range(count):
            start, rest = number * LANES, (count + number) * LANES
            high = ref[top : top + RIDERS, start : start + LANES].astype(F32)
            parts[number] = high + ref[top : top + RIDERS, rest : rest + LANES].astype(F32)
    return parts[0] if count == 1 else jnp.concatenate(parts, axis=0)


def combine(plan, count, rider, ready, *refs):
    arrays, results = refs[:count], refs[count:]
    if rider is not None:
        plain, packed, into, beside = rider
        out_ref = results[len(plan)]
        total = None
        for number in plain:
            total = arrays[number][...] if total is None else total + arrays[number][...]
        for number, top, side in packed:
            total = total + unpack(arrays[number], total.shape[0] // RIDERS, top, side)
        out_ref[...] = total
    for number, (parts, result) in enumerate(zip(plan, results)):
        top = 0
        for rows, width, terms in parts:
            total_rows = None
            wide = len(terms) > 2
            for array, row, column in terms:
                term = arrays[array][row : row + rows, column : column + width]
                term = term.astype(F32) if wide else term
                total_rows = term if total_rows is None else total_rows + term
            result[top : top + rows, :width] = total_rows.astype(result.dtype)
            top += rows
        if rider is not None and number in into:
            pack(result, total, top, parts[0][1] if beside else None)


def combined(results, after=(), rider=None):
    arrays = []

    def number(array):
        for place, one in enumerate(arrays):
            if one is array:
                return place
        arrays.append(array)
        return len(arrays) - 1

    plan = [
        [(rows, width, [(number(array), row, column) for array, row, column in terms]) for rows, terms in parts]
        for width, _, parts in results
    ]
    ride, extra, into, beside = None, [], (), False
    if rider is not None:
        plain, packed, into, *rest = rider
        beside = bool(rest)
        ride = ([number(one) for one in plain], [(number(one), *where) for one, *where in packed], into, beside)
        extra = [(plain[0].shape, F32, NEAR)]
    shapes = []
    for place, (width, kind, parts) in enumerate(results):
        height = sum(part[0] for part in parts)
        if place in into and beside:
            width = width + rider_width(height, plain[0].shape[0])
        elif place in into:
            height = height + RIDERS
        shapes.append(((height, width), kind))
    return call(
        partial(combine, plan, len(arrays) + len(after), ride),
        [(shape, kind, NEAR) for shape, kind in shapes] + extra + [((8, LANES), F32, FAR)],
        [(array, NEAR) for array in arrays] + [(array, FAR) for array in after],
        nbytes=sum(8 * shape[0] * shape[1] for shape, _ in shapes),
        limit=SMALL_BYTES,
    )


class Chain:
    def __init__(self, sends, own):
        self.own = own
        self.got = [swap_core(one) for one in sends]
        self.heights = [one.shape[0] for one in sends]
        self.width = own.shape[1]

    def come(self, start, count, skip=0):
        spans = []
        top = 0
        for one, height in zip(self.got, self.heights):
            low, high = max(start, top), min(start + count, top + height)
            if low < high:
                spans.append((high - low, (one, low - top, 0)))
            top += height
        return spans

    def parts(self, start, count):
        result = []
        for rows, place in self.come(start, count):
            result.append((rows, [(self.own, start, 0), place]))
            start += rows
        return result

    def halves(self, pieces):
        rows = self.own.shape[0] // 2
        size = rows // pieces
        spans = [(start, size) for start in range(0, rows, size)] + [(rows, rows)]
        return [(self.width, LOW, self.parts(*span)) for span in spans]

    def add_first(self, pieces=1):
        return self.halves(pieces)

    def send_first(self, *arrays):
        self.send(arrays, 1, 2)

    def send(self, arrays, even, odd):
        self.got, self.own = [shift(one, even, odd) for one in arrays[:-1]], arrays[-1]
        self.heights = [self.own.shape[0] // (len(arrays) - 1)] * (len(arrays) - 1)

    def add_second(self, pieces=1):
        return self.halves(pieces)

    def send_second(self, *arrays):
        self.send(arrays, 2, 1)

    def add_third(self):
        rows = self.own.shape[0] // 4
        return [(self.width, LOW, self.parts(start * rows, rows)) for start in range(4)]

    def send_third(self, *arrays):
        self.planes = [
            shift(one, (number + 1) << 2, (number + 1) << 2) for number, one in enumerate(arrays[:3])
        ]
        self.own = arrays[3]

    def rider(self):
        return (self.got[0], self.got[0].shape[0] - RIDERS, None)

    def riders(self):
        return [(one, 0, self.width) for one in self.planes]

    def gather(self, results, number, *terms):
        width, kind, parts = results[number]
        results[number] = (width, kind, parts + list(terms))
        return results

    def add_last(self, widths):
        results = []
        start = 0
        for width in widths:
            terms = [(array, 0, start) for array in [self.own] + self.planes]
            results.append((width, F32, [(self.own.shape[0], terms)]))
            start += width
        return results

    def plain(self, widths):
        total = (self.own.astype(F32) + self.got[0].astype(F32)).astype(LOW)
        rows = lax.psum_scatter(total, "dp", scatter_dimension=0, tiled=True).astype(F32)
        ends = [sum(widths[: one + 1]) for one in range(len(widths))]
        return [rows[:, end - width : end] for width, end in zip(widths, ends)]


EARLY_ROWS, LATE_ROWS = 96, 32


def put_rows(out_ref, place, row):
    for start in range(0, row.shape[1], LANES):
        out_ref[place : place + 1, :] = row[:, start : start + LANES]
        place += 1
    return place


def collect_late(ready, mixed_ref, after_far, out_ref):
    ready()
    out_ref[...] = jnp.zeros(out_ref.shape, F32)
    place = 0
    for number in range(5):
        place = put_rows(out_ref, place, mixed_ref[number : number + 1, :])


def collect_early(ready, first_ref, second_ref, after_far, out_ref):
    ready()
    out_ref[...] = jnp.zeros(out_ref.shape, F32)
    place = 0
    for number in range(first_ref.shape[0] // 2):
        place = put_rows(out_ref, place, first_ref[number : number + 1, :])
    for number in range(3):
        place = put_rows(out_ref, place, second_ref[number : number + 1, :])
    for base in (8, 16):
        for number in range(1 + CLASSES):
            place = put_rows(out_ref, place, second_ref[base + number : base + number + 1, :])
    for number in (3, 12, 20):
        place = put_rows(out_ref, place, second_ref[number : number + 1, :LANES])


def add_all(ready, *refs):
    ready()
    *refs, after_far, out_ref = refs
    total = refs[0][...]
    for ref in refs[1:]:
        total = total + ref[...]
    out_ref[...] = total


def add_over(values, masks, after=None):
    got = [shift(values, mask, mask) for mask in masks]
    (total,) = call(
        add_all,
        [(values.shape, values.dtype, VMEM)],
        [(one, VMEM) for one in [values] + got] + [((after or [values])[0], FAR)],
        limit=SMALL_BYTES,
    )
    return total


def take_rows(all_ref, place, ref, start, width):
    for column in range(0, width, LANES):
        ref[pl.ds(start + column, LANES)] = all_ref[place, :]
        place += 1
    return place


def hand_out(features, entries, ready, all_ref, late_ref, *outs):
    ready()
    place = 0
    for ref in outs[8:]:
        place = take_rows(late_ref, place, ref, 0, features)
    outs = outs[:8]
    core = lax.axis_index("ramp")
    rms_ref, inner_ref, outer_ref, second_scale_ref, second_shift_ref = outs[:5]
    pool_ref, class_ref, class_bias_ref = outs[5:]
    place = 0
    for ref in (inner_ref, outer_ref, second_scale_ref, second_shift_ref):
        place = take_rows(all_ref, place, ref, 0, ref.shape[0])
    step = features // LANES
    size = step * (1 + CLASSES)
    for column in range(step):
        at = column * LANES
        first = all_ref[place + column : place + column + 1, :]
        second = all_ref[place + size + column : place + size + column + 1, :]
        pool_ref[:, at : at + LANES] = jnp.where(core == 0, first, second)
        for kind in range(CLASSES):
            row = place + (1 + kind) * step + column
            first = all_ref[row : row + 1, :]
            second = all_ref[row + size : row + size + 1, :]
            class_ref[kind : kind + 1, at : at + LANES] = jnp.where(core == 0, first, second)
    place += 2 * size
    rms_ref[...] = jnp.sqrt(all_ref[place : place + 1, :] * (1.0 / entries))
    first = all_ref[place + 1 : place + 2, :CLASSES]
    second = all_ref[place + 2 : place + 3, :CLASSES]
    class_bias_ref[...] = jnp.where(core == 0, first, second)


def pool_gradient(ready, pair_ref, after_far, out_ref, token_far, all_ref):
    ready()
    height, half = pair_ref.shape
    blocks = pair_ref[...].astype(F32).reshape(height // 16, 16, half)
    rows = jnp.concatenate([blocks[:, 0:8, :], blocks[:, 8:16, :]], axis=2)
    rows = rows.reshape(height // 2, 2 * half).astype(LOW)
    at = lax.broadcasted_iota(jnp.int32, (height // 2, height // 2), 0)
    beyond = lax.broadcasted_iota(jnp.int32, (height // 2, height // 2), 1)
    moved = ((beyond == at + 2) & (at % 4 < 2)).astype(F32).astype(LOW)
    all_ref[...] = first_times(rows, times(moved, rows).astype(LOW))
    count = out_ref.shape[0]
    out_ref[...] = all_ref[pl.ds(pl.multiple_of(lax.axis_index("dp") * count, 8), count), :]


def on_device(
    hidden_in, cotangent, qkv_weight, query_bias, value_bias, output_weight, output_bias,
    first_scale, first_shift, inner_weight, inner_bias, outer_weight, outer_bias,
    second_scale, second_shift, pool_weight, pool_bias, class_weight, class_bias,
    labels, ramp_index,
):
    rows, features = hidden_in.shape
    seqs = labels.shape[0]
    length = rows // seqs
    units = inner_weight.shape[1]
    dp = lax.axis_size("dp")
    ramps = lax.axis_size("ramp")
    pairs = features // LANES
    place = Place(dp, features)
    half = features // 2

    pool_other = swap_core(pool_weight)
    pool_bias_other = swap_core(pool_bias)
    class_other = swap_core(class_weight)
    class_bias_other = swap_core(class_bias)
    (
        mixed, probs, context, normal, spread, output, logits, slope, second_resid, outer_full,
        second_vector, pair_own, pair_send, *outer_parts,
    ) = call(
        partial(forward, place, length, ramps),
        [
            ((rows, 3 * features), LOW, FAR),
            ((seqs * pairs, length, 2 * length), LOW, FAR),
            ((rows, features), LOW, FAR),
            ((rows, features), F32, FAR),
            ((rows, 1), F32, VMEM),
            ((rows, features), LOW, FAR),
            ((seqs, CLASSES), F32, VMEM),
            ((rows, units), LOW, FAR),
            ((rows, features), F32, FAR),
            ((rows, features), LOW, FAR),
            ((8 * (ramps + 1), features), F32, VMEM),
            ((16, half), LOW, VMEM),
            ((16, half), LOW, VMEM),
        ]
        + [((units // place.count, half), LOW, FAR)] * place.count
        + [((units, half), LOW, FAR)],
        [
            (hidden_in, FAR),
            (qkv_weight, FAR),
            (query_bias, VMEM),
            (value_bias, VMEM),
            (output_weight, FAR),
            (output_bias, VMEM),
            (first_scale, VMEM),
            (first_shift, VMEM),
            (inner_weight, FAR),
            (inner_bias, VMEM),
            (outer_weight, FAR),
            (outer_bias, VMEM),
            (second_scale, VMEM),
            (second_shift, VMEM),
            (cotangent, FAR),
            (pool_weight, FAR),
            (pool_other, FAR),
            (pool_bias, VMEM),
            (pool_bias_other, VMEM),
            (class_weight, VMEM),
            (class_other, VMEM),
            (class_bias, VMEM),
            (class_bias_other, VMEM),
            (labels, SMEM),
            (ramp_index, SMEM),
        ],
        scratch=[
            pltpu.VMEM((rows, features), LOW),
            pltpu.VMEM((features, 3 * features), LOW),
            pltpu.VMEM((features, features), LOW),
            pltpu.VMEM((rows, 3 * features), LOW),
            pltpu.VMEM((seqs * pairs, length, 2 * length), LOW),
            pltpu.VMEM((rows, features), LOW),
            pltpu.VMEM((rows, features), F32),
            pltpu.VMEM((features, units), LOW),
            pltpu.VMEM((units, features), LOW),
            pltpu.VMEM((rows, features), LOW),
            pltpu.VMEM((1, features, features), LOW),
            pltpu.VMEM((1, features, features), LOW),
            pltpu.VMEM((rows, features), LOW),
            pltpu.VMEM((rows, units), LOW),
            pltpu.VMEM((rows, units), LOW),
            pltpu.VMEM((rows, features), F32),
            pltpu.VMEM((rows, features), LOW),
            pltpu.VMEM((rows, features), LOW),
            pltpu.VMEM((rows, features), F32),
            pltpu.VMEM((rows, 1), F32),
            pltpu.SemaphoreType.DMA((16 + 3 * (units // features) + 2 * dp,)),
        ],
        flops=2 * rows * features * (4 * features + 3 * units) + 8 * rows * features * length,
        nbytes=40 << 20,
        limit=VMEM_BYTES,
    )
    outer_chain = Chain(outer_parts[: place.count], outer_parts[place.count])
    pair_other = swap_core(pair_send)
    token = second_vector
    if place.fast:
        shared = [(pair_own, 0, 0), (pair_other, 0, 0)]
        results = outer_chain.gather(outer_chain.add_first(), 0, (16, shared))
        *sends, pair, token = combined(results + [(half, LOW, [(16, shared)])])
        outer_chain.send_first(*sends)

    first_grad, first_vector, *inner_parts = call(
        partial(feed_backward, place, length),
        [((rows, features), F32, FAR), ((8, features), F32, VMEM)]
        + [((features // place.count, units // 2), LOW, NEAR)] * place.count
        + [((features, units // 2), LOW, NEAR)],
        [
            (outer_full, FAR),
            (slope, FAR),
            (outer_weight, FAR),
            (inner_weight, FAR),
            (second_resid, FAR),
            (normal, FAR),
            (first_scale, VMEM),
            (first_shift, VMEM),
            (token, FAR),
        ],
        scratch=[
            pltpu.VMEM((rows, features), LOW),
            pltpu.VMEM((rows, units), LOW),
            pltpu.VMEM((units, features), LOW),
            pltpu.VMEM((features, units), LOW),
            pltpu.VMEM((rows, features), F32),
            pltpu.VMEM((rows, features), F32),
            pltpu.VMEM((features, units), LOW),
            pltpu.VMEM((rows, features), LOW),
            pltpu.SemaphoreType.DMA((8 + 3 * (units // features),)),
        ],
        flops=6 * rows * features * units,
        nbytes=25 << 20,
        limit=44 << 20,
    )
    inner_chain = Chain(inner_parts[: place.count], inner_parts[place.count])
    token = first_vector
    if place.fast:
        low = outer_chain.got[0].shape[0] - 16
        shared = [(16, [(pair, 0, 0)]), (16, [(outer_chain.got[0], low, 0)])]
        results = outer_chain.gather(outer_chain.add_second(), 0, *shared)
        *sends, pair, token = combined(results + [(half, LOW, shared)], after=[first_vector])
        outer_chain.send_second(*sends)
    (early,) = call(
        collect_early,
        [((EARLY_ROWS, LANES), F32, VMEM)],
        [(first_vector, VMEM), (second_vector, VMEM), (token, FAR)],
        limit=SMALL_BYTES,
    )
    early_other = swap_core(early)
    if place.fast:
        *sends, early, token = combined(
            inner_chain.add_first(), after=[token], rider=([early, early_other], [], (0,))
        )
        inner_chain.send_first(*sends)

    mixed_grad, first_resid, mixed_vector, *qkv_parts = call(
        partial(attention_backward, place, length),
        [((rows, 3 * features), LOW, FAR), ((rows, features), F32, FAR), ((8, features), F32, VMEM)]
        + [((features // place.count, 4 * half), LOW, NEAR)] * place.count
        + [((features, 4 * half), LOW, NEAR)],
        [
            (first_grad, FAR),
            (normal, FAR),
            (spread, VMEM),
            (first_scale, VMEM),
            (output_weight, FAR),
            (context, FAR),
            (mixed, FAR),
            (probs, FAR),
            (hidden_in, FAR),
            (token, FAR),
        ],
        scratch=[
            pltpu.VMEM((rows, features), F32),
            pltpu.VMEM((rows, features), F32),
            pltpu.VMEM((features, features), LOW),
            pltpu.VMEM((rows, features), LOW),
            pltpu.VMEM((rows, features), LOW),
            pltpu.VMEM((rows, features), F32),
            pltpu.VMEM((rows, 3 * features), LOW),
            pltpu.VMEM((seqs * pairs, length, 2 * length), LOW),
            pltpu.VMEM((rows, features), LOW),
            pltpu.VMEM((rows, features), LOW),
            pltpu.VMEM((rows, 3 * features), LOW),
            pltpu.VMEM((features, 4 * features), LOW),
            pltpu.SemaphoreType.DMA((2, seqs)),
            pltpu.SemaphoreType.DMA((8,)),
        ],
        flops=20 * rows * features * length + 10 * rows * features * features,
        nbytes=12 << 20,
        limit=36 << 20,
    )
    qkv_chain = Chain(qkv_parts[: place.count], qkv_parts[place.count])
    token = mixed_vector
    if place.fast:
        low = outer_chain.got[0].shape[0] - 32
        shared = [(32, [(pair, 0, 0)]), (32, [(outer_chain.got[0], low, 0)])]
        results = outer_chain.add_third()
        for number in range(3):
            outer_chain.gather(results, number, *shared)
        *sends, pair, early, token = combined(
            results + inner_chain.add_second() + [(half, LOW, shared)],
            after=[mixed_vector],
            rider=([early], [inner_chain.rider()], (4,)),
        )
        outer_chain.send_third(*sends[:4])
        inner_chain.send_second(*sends[4:])
    (late,) = call(
        collect_late,
        [((LATE_ROWS, LANES), F32, VMEM)],
        [(mixed_vector, VMEM), (mixed_vector, FAR)],
        limit=SMALL_BYTES,
    )
    late_other = swap_core(late)

    if place.fast:
        *sends, late, token = combined(
            qkv_chain.add_first(), after=[token], rider=([late, late_other], [], (0,))
        )
        qkv_chain.send_first(*sends)
    input_grad, token = call(
        input_gradient,
        [((rows, features), LOW, FAR), ((8, LANES), F32, FAR)],
        [(mixed_grad, FAR), (qkv_weight, FAR), (first_resid, FAR), (token, FAR)],
        scratch=[
            pltpu.VMEM((rows, 3 * features), LOW),
            pltpu.VMEM((features, 3 * features), LOW),
            pltpu.VMEM((rows, features), F32),
            pltpu.VMEM((rows, features), LOW),
            pltpu.SemaphoreType.DMA((8,)),
        ],
        flops=6 * rows * features * features,
        nbytes=10 << 20,
        limit=20 << 20,
    )

    if place.fast:
        late, token = combined([], after=[token], rider=([late], [qkv_chain.rider()], ()))
        low = outer_chain.planes[0].shape[0] - 64
        shared = [(64, [(pair, 0, 0)])] + [(64, [(one, low, 0)]) for one in outer_chain.planes]
        *sends, outer_sum, pair, early, token = combined(
            inner_chain.add_third()
            + qkv_chain.add_second()
            + outer_chain.add_last([half])
            + [(half, LOW, shared)],
            after=[token],
            rider=([early], [inner_chain.rider()], (0, 1, 2), True),
        )
        inner_chain.send_third(*sends[:4])
        qkv_chain.send_second(*sends[4:])
        late_other = shift(late, 2, 1)
        pool_sum, token = call(
            pool_gradient,
            [((features // dp, features), F32, VMEM), ((8, LANES), F32, FAR)],
            [(pair, VMEM), (token, FAR)],
            scratch=[pltpu.VMEM((features, features), F32)],
            limit=SMALL_BYTES,
        )
        *sends, inner_sum, late, token = combined(
            qkv_chain.add_third() + inner_chain.add_last([units // 2]),
            after=[token],
            rider=([late, late_other], [], (0, 1, 2), True),
        )
        qkv_chain.send_third(*sends)
        early, token = combined([], after=[token], rider=([early], inner_chain.riders(), ()))
        qkv_sum, output_sum, late, token = combined(
            qkv_chain.add_last([3 * half, half]),
            rider=([late], qkv_chain.riders(), ()),
        )
    else:
        early = add_over(early + early_other, list(range(1, dp)))
        late = add_over(late + late_other, list(range(1, dp)))
    if not place.fast:
        pair = lax.all_gather(pair_own + pair_other, "dp")
        pair = pair.reshape(dp, 2, 2, 2, seqs // ramps, half)
        pair = jnp.moveaxis(pair, 1, 4).reshape(dp, 2, 2, seqs // ramps, features)
        states = pair[:, :, 0].reshape(-1, features)
        pre_grads = pair[:, :, 1].reshape(-1, features)
        own_rows = features // dp
        states = lax.dynamic_slice_in_dim(
            states, lax.axis_index("dp") * own_rows, own_rows, axis=1
        )
        pool_sum = first_times(states, pre_grads)
        (outer_sum,) = outer_chain.plain([half])
        (inner_sum,) = inner_chain.plain([units // 2])
        qkv_sum, output_sum = qkv_chain.plain([3 * half, half])
    (
        rms, inner_bias_sum, outer_bias_sum, second_scale_sum, second_shift_sum,
        pool_bias_sum, class_sum, class_bias_sum,
        query_bias_sum, value_bias_sum, output_bias_sum, first_scale_sum, first_shift_sum,
    ) = call(
        partial(hand_out, features, rows * features * dp * ramps),
        [((1, LANES), F32, VMEM)]
        + [((units,), F32, VMEM)]
        + [((features,), F32, VMEM)] * 3
        + [((1, features), F32, VMEM), ((CLASSES, features), F32, VMEM), ((1, CLASSES), F32, VMEM)]
        + [((features,), F32, VMEM)] * 5,
        [(early, VMEM), (late, VMEM)],
        limit=SMALL_BYTES,
    )
    return (
        output,
        logits,
        rms[0, :3],
        input_grad,
        qkv_sum,
        query_bias_sum,
        value_bias_sum,
        output_sum,
        output_bias_sum,
        first_scale_sum,
        first_shift_sum,
        inner_sum,
        inner_bias_sum,
        outer_sum,
        outer_bias_sum,
        second_scale_sum,
        second_shift_sum,
        pool_sum[None],
        pool_bias_sum,
        class_sum.T[None],
        class_bias_sum,
    )


def solution(mesh):
    whole = P(("dp", "ramp"), None)
    return jax.shard_map(
        on_device,
        mesh=mesh,
        in_specs=(whole, whole)
        + (P(),) * 13
        + (
            P("ramp", None, None),
            P("ramp", None),
            P("ramp", None, None),
            P("ramp", None),
            P(("dp", "ramp")),
            P(("dp", "ramp")),
        ),
        out_specs=(
            whole,
            whole,
            P(),
            whole,
            P("dp", "ramp"),
            P(),
            P(),
            P("dp", "ramp"),
            P(),
            P(),
            P(),
            P("dp", "ramp"),
            P(),
            P("dp", "ramp"),
            P(),
            P(),
            P(),
            P("ramp", "dp", None),
            P("ramp", None),
            P("ramp", None, None),
            P("ramp", None),
        ),
        check_vma=False,
    )
```

```python
from functools import partial

import jax
import jax.numpy as jnp
from jax import lax
from jax.experimental import pallas as pl
from jax.experimental.pallas import tpu as pltpu
from jax.sharding import PartitionSpec as P

HEADS = 12
CLASSES = 3
LANES = 128
EPS = 1e-06
F32 = jnp.float32
LOW = jnp.bfloat16
NEAR = pl.BlockSpec(memory_space=pltpu.VMEM)
VMEM = pltpu.VMEM
SMEM = pltpu.SMEM
FAR = pl.BlockSpec(memory_space=pl.ANY)
VMEM_BYTES = 60 * 1024 * 1024
SMALL_BYTES = 16 * 1024 * 1024


def times(left, right):
    return lax.dot_general(left, right, (((1,), (0,)), ((), ())), preferred_element_type=F32)


def times_transposed(left, right):
    return lax.dot_general(left, right, (((1,), (1,)), ((), ())), preferred_element_type=F32)


def first_times(left, right):
    return lax.dot_general(left, right, (((0,), (0,)), ((), ())), preferred_element_type=F32)


def row_sum(values):
    return jnp.sum(values, axis=-1, keepdims=True)


def column_sum(values):
    return jnp.sum(values, axis=0, keepdims=True)


def call(body, outs, args, scratch=(), flops=0, nbytes=0, limit=VMEM_BYTES):
    near_in = [number for number, (_, spec) in enumerate(args) if spec in (VMEM, SMEM)]
    near_out = [number for number, (_, _, spec) in enumerate(outs) if spec in (VMEM, SMEM)]
    copies = [args[number][1](args[number][0].shape, args[number][0].dtype) for number in near_in]
    copies += [outs[number][2](outs[number][0], outs[number][1]) for number in near_out]

    def kernel(*refs):
        ins, refs = list(refs[: len(args)]), refs[len(args) :]
        results, refs = list(refs[: len(outs)]), refs[len(outs) :]
        own, refs = refs[: len(scratch)], refs[len(scratch) :]
        held, sems = refs[:-1], refs[-1]
        moving = []
        for place, number in enumerate(near_in):
            moving.append(pltpu.make_async_copy(ins[number], held[place], sems.at[place]))
            ins[number] = held[place]
        for copy in moving:
            copy.start()

        def ready():
            while moving:
                moving.pop(0).wait()

        far = {}
        for place, number in enumerate(near_out, len(near_in)):
            far[place] = results[number]
            results[number] = held[place]
        mover = body(ready, *ins, *results, *own)
        ready()
        leaving = [
            pltpu.make_async_copy(held[place], target, sems.at[place]) for place, target in far.items()
        ]
        for copy in leaving:
            copy.start()
        if mover is not None:
            mover.finish()
        for copy in leaving:
            copy.wait()

    return pl.pallas_call(
        kernel,
        out_shape=tuple(jax.ShapeDtypeStruct(shape, kind) for shape, kind, _ in outs),
        in_specs=[NEAR if spec is NEAR else FAR for _, spec in args],
        out_specs=tuple([NEAR if spec is NEAR else FAR for _, _, spec in outs]),
        scratch_shapes=list(scratch)
        + copies
        + [pltpu.SemaphoreType.DMA((max(1, len(near_in) + len(near_out)),))],
        compiler_params=pltpu.CompilerParams(vmem_limit_bytes=limit),
        cost_estimate=pl.CostEstimate(flops=flops, bytes_accessed=nbytes, transcendentals=0),
    )(*[array for array, _ in args])


class Mover:
    def __init__(self, sems):
        self.sems = sems
        self.used = 0
        self.open = []

    def start(self, source, target):
        copy = pltpu.make_async_copy(source, target, self.sems.at[self.used])
        self.used += 1
        copy.start()
        return copy

    def out(self, source, target):
        self.open.append(self.start(source, target))

    def finish(self):
        for copy in self.open:
            copy.wait()


class Feed:
    def __init__(self, mover, pairs, depth):
        self.mover = mover
        self.pairs = pairs
        self.running = []
        self.done = 0
        for _ in range(depth):
            self.more()

    def more(self):
        if len(self.running) < len(self.pairs):
            self.running.append(self.mover.start(*self.pairs[len(self.running)]))

    def ahead(self):
        while len(self.running) < len(self.pairs):
            self.more()

    def need(self, count):
        while self.done < count:
            self.running[self.done].wait()
            self.done += 1
            self.more()


X, Y, NEAR_Z, FAR_Z = 1, 2, 4, 8
STEPS = 4
OUTER_WAYS = ((X, Y, NEAR_Z, FAR_Z), (NEAR_Z, Y, X, FAR_Z))
INNER_WAYS = OUTER_WAYS
QKV_WAYS = ((X, Y, NEAR_Z, FAR_Z), (NEAR_Z, X, Y, FAR_Z))


class Place:
    def __init__(self, dp, rows):
        self.dp = dp
        self.fast = dp == 1 << STEPS and rows % (16 * dp) == 0
        self.count = 4 if self.fast else 1

    def flip(self, position, ways, core):
        flips = []
        for way in ways:
            flips.append(sum(way[step] for step in range(STEPS) if not position >> (STEPS - 1 - step) & 1))
        return jnp.where(core == 0, flips[0], flips[1])

    def out(self, mover, source, columns, fars, core, size, ways, start=0):
        width = columns.size if isinstance(columns, pl.Slice) else columns.stop - columns.start
        target = slice(start, start + width)
        if not self.fast:
            there = slice(0, source.shape[0])
            if mover is None:
                fars[0][there, target] = source[:, columns]
            else:
                mover.out(source.at[:, columns], fars[0].at[there, target])
            return
        each = self.dp // len(fars)
        for position in range(self.dp):
            block = lax.axis_index("dp") ^ self.flip(position, ways, core)
            here = pl.ds(pl.multiple_of(block * size, 16), size)
            inside = position % each
            there = slice(inside * size, (inside + 1) * size)
            far = fars[position // each]
            if mover is None:
                far[there, target] = source[here, columns]
            else:
                mover.out(source.at[here, columns], far.at[there, target])

    def out_part(self, mover, source, columns, far, core, first, size, ways):
        if not self.fast:
            rows = slice(first * size, first * size + source.shape[0])
            mover.out(source.at[:, columns], far.at[rows, :])
            return
        for step in range(source.shape[0] // size):
            diff = lax.axis_index("dp") ^ (first + step)
            place = 0
            for number in range(STEPS):
                mask = jnp.where(core == 0, ways[0][number], ways[1][number])
                place = place * 2 + ((diff & mask) == 0).astype(jnp.int32)
            offset = pl.multiple_of(place * size, 16)
            mover.out(
                source.at[step * size : (step + 1) * size, columns], far.at[pl.ds(offset, size), :]
            )


def half_of(which, half):
    return pl.ds(pl.multiple_of(which * half, LANES), half)


def head_masks(rows):
    lane = lax.broadcasted_iota(jnp.int32, (rows, LANES), 1)
    left = (lane < LANES // 2).astype(F32).astype(LOW)
    right = (lane >= LANES // 2).astype(F32).astype(LOW)
    return left, right


def gelu_both(inner):
    density = jnp.exp(inner * inner * (-0.5)) * 0.3989422804014327
    below = 0.5 + 0.5 * lax.erf(inner * 0.7071067811865476)
    return inner * below, below + inner * density


def forward(
    place, length, ramp_count, ready,
    x_far, qkv_far, query_bias_ref, value_bias_ref, output_far, output_bias_ref,
    first_scale_ref, first_shift_ref, inner_far, inner_bias_ref, outer_far,
    outer_bias_ref, second_scale_ref, second_shift_ref, cot_far, pool_own_far, pool_other_far,
    pool_bias_own_ref, pool_bias_other_ref, class_own_ref, class_other_ref,
    class_bias_own_ref, class_bias_other_ref, labels_ref, ramps_ref,
    mixed_far, probs_far, context_far, normal_far, spread_ref,
    final_far, logits_ref, slope_far, resid_far, full_far, vector_ref, *refs,
):
    sends, owns, refs = refs[: place.count], refs[place.count : place.count + 1], refs[place.count + 1 :]
    (
    x_ref, qkv_ref, output_ref, mixed_ref, probs_ref, context_ref, normal_ref,
    inner_ref, outer_ref, cot_ref, pool_own_ref, pool_other_ref,
    final_ref, acted_ref, slope_ref, resid_ref, full_ref,
    low_ref, sum_ref, second_spread_ref, pair_own_ref, pair_send_ref, sems,
    ) = refs
    rows, features = x_ref.shape
    hidden_units = inner_ref.shape[1]
    seqs = rows // length
    pairs = features // LANES
    factor = (features // HEADS) ** (-0.5)
    core = lax.axis_index("ramp")
    mover = Mover(sems)
    parts = [slice(part * features, (part + 1) * features) for part in range(3)]
    steps = [
        slice(one * features, (one + 1) * features) for one in range(hidden_units // features)
    ]
    wanted = [(x_far, x_ref)]
    wanted += [(qkv_far.at[:, one], qkv_ref.at[:, one]) for one in parts]
    wanted += [(output_far, output_ref)]
    for one in steps:
        wanted += [(inner_far.at[:, one], inner_ref.at[:, one])]
        wanted += [(outer_far.at[one], outer_ref.at[one])]
    wanted += [(pool_own_far, pool_own_ref), (pool_other_far, pool_other_ref), (cot_far, cot_ref)]
    feed = Feed(mover, wanted, 3)
    ready()
    for part, columns in enumerate(parts):
        feed.need(2 + part)
        mixed = times(x_ref[...], qkv_ref[:, columns])
        if part == 0:
            mixed = mixed + query_bias_ref[...][None, :]
        if part == 2:
            mixed = mixed + value_bias_ref[...][None, :]
        mixed_ref[:, columns] = mixed.astype(LOW)
    feed.ahead()
    left, right = head_masks(length)
    left_t, right_t = left.T, right.T

    def one_sequence(seq, carry):
        here = pl.ds(pl.multiple_of(seq * length, length), length)
        for pair in range(pairs):
            start = pair * LANES
            query = mixed_ref[here, start : start + LANES]
            key = mixed_ref[here, features + start : features + start + LANES]
            value = mixed_ref[here, 2 * features + start : 2 * features + start + LANES]
            stacked = jnp.concatenate([query * left, query * right], axis=0)
            scores = times_transposed(key, stacked)
            top = jnp.max(scores, axis=0, keepdims=True)
            raised = jnp.exp((scores - top) * factor)
            probs = (raised * (1.0 / column_sum(raised))).astype(LOW)
            probs_ref[pl.ds(seq * pairs + pair, 1)] = probs[None]
            value_t = value.T
            both = jnp.concatenate([value_t * left_t, value_t * right_t], axis=1)
            tall = jnp.concatenate([probs[:, :length], probs[:, length:]], axis=0)
            context_t = times(both, tall).astype(LOW)
            context_ref[here, start : start + LANES] = context_t.T
        return carry

    lax.fori_loop(0, seqs, one_sequence, 0, unroll=2)
    feed.need(5)
    mover.out(mixed_ref, mixed_far)
    mover.out(probs_ref, probs_far)
    mover.out(context_ref, context_far)
    normal_ref[...] = times(context_ref[...], output_ref[...]) + output_bias_ref[...][None, :]
    hidden_square = jnp.zeros((1, features), F32)
    attended_square = jnp.zeros((1, features), F32)
    first_scale = first_scale_ref[...][None, :]
    first_shift = first_shift_ref[...][None, :]
    outer_bias = outer_bias_ref[...][None, :]
    for seq in range(seqs):
        here = slice(seq * length, (seq + 1) * length)
        hidden = x_ref[here, :].astype(F32)
        attended = normal_ref[here, :]
        residual = hidden + attended
        centred = residual - row_sum(residual) * (1.0 / features)
        spread = lax.rsqrt(row_sum(centred * centred) * (1.0 / features) + EPS)
        normal = centred * spread
        normal_ref[here, :] = normal
        spread_ref[here, :] = spread
        first = normal * first_scale + first_shift
        low_ref[here, :] = first.astype(LOW)
        sum_ref[here, :] = first + outer_bias
        hidden_square = hidden_square + column_sum(hidden * hidden)
        attended_square = attended_square + column_sum(attended * attended)
    mover.out(normal_ref, normal_far)

    feed.need(5 + 2 * len(steps))

    def inner_of(columns):
        return times(low_ref[...], inner_ref[:, columns]) + inner_bias_ref[columns][None, :]

    inner = inner_of(steps[0])
    for step, columns in enumerate(steps):
        following = inner_of(steps[step + 1]) if step + 1 < len(steps) else None
        acted, slope = gelu_both(inner)
        acted = acted.astype(LOW)
        acted_ref[:, columns] = acted
        slope_ref[:, columns] = slope.astype(LOW)
        sum_ref[...] += times(acted, outer_ref[columns, :])
        inner = following
    mover.out(slope_ref, slope_far)

    scale = second_scale_ref[...][None, :]
    shift = second_shift_ref[...][None, :]
    square = jnp.zeros((1, features), F32)
    leading = []
    for seq in range(seqs):
        here = slice(seq * length, (seq + 1) * length)
        residual = sum_ref[here, :]
        outer = residual - (normal_ref[here, :] * first_scale + first_shift)
        square = square + column_sum(outer * outer)
        centred = residual - row_sum(residual) * (1.0 / features)
        spread = lax.rsqrt(row_sum(centred * centred) * (1.0 / features) + EPS)
        normal = centred * spread
        sum_ref[here, :] = normal
        second_spread_ref[here, :] = spread
        final = (normal * scale + shift).astype(LOW)
        final_ref[here, :] = final
        leading.append(final[0:1, :].astype(F32))
    mover.out(final_ref, final_far)

    feed.need(len(wanted) - 1)
    leading = jnp.concatenate(leading + [jnp.zeros((8 - seqs, features), F32)], axis=0)
    states = leading.astype(LOW)
    row = lax.broadcasted_iota(jnp.int32, (8, 1), 0)
    ramp_of = jnp.full((8, 1), -1, jnp.int32)
    label_of = jnp.full((8, 1), -1, jnp.int32)
    for seq in range(seqs):
        ramp_of = jnp.where(row == seq, ramps_ref[seq], ramp_of)
        label_of = jnp.where(row == seq, labels_ref[seq], label_of)
    own = ramp_of == core
    pre_own = times(states, pool_own_ref[0]) + pool_bias_own_ref[...]
    pre_other = times(states, pool_other_ref[0]) + pool_bias_other_ref[...]
    pooled = jnp.tanh(jnp.where(own, pre_own, pre_other))
    pooled_low = pooled.astype(LOW)
    logits = jnp.where(
        own,
        times_transposed(pooled_low, class_own_ref[0]) + class_bias_own_ref[...],
        times_transposed(pooled_low, class_other_ref[0]) + class_bias_other_ref[...],
    )
    logits_ref[...] = logits[:seqs, :]
    raised = jnp.exp(logits - jnp.max(logits, axis=-1, keepdims=True))
    kind = lax.broadcasted_iota(jnp.int32, (8, CLASSES), 1)
    grads = raised / row_sum(raised) - (kind == label_of).astype(F32)
    grads = jnp.where(ramp_of >= 0, grads, 0.0)
    grads_high = grads.astype(LOW)
    grads_rest = (grads - grads_high.astype(F32)).astype(LOW)

    def from_logits(weight):
        return times(grads_high, weight) + times(grads_rest, weight)

    pooled_grad = jnp.where(own, from_logits(class_own_ref[0]), from_logits(class_other_ref[0]))
    pre_low = (pooled_grad * (1.0 - pooled * pooled)).astype(LOW).astype(F32)
    pre_own_low = jnp.where(own, pre_low, 0.0).astype(LOW)
    pre_other_low = jnp.where(own, 0.0, pre_low).astype(LOW)
    state_grad = times_transposed(pre_own_low, pool_own_ref[0])
    state_grad = state_grad + times_transposed(pre_other_low, pool_other_ref[0])
    chosen_row = lax.broadcasted_iota(jnp.int32, (8, 8), 0)
    chosen_seq = lax.broadcasted_iota(jnp.int32, (8, 8), 1)
    per_ramp = seqs // ramp_count
    for ref, which, top in ((pair_own_ref, core, 0), (pair_send_ref, 1 - core, 2 * per_ramp)):
        pick_states = jnp.zeros((8, 8), jnp.bool_)
        pick_grads = jnp.zeros((8, 8), jnp.bool_)
        for seq in range(seqs):
            rank = jnp.int32(0)
            for other in range(seq):
                rank = rank + (ramps_ref[other] == which).astype(jnp.int32)
            here = (chosen_seq == seq) & (ramps_ref[seq] == which)
            pick_states = pick_states | (here & (chosen_row == top + rank))
            pick_grads = pick_grads | (here & (chosen_row == top + per_ramp + rank))
        rows_of_pair = times(pick_states.astype(F32).astype(LOW), states)
        rows_of_pair = rows_of_pair + times(pick_grads.astype(F32).astype(LOW), pre_low.astype(LOW))
        folded = jnp.concatenate([rows_of_pair[:, : features // 2], rows_of_pair[:, features // 2 :]], axis=0)
        ref[...] = folded.astype(LOW)

    vector_ref[...] = jnp.zeros(vector_ref.shape, F32)
    for ramp in range(ramp_count):
        mask = ramp_of == ramp
        base = 8 * (ramp + 1)
        vector_ref[base : base + 1, :] = column_sum(jnp.where(mask, pre_low, 0.0))
        high = jnp.where(mask, grads_high.astype(F32), 0.0).astype(LOW)
        rest = jnp.where(mask, grads_rest.astype(F32), 0.0).astype(LOW)
        vector_ref[base + 1 : base + 1 + CLASSES, :] = first_times(high, pooled_low) + first_times(
            rest, pooled_low
        )
        vector_ref[base + 4 : base + 5, 0:CLASSES] = column_sum(jnp.where(mask, grads, 0.0))

    feed.need(len(wanted))
    scale_grad = jnp.zeros((1, features), F32)
    shift_grad = jnp.zeros((1, features), F32)
    bias_grad = jnp.zeros((1, features), F32)
    at_first = lax.broadcasted_iota(jnp.int32, (length, 1), 0) == 0
    for seq in range(seqs):
        here = slice(seq * length, (seq + 1) * length)
        final_grad = cot_ref[here, :].astype(F32)
        final_grad = final_grad + jnp.where(at_first, state_grad[seq : seq + 1, :], 0.0)
        normal = sum_ref[here, :]
        scale_grad = scale_grad + column_sum(final_grad * normal)
        shift_grad = shift_grad + column_sum(final_grad)
        scaled = final_grad * scale
        resid = second_spread_ref[here, :] * (
            scaled
            - row_sum(scaled) * (1.0 / features)
            - normal * (row_sum(scaled * normal) * (1.0 / features))
        )
        resid_ref[here, :] = resid
        low = resid.astype(LOW)
        full_ref[here, :] = low
        bias_grad = bias_grad + column_sum(low.astype(F32))
    mover.out(full_ref, full_far)
    mover.out(resid_ref, resid_far)
    below = pl.ds(hidden_units, 16)
    mover.out(pair_own_ref, owns[0].at[below])
    mover.out(pair_send_ref, sends[0].at[pl.ds(hidden_units // place.count, 16)])
    size = hidden_units // place.dp
    half = features // 2
    for step, columns in enumerate(steps):
        outer_ref[columns, :] = first_times(acted_ref[:, columns], full_ref[...]).astype(LOW)
        place.out_part(
            mover, outer_ref.at[columns], half_of(core, half), owns[0], core, step * features // size, size, OUTER_WAYS
        )
    place.out(mover, outer_ref, half_of(1 - core, half), sends, 1 - core, size, OUTER_WAYS)
    vector_ref[0:1, :] = bias_grad
    vector_ref[1:2, :] = scale_grad
    vector_ref[2:3, :] = shift_grad
    vector_ref[3:4, 0:1] = row_sum(hidden_square)
    vector_ref[3:4, 1:2] = row_sum(attended_square)
    vector_ref[3:4, 2:3] = row_sum(square)
    return mover


def feed_backward(
    place, length, ready,
    full_far, slope_far, outer_far, inner_far, resid_far, normal_far,
    first_scale_ref, first_shift_ref, after_far,
    first_grad_far, vector_ref, *refs,
):
    sends, owns, refs = refs[: place.count], refs[place.count : place.count + 1], refs[place.count + 1 :]
    full_ref, slope_ref, outer_ref, inner_ref, sum_ref, normal_ref, weight_ref, first_ref, sems = refs
    rows, features = normal_ref.shape
    core = lax.axis_index("ramp")
    hidden_units = slope_ref.shape[1]
    half = hidden_units // 2
    mover = Mover(sems)
    order = []
    for fars, who in ((sends, 1 - core), (owns, core)):
        for start in range(0, half, features):
            number = who * (half // features) + start // features
            columns = pl.ds(pl.multiple_of(number * features, LANES), features)
            order.append((fars, who, start, number, columns))
    wanted = [(full_far, full_ref)]
    for _, _, _, _, columns in order:
        wanted.append((outer_far.at[columns], outer_ref.at[columns]))
        wanted.append((slope_far.at[:, columns], slope_ref.at[:, columns]))
        if len(wanted) == 3:
            wanted.append((normal_far, normal_ref))
        wanted.append((inner_far.at[:, columns], inner_ref.at[:, columns]))
        if len(wanted) == 5:
            wanted.append((resid_far, sum_ref))
    feed = Feed(mover, wanted, 7)
    ready()
    scale = first_scale_ref[...][None, :]
    vector_ref[...] = jnp.zeros(vector_ref.shape, F32)
    size = features // place.dp

    def acted_grad_of(step):
        return times_transposed(full_ref[...], outer_ref[order[step][4], :])

    feed.need(2)
    acted_grad = acted_grad_of(0)
    feed.need(4)
    first_ref[...] = (normal_ref[...] * scale + first_shift_ref[...][None, :]).astype(LOW)
    for step, (fars, who, start, number, columns) in enumerate(order):
        feed.need(min(6 + 3 * step + 1, len(wanted)))
        following = acted_grad_of(step + 1) if step + 1 < len(order) else None
        inner_grad = (slope_ref[:, columns].astype(F32) * acted_grad).astype(LOW)
        vector_ref[pl.ds(number, 1), :] = column_sum(inner_grad.astype(F32))
        sum_ref[...] += times_transposed(inner_grad, inner_ref[:, columns])
        here = slice(step * features, (step + 1) * features)
        weight_ref[:, here] = first_times(first_ref[...], inner_grad).astype(LOW)
        place.out(None, weight_ref, here, fars, who, size, INNER_WAYS, start)
        acted_grad = following
    mover.out(sum_ref, first_grad_far)
    return mover


def attention_backward(
    place, length, ready,
    first_grad_far, normal_far, spread_ref, first_scale_ref, output_far, context_far,
    mixed_far, probs_far, x_far, after_far,
    grad_far, first_resid_far, vector_ref, *refs,
):
    sends, owns, refs = refs[: place.count], refs[place.count : place.count + 1], refs[place.count + 1 :]
    (
        first_grad_ref, normal_ref, output_ref, context_ref, low_ref, first_resid_ref,
        mixed_ref, probs_ref, context_grad_ref, x_ref, grad_ref, weight_ref, sems, out_sems,
    ) = refs
    rows, features = context_grad_ref.shape
    seqs = rows // length
    core = lax.axis_index("ramp")
    pairs = features // LANES
    factor = (features // HEADS) ** (-0.5)
    half = features // 2
    size = features // place.dp
    left, right = head_masks(length)
    mover = Mover(out_sems)
    wanted = [
        (first_grad_far, first_grad_ref),
        (normal_far, normal_ref),
        (output_far, output_ref),
        (context_far, context_ref),
    ]
    feed = Feed(mover, wanted, len(wanted))

    def copies(seq):
        here = pl.ds(pl.multiple_of(seq * length, length), length)
        heads = pl.ds(seq * pairs, pairs)
        return (
            pltpu.make_async_copy(mixed_far.at[here], mixed_ref.at[here], sems.at[0, seq]),
            pltpu.make_async_copy(probs_far.at[heads], probs_ref.at[heads], sems.at[1, seq]),
        )

    for seq in range(seqs):
        for copy in copies(seq):
            copy.start()
    got_x = mover.start(x_far, x_ref)
    ready()
    feed.need(2)
    scale = first_scale_ref[...][None, :]
    zero = jnp.zeros((1, features), F32)
    sums = [zero, zero, zero]
    for seq in range(seqs):
        here = slice(seq * length, (seq + 1) * length)
        first_grad = first_grad_ref[here, :]
        normal = normal_ref[here, :]
        scaled = first_grad * scale
        resid = spread_ref[here, :] * (
            scaled
            - row_sum(scaled) * (1.0 / features)
            - normal * (row_sum(scaled * normal) * (1.0 / features))
        )
        first_resid_ref[here, :] = resid
        low = resid.astype(LOW)
        low_ref[here, :] = low
        sums[0] = sums[0] + column_sum(low.astype(F32))
        sums[1] = sums[1] + column_sum(first_grad * normal)
        sums[2] = sums[2] + column_sum(first_grad)
    mover.out(first_resid_ref, first_resid_far)
    feed.need(len(wanted))
    context_grad_ref[...] = times_transposed(low_ref[...], output_ref[...]).astype(LOW)
    columns = slice(3 * features, 4 * features)
    weight_ref[:, columns] = first_times(context_ref[...], low_ref[...]).astype(LOW)
    for fars, who in ((sends, 1 - core), (owns, core)):
        columns = pl.ds(pl.multiple_of(3 * features + who * half, LANES), half)
        place.out(None, weight_ref, columns, fars, who, size, QKV_WAYS, 3 * half)

    def one_sequence(seq, carry):
        here = pl.ds(pl.multiple_of(seq * length, length), length)
        for copy in copies(seq):
            copy.wait()
        for pair in range(pairs):
            start = pair * LANES
            query = mixed_ref[here, start : start + LANES]
            key = mixed_ref[here, features + start : features + start + LANES]
            value = mixed_ref[here, 2 * features + start : 2 * features + start + LANES]
            context_grad = context_grad_ref[here, start : start + LANES]
            queries = jnp.concatenate([query * left, query * right], axis=0)
            keys = jnp.concatenate([key * left, key * right], axis=0)
            grads = jnp.concatenate([context_grad * left, context_grad * right], axis=0)
            probs = probs_ref[pl.ds(seq * pairs + pair, 1)][0]
            probs_grad = times_transposed(value, grads)
            wide = probs.astype(F32)
            score_grad = wide * (probs_grad - column_sum(wide * probs_grad))
            score_grad = score_grad.astype(LOW)
            value_grad = times(probs, grads).astype(LOW)
            key_grad = (times(score_grad, queries) * factor).astype(LOW)
            turned = jnp.concatenate(
                [score_grad[:, :length].T, score_grad[:, length:].T], axis=1
            )
            query_grad = (times(turned, keys) * factor).astype(LOW)
            grad_ref[here, start : start + LANES] = query_grad
            grad_ref[here, features + start : features + start + LANES] = key_grad
            grad_ref[here, 2 * features + start : 2 * features + start + LANES] = value_grad
        return carry

    lax.fori_loop(0, seqs, one_sequence, 0, unroll=2)
    mover.out(grad_ref, grad_far)
    got_x.wait()
    for fars, who in ((sends, 1 - core), (owns, core)):
        for start, width in ((0, features), (features, half)):
            columns = pl.ds(pl.multiple_of(who * 3 * half + start, LANES), width)
            weight_ref[:, columns] = first_times(x_ref[...], grad_ref[:, columns]).astype(LOW)
            place.out(None, weight_ref, columns, fars, who, size, QKV_WAYS, start)
    vector_ref[...] = jnp.zeros(vector_ref.shape, F32)
    vector_ref[0:1, :] = column_sum(grad_ref[:, :features].astype(F32))
    vector_ref[1:2, :] = column_sum(grad_ref[:, 2 * features :].astype(F32))
    for number, one in enumerate(sums):
        vector_ref[2 + number : 3 + number, :] = one
    return mover


def input_gradient(
    ready,
    grad_far, qkv_far, resid_far, after_far,
    result_far, token_far,
    grad_ref, qkv_ref, resid_ref, result_ref, sems,
):
    mover = Mover(sems)
    features = resid_ref.shape[1]
    parts = [slice(part * features, (part + 1) * features) for part in range(3)]
    got = []
    for one in parts:
        got.append(
            (
                mover.start(grad_far.at[:, one], grad_ref.at[:, one]),
                mover.start(qkv_far.at[:, one], qkv_ref.at[:, one]),
            )
        )
    got_resid = mover.start(resid_far, resid_ref)
    total = None
    for columns, copies in zip(parts, got):
        for copy in copies:
            copy.wait()
        product = times_transposed(grad_ref[:, columns], qkv_ref[:, columns])
        total = product if total is None else total + product
    got_resid.wait()
    result_ref[...] = (resid_ref[...] + total).astype(LOW)
    mover.out(result_ref, result_far)
    return mover


def swap_core(values):
    return lax.ppermute(values, "ramp", [(0, 1), (1, 0)])


def shift(values, even, odd):
    dp = lax.axis_size("dp")
    pairs = []
    for one in range(dp):
        pairs.append((2 * one, 2 * (one ^ even)))
        pairs.append((2 * one + 1, 2 * (one ^ odd) + 1))
    return lax.ppermute(values, ("dp", "ramp"), pairs)


RIDERS = 16


def pack(ref, total, top, beside):
    high = total.astype(LOW)
    rest = (total - high.astype(F32)).astype(LOW)
    count = total.shape[0] // RIDERS
    if beside is not None:
        spots = rider_spots(ref.shape[0], total.shape[0])
        ref[:, beside:] = jnp.zeros((ref.shape[0], ref.shape[1] - beside), LOW)
        for values, number, row, start in spots:
            part = (high, rest)[values][number * RIDERS : (number + 1) * RIDERS, :]
            ref[row : row + RIDERS, beside + start : beside + start + LANES] = part
        return
    ref[top : top + RIDERS, :] = jnp.zeros((RIDERS, ref.shape[1]), LOW)
    for number in range(count):
        rows = slice(number * RIDERS, (number + 1) * RIDERS)
        for part, values in enumerate((high, rest)):
            start = (part * count + number) * LANES
            ref[top : top + RIDERS, start : start + LANES] = values[rows, :]


def rider_spots(height, rows):
    spots = []
    for number in range(rows // RIDERS):
        below, beside = number % (height // RIDERS), number // (height // RIDERS)
        spots.append((0, number, below * RIDERS, beside * LANES))
    return spots


def rider_width(height, rows):
    return rider_spots(height, rows)[-1][3] + LANES


def unpack(ref, count, top, beside):
    parts = [None] * count
    if beside is not None:
        for _, number, row, start in rider_spots(ref.shape[0], count * RIDERS):
            term = ref[row : row + RIDERS, beside + start : beside + start + LANES].astype(F32)
            parts[number] = term if parts[number] is None else parts[number] + term
    else:
        for number in range(count):
            start, rest = number * LANES, (count + number) * LANES
            high = ref[top : top + RIDERS, start : start + LANES].astype(F32)
            parts[number] = high + ref[top : top + RIDERS, rest : rest + LANES].astype(F32)
    return parts[0] if count == 1 else jnp.concatenate(parts, axis=0)


def combine(plan, count, rider, carried, ready, *refs):
    arrays, results = refs[:count], refs[count:]
    if rider is not None:
        plain, packed, into, beside = rider
        out_ref = results[len(plan)]
        total = None
        for number in plain:
            total = arrays[number][...] if total is None else total + arrays[number][...]
        for number, top, side in packed:
            total = total + unpack(arrays[number], total.shape[0] // RIDERS, top, side)
        out_ref[...] = total
    for number, (parts, result) in enumerate(zip(plan, results)):
        top = 0
        for rows, width, terms in parts:
            total_rows = None
            wide = len(terms) > 2 or result.dtype == F32
            for array, row, column in terms:
                term = arrays[array][row : row + rows, column : column + width]
                term = term.astype(F32) if wide else term
                total_rows = term if total_rows is None else total_rows + term
            result[top : top + rows, :width] = total_rows.astype(result.dtype)
            top += rows
        if rider is not None and number in into:
            pack(result, total, top, parts[0][1] if beside else None)
        if number in carried:
            sums, side = carried[number]
            pack(result, arrays[sums][...], top, parts[0][1] if side else None)


def combined(results, after=(), rider=None, riders=()):
    arrays = []

    def number(array):
        for place, one in enumerate(arrays):
            if one is array:
                return place
        arrays.append(array)
        return len(arrays) - 1

    plan = [
        [(rows, width, [(number(array), row, column) for array, row, column in terms]) for rows, terms in parts]
        for width, _, parts in results
    ]
    ride, extra, into, beside = None, [], (), False
    if rider is not None:
        plain, packed, into, *rest = rider
        beside = bool(rest)
        ride = ([number(one) for one in plain], [(number(one), *where) for one, *where in packed], into, beside)
        extra = [(plain[0].shape, F32, NEAR)]
    shapes = []
    carried = {}
    for place, sums, *rest in riders:
        carried[place] = (number(sums), bool(rest))
    for place, (width, kind, parts) in enumerate(results):
        height = sum(part[0] for part in parts)
        if place in carried and carried[place][1]:
            width = width + rider_width(height, arrays[carried[place][0]].shape[0])
        elif place in carried:
            height = height + RIDERS
        if place in into and beside:
            width = width + rider_width(height, plain[0].shape[0])
        elif place in into:
            height = height + RIDERS
        shapes.append(((height, width), kind))
    return call(
        partial(combine, plan, len(arrays) + len(after), ride, carried),
        [(shape, kind, NEAR) for shape, kind in shapes] + extra + [((8, LANES), F32, FAR)],
        [(array, NEAR) for array in arrays] + [(array, FAR) for array in after],
        nbytes=sum(8 * shape[0] * shape[1] for shape, _ in shapes),
        limit=SMALL_BYTES,
    )


class Chain:
    def __init__(self, sends, own, ways, spare=0):
        self.own = own
        self.ways = ways
        self.step = 0
        self.count = own.shape[0] - spare
        self.got = [swap_core(one) for one in sends]
        self.heights = [self.count // len(sends)] * len(sends)
        self.width = own.shape[1]

    def come(self, start, count):
        spans = []
        top = 0
        for one, height in zip(self.got, self.heights):
            low, high = max(start, top), min(start + count, top + height)
            if low < high:
                spans.append((high - low, (one, low - top, 0)))
            top += height
        return spans

    def parts(self, start, count):
        result = []
        for rows, place in self.come(start, count):
            result.append((rows, [(self.own, start, 0), place]))
            start += rows
        return result

    def add(self):
        rows = self.count // 2
        return [(self.width, LOW, self.parts(start, rows)) for start in (0, rows)]

    def send(self, array, keep):
        self.got, self.own = [shift(array, self.ways[0][self.step], self.ways[1][self.step])], keep
        self.step += 1
        self.count = keep.shape[0]
        self.heights = [self.count]

    def rider(self, beside=False):
        return (self.got[0], 0, self.width) if beside else (self.got[0], self.count, None)

    def gather(self, results, number, *terms):
        width, kind, parts = results[number]
        results[number] = (width, kind, parts + list(terms))
        return results

    def add_last(self, widths):
        results = []
        start = 0
        for width in widths:
            terms = [(array, 0, start) for array in (self.own, self.got[0])]
            results.append((width, F32, [(self.count, terms)]))
            start += width
        return results

    def plain(self, widths):
        total = (self.own[: self.count].astype(F32) + self.got[0][: self.count].astype(F32)).astype(LOW)
        rows = lax.psum_scatter(total, "dp", scatter_dimension=0, tiled=True).astype(F32)
        ends = [sum(widths[: one + 1]) for one in range(len(widths))]
        return [rows[:, end - width : end] for width, end in zip(widths, ends)]


EARLY_ROWS, LATE_ROWS = 96, 32


def put_rows(out_ref, place, row):
    for start in range(0, row.shape[1], LANES):
        out_ref[place : place + 1, :] = row[:, start : start + LANES]
        place += 1
    return place


def collect_late(ready, mixed_ref, after_far, out_ref):
    ready()
    out_ref[...] = jnp.zeros(out_ref.shape, F32)
    place = 0
    for number in range(5):
        place = put_rows(out_ref, place, mixed_ref[number : number + 1, :])


def collect_early(ready, first_ref, second_ref, after_far, out_ref):
    ready()
    out_ref[...] = jnp.zeros(out_ref.shape, F32)
    place = 0
    for number in range(first_ref.shape[0] // 2):
        place = put_rows(out_ref, place, first_ref[number : number + 1, :])
    for number in range(3):
        place = put_rows(out_ref, place, second_ref[number : number + 1, :])
    for base in (8, 16):
        for number in range(1 + CLASSES):
            place = put_rows(out_ref, place, second_ref[base + number : base + number + 1, :])
    for number in (3, 12, 20):
        place = put_rows(out_ref, place, second_ref[number : number + 1, :LANES])


def add_all(ready, *refs):
    ready()
    *refs, after_far, out_ref = refs
    total = refs[0][...]
    for ref in refs[1:]:
        total = total + ref[...]
    out_ref[...] = total


def add_over(values, masks, after=None):
    got = [shift(values, mask, mask) for mask in masks]
    (total,) = call(
        add_all,
        [(values.shape, values.dtype, VMEM)],
        [(one, VMEM) for one in [values] + got] + [((after or [values])[0], FAR)],
        limit=SMALL_BYTES,
    )
    return total


def take_rows(all_ref, place, ref, start, width):
    for column in range(0, width, LANES):
        ref[pl.ds(start + column, LANES)] = all_ref[place, :]
        place += 1
    return place


def hand_out(features, entries, ready, all_ref, other_ref, late_ref, *outs):
    ready()
    all_ref[...] += other_ref[...]
    place = 0
    for ref in outs[8:]:
        place = take_rows(late_ref, place, ref, 0, features)
    outs = outs[:8]
    core = lax.axis_index("ramp")
    rms_ref, inner_ref, outer_ref, second_scale_ref, second_shift_ref = outs[:5]
    pool_ref, class_ref, class_bias_ref = outs[5:]
    place = 0
    for ref in (inner_ref, outer_ref, second_scale_ref, second_shift_ref):
        place = take_rows(all_ref, place, ref, 0, ref.shape[0])
    step = features // LANES
    size = step * (1 + CLASSES)
    for column in range(step):
        at = column * LANES
        first = all_ref[place + column : place + column + 1, :]
        second = all_ref[place + size + column : place + size + column + 1, :]
        pool_ref[:, at : at + LANES] = jnp.where(core == 0, first, second)
        for kind in range(CLASSES):
            row = place + (1 + kind) * step + column
            first = all_ref[row : row + 1, :]
            second = all_ref[row + size : row + size + 1, :]
            class_ref[kind, :, at : at + LANES] = jnp.where(core == 0, first, second)
    place += 2 * size
    rms_ref[...] = jnp.sqrt(all_ref[place, :] * (1.0 / entries))[: rms_ref.shape[0]]
    first = all_ref[place + 1 : place + 2, :CLASSES]
    second = all_ref[place + 2 : place + 3, :CLASSES]
    class_bias_ref[...] = jnp.where(core == 0, first, second)


def pool_gradient(ready, pair_ref, after_far, out_ref, token_far, all_ref):
    ready()
    height, half = pair_ref.shape
    blocks = pair_ref[...].astype(F32).reshape(height // 16, 16, half)
    rows = jnp.concatenate([blocks[:, 0:8, :], blocks[:, 8:16, :]], axis=2)
    rows = rows.reshape(height // 2, 2 * half).astype(LOW)
    at = lax.broadcasted_iota(jnp.int32, (height // 2, height // 2), 0)
    beyond = lax.broadcasted_iota(jnp.int32, (height // 2, height // 2), 1)
    moved = ((beyond == at + 2) & (at % 4 < 2)).astype(F32).astype(LOW)
    all_ref[...] = first_times(rows, times(moved, rows).astype(LOW))
    count = out_ref.shape[0]
    out_ref[...] = all_ref[pl.ds(pl.multiple_of(lax.axis_index("dp") * count, 8), count), :]


def on_device(
    hidden_in, cotangent, qkv_weight, query_bias, value_bias, output_weight, output_bias,
    first_scale, first_shift, inner_weight, inner_bias, outer_weight, outer_bias,
    second_scale, second_shift, pool_weight, pool_bias, class_weight, class_bias,
    labels, ramp_index,
):
    rows, features = hidden_in.shape
    seqs = labels.shape[0]
    length = rows // seqs
    units = inner_weight.shape[1]
    dp = lax.axis_size("dp")
    ramps = lax.axis_size("ramp")
    pairs = features // LANES
    place = Place(dp, features)
    half = features // 2

    pool_other = swap_core(pool_weight)
    pool_bias_other = swap_core(pool_bias)
    class_weight = jnp.swapaxes(class_weight, 1, 2)
    class_other = swap_core(class_weight)
    class_bias_other = swap_core(class_bias)
    (
        mixed, probs, context, normal, spread, output, logits, slope, second_resid, outer_full,
        second_vector, *outer_parts,
    ) = call(
        partial(forward, place, length, ramps),
        [
            ((rows, 3 * features), LOW, FAR),
            ((seqs * pairs, length, 2 * length), LOW, FAR),
            ((rows, features), LOW, FAR),
            ((rows, features), F32, FAR),
            ((rows, 1), F32, VMEM),
            ((rows, features), LOW, FAR),
            ((seqs, CLASSES), F32, VMEM),
            ((rows, units), LOW, FAR),
            ((rows, features), F32, FAR),
            ((rows, features), LOW, FAR),
            ((8 * (ramps + 1), features), F32, VMEM),
        ]
        + [((units // place.count + 16, half), LOW, FAR)]
        + [((units // place.count, half), LOW, FAR)] * (place.count - 1)
        + [((units + 16, half), LOW, FAR)],
        [
            (hidden_in, FAR),
            (qkv_weight, FAR),
            (query_bias, VMEM),
            (value_bias, VMEM),
            (output_weight, FAR),
            (output_bias, VMEM),
            (first_scale, VMEM),
            (first_shift, VMEM),
            (inner_weight, FAR),
            (inner_bias, VMEM),
            (outer_weight, FAR),
            (outer_bias, VMEM),
            (second_scale, VMEM),
            (second_shift, VMEM),
            (cotangent, FAR),
            (pool_weight, FAR),
            (pool_other, FAR),
            (pool_bias, VMEM),
            (pool_bias_other, VMEM),
            (class_weight, VMEM),
            (class_other, VMEM),
            (class_bias, VMEM),
            (class_bias_other, VMEM),
            (labels, SMEM),
            (ramp_index, SMEM),
        ],
        scratch=[
            pltpu.VMEM((rows, features), LOW),
            pltpu.VMEM((features, 3 * features), LOW),
            pltpu.VMEM((features, features), LOW),
            pltpu.VMEM((rows, 3 * features), LOW),
            pltpu.VMEM((seqs * pairs, length, 2 * length), LOW),
            pltpu.VMEM((rows, features), LOW),
            pltpu.VMEM((rows, features), F32),
            pltpu.VMEM((features, units), LOW),
            pltpu.VMEM((units, features), LOW),
            pltpu.VMEM((rows, features), LOW),
            pltpu.VMEM((1, features, features), LOW),
            pltpu.VMEM((1, features, features), LOW),
            pltpu.VMEM((rows, features), LOW),
            pltpu.VMEM((rows, units), LOW),
            pltpu.VMEM((rows, units), LOW),
            pltpu.VMEM((rows, features), F32),
            pltpu.VMEM((rows, features), LOW),
            pltpu.VMEM((rows, features), LOW),
            pltpu.VMEM((rows, features), F32),
            pltpu.VMEM((rows, 1), F32),
            pltpu.VMEM((16, half), LOW),
            pltpu.VMEM((16, half), LOW),
            pltpu.SemaphoreType.DMA((18 + 3 * (units // features) + 2 * dp,)),
        ],
        flops=2 * rows * features * (4 * features + 3 * units) + 8 * rows * features * length,
        nbytes=40 << 20,
        limit=VMEM_BYTES,
    )
    outer_chain = Chain(outer_parts[: place.count], outer_parts[place.count], OUTER_WAYS, 16)
    token = second_vector
    if place.fast:
        shared = [(outer_chain.own, units, 0), (outer_chain.got[0], units // place.count, 0)]
        results = outer_chain.gather(outer_chain.add(), 0, (16, shared))
        send, pair, token = combined(results[:1] + [(half, LOW, [(16, shared)])])
        keep, token = combined(results[1:], after=[token])
        outer_chain.send(send, keep)

    first_grad, first_vector, *inner_parts = call(
        partial(feed_backward, place, length),
        [((rows, features), F32, FAR), ((8, features), F32, VMEM)]
        + [((features // place.count, units // 2), LOW, NEAR)] * place.count
        + [((features, units // 2), LOW, NEAR)],
        [
            (outer_full, FAR),
            (slope, FAR),
            (outer_weight, FAR),
            (inner_weight, FAR),
            (second_resid, FAR),
            (normal, FAR),
            (first_scale, VMEM),
            (first_shift, VMEM),
            (token, FAR),
        ],
        scratch=[
            pltpu.VMEM((rows, features), LOW),
            pltpu.VMEM((rows, units), LOW),
            pltpu.VMEM((units, features), LOW),
            pltpu.VMEM((features, units), LOW),
            pltpu.VMEM((rows, features), F32),
            pltpu.VMEM((rows, features), F32),
            pltpu.VMEM((features, units), LOW),
            pltpu.VMEM((rows, features), LOW),
            pltpu.SemaphoreType.DMA((8 + 3 * (units // features),)),
        ],
        flops=6 * rows * features * units,
        nbytes=25 << 20,
        limit=44 << 20,
    )
    inner_chain = Chain(inner_parts[: place.count], inner_parts[place.count], INNER_WAYS)
    token = first_vector

    def with_pair():
        height = pair.shape[0]
        shared = [(height, [(pair, 0, 0)]), (height, [(outer_chain.got[0], outer_chain.count, 0)])]
        return outer_chain.gather(outer_chain.add(), 0, *shared) + [(half, LOW, shared)]

    if place.fast:
        send, keep, pair, token = combined(with_pair(), after=[first_vector])
        outer_chain.send(send, keep)
    (early,) = call(
        collect_early,
        [((EARLY_ROWS, LANES), F32, VMEM)],
        [(first_vector, VMEM), (second_vector, VMEM), (token, FAR)],
        limit=SMALL_BYTES,
    )
    if place.fast:
        results = inner_chain.add()
        send, early, token = combined(results[:1], after=[token], rider=([early], [], (0,)))
        keep, token = combined(results[1:], after=[token])
        inner_chain.send(send, keep)

    mixed_grad, first_resid, mixed_vector, *qkv_parts = call(
        partial(attention_backward, place, length),
        [((rows, 3 * features), LOW, FAR), ((rows, features), F32, FAR), ((8, features), F32, VMEM)]
        + [((features // place.count, 4 * half), LOW, NEAR)] * place.count
        + [((features, 4 * half), LOW, NEAR)],
        [
            (first_grad, FAR),
            (normal, FAR),
            (spread, VMEM),
            (first_scale, VMEM),
            (output_weight, FAR),
            (context, FAR),
            (mixed, FAR),
            (probs, FAR),
            (hidden_in, FAR),
            (token, FAR),
        ],
        scratch=[
            pltpu.VMEM((rows, features), F32),
            pltpu.VMEM((rows, features), F32),
            pltpu.VMEM((features, features), LOW),
            pltpu.VMEM((rows, features), LOW),
            pltpu.VMEM((rows, features), LOW),
            pltpu.VMEM((rows, features), F32),
            pltpu.VMEM((rows, 3 * features), LOW),
            pltpu.VMEM((seqs * pairs, length, 2 * length), LOW),
            pltpu.VMEM((rows, features), LOW),
            pltpu.VMEM((rows, features), LOW),
            pltpu.VMEM((rows, 3 * features), LOW),
            pltpu.VMEM((features, 4 * features), LOW),
            pltpu.SemaphoreType.DMA((2, seqs)),
            pltpu.SemaphoreType.DMA((8,)),
        ],
        flops=20 * rows * features * length + 10 * rows * features * features,
        nbytes=12 << 20,
        limit=36 << 20,
    )
    qkv_chain = Chain(qkv_parts[: place.count], qkv_parts[place.count], QKV_WAYS)
    token = mixed_vector
    if place.fast:
        *sends, pair, early, token = combined(
            inner_chain.add() + with_pair(),
            after=[mixed_vector],
            rider=([early], [inner_chain.rider()], (0,)),
        )
        inner_chain.send(*sends[:2])
        outer_chain.send(*sends[2:])
    (late,) = call(
        collect_late,
        [((LATE_ROWS, LANES), F32, VMEM)],
        [(mixed_vector, VMEM), (mixed_vector, FAR)],
        limit=SMALL_BYTES,
    )
    late_other = swap_core(late)

    if place.fast:
        send, keep, late, token = combined(
            qkv_chain.add(), after=[token], rider=([late, late_other], [], (0,))
        )
        qkv_chain.send(send, keep)
    input_grad, token = call(
        input_gradient,
        [((rows, features), LOW, FAR), ((8, LANES), F32, FAR)],
        [(mixed_grad, FAR), (qkv_weight, FAR), (first_resid, FAR), (token, FAR)],
        scratch=[
            pltpu.VMEM((rows, 3 * features), LOW),
            pltpu.VMEM((features, 3 * features), LOW),
            pltpu.VMEM((rows, features), F32),
            pltpu.VMEM((rows, features), LOW),
            pltpu.SemaphoreType.DMA((8,)),
        ],
        flops=6 * rows * features * features,
        nbytes=10 << 20,
        limit=20 << 20,
    )

    if place.fast:
        early, token = combined([], after=[token], rider=([early], [inner_chain.rider()], ()))
        late, token = combined([], after=[token], rider=([late], [qkv_chain.rider()], ()))
        *sends, pair, token = combined(
            inner_chain.add() + qkv_chain.add() + with_pair(), after=[token], riders=[(0, early), (2, late)]
        )
        inner_chain.send(*sends[:2])
        qkv_chain.send(*sends[2:4])
        outer_chain.send(*sends[4:])
        early, token = combined([], after=[token], rider=([early], [inner_chain.rider()], ()))
        late, token = combined([], after=[token], rider=([late], [qkv_chain.rider()], ()))
        height = pair.shape[0]
        shared = [(height, [(pair, 0, 0)]), (height, [(outer_chain.got[0], outer_chain.count, 0)])]
        *sends, outer_sum, pair, token = combined(
            inner_chain.add() + qkv_chain.add() + outer_chain.add_last([half]) + [(half, LOW, shared)],
            after=[token],
            riders=[(0, early, True), (2, late)],
        )
        inner_chain.send(*sends[:2])
        qkv_chain.send(*sends[2:])
        pool_sum, token = call(
            pool_gradient,
            [((features // dp, features), F32, VMEM), ((8, LANES), F32, FAR)],
            [(pair, VMEM), (token, FAR)],
            scratch=[pltpu.VMEM((features, features), F32)],
            limit=SMALL_BYTES,
        )
        late, token = combined([], after=[token], rider=([late], [qkv_chain.rider()], ()))
        *sends, inner_sum, token = combined(
            qkv_chain.add() + inner_chain.add_last([units // 2]), after=[token], riders=[(0, late, True)]
        )
        early, token = combined([], after=[token], rider=([early], [inner_chain.rider(True)], ()))
        qkv_chain.send(*sends)
        qkv_sum, output_sum, late, token = combined(
            qkv_chain.add_last([3 * half, half]),
            rider=([late], [qkv_chain.rider(True)], ()),
        )
    else:
        early = add_over(early, list(range(1, dp)))
        late = add_over(late + late_other, list(range(1, dp)))
    if not place.fast:
        pair = outer_chain.own[units:] + outer_chain.got[0][units:]
        pair = lax.all_gather(pair, "dp")
        pair = pair.reshape(dp, 2, 2, 2, seqs // ramps, half)
        pair = jnp.moveaxis(pair, 1, 4).reshape(dp, 2, 2, seqs // ramps, features)
        states = pair[:, :, 0].reshape(-1, features)
        pre_grads = pair[:, :, 1].reshape(-1, features)
        own_rows = features // dp
        states = lax.dynamic_slice_in_dim(
            states, lax.axis_index("dp") * own_rows, own_rows, axis=1
        )
        pool_sum = first_times(states, pre_grads)
        (outer_sum,) = outer_chain.plain([half])
        (inner_sum,) = inner_chain.plain([units // 2])
        qkv_sum, output_sum = qkv_chain.plain([3 * half, half])
    early_other = swap_core(early)
    (
        rms, inner_bias_sum, outer_bias_sum, second_scale_sum, second_shift_sum,
        pool_bias_sum, class_sum, class_bias_sum,
        query_bias_sum, value_bias_sum, output_bias_sum, first_scale_sum, first_shift_sum,
    ) = call(
        partial(hand_out, features, rows * features * dp * ramps),
        [((3,), F32, VMEM), ((units,), F32, VMEM)]
        + [((features,), F32, VMEM)] * 3
        + [((1, features), F32, VMEM), ((CLASSES, 1, features), F32, VMEM), ((1, CLASSES), F32, VMEM)]
        + [((features,), F32, VMEM)] * 5,
        [(early, VMEM), (early_other, VMEM), (late, VMEM)],
        limit=SMALL_BYTES,
    )
    return (
        output,
        logits,
        rms,
        input_grad,
        qkv_sum,
        query_bias_sum,
        value_bias_sum,
        output_sum,
        output_bias_sum,
        first_scale_sum,
        first_shift_sum,
        inner_sum,
        inner_bias_sum,
        outer_sum,
        outer_bias_sum,
        second_scale_sum,
        second_shift_sum,
        pool_sum[None],
        pool_bias_sum,
        jnp.transpose(class_sum, (1, 2, 0)),
        class_bias_sum,
    )


def solution(mesh):
    whole = P(("dp", "ramp"), None)
    return jax.shard_map(
        on_device,
        mesh=mesh,
        in_specs=(whole, whole)
        + (P(),) * 13
        + (
            P("ramp", None, None),
            P("ramp", None),
            P("ramp", None, None),
            P("ramp", None),
            P(("dp", "ramp")),
            P(("dp", "ramp")),
        ),
        out_specs=(
            whole,
            whole,
            P(),
            whole,
            P("dp", "ramp"),
            P(),
            P(),
            P("dp", "ramp"),
            P(),
            P(),
            P(),
            P("dp", "ramp"),
            P(),
            P("dp", "ramp"),
            P(),
            P(),
            P(),
            P("ramp", "dp", None),
            P("ramp", None),
            P("ramp", None, None),
            P("ramp", None),
        ),
        check_vma=False,
    )
```

```python
from functools import partial

import jax
import jax.numpy as jnp
from jax import lax
from jax.experimental import pallas as pl
from jax.experimental.pallas import tpu as pltpu
from jax.sharding import PartitionSpec as P

HEADS = 12
CLASSES = 3
LANES = 128
EPS = 1e-06
F32 = jnp.float32
LOW = jnp.bfloat16
NEAR = pl.BlockSpec(memory_space=pltpu.VMEM)
VMEM = pltpu.VMEM
SMEM = pltpu.SMEM
FAR = pl.BlockSpec(memory_space=pl.ANY)
VMEM_BYTES = 60 * 1024 * 1024
SMALL_BYTES = 16 * 1024 * 1024


def times(left, right):
    return lax.dot_general(left, right, (((1,), (0,)), ((), ())), preferred_element_type=F32)


def times_transposed(left, right):
    return lax.dot_general(left, right, (((1,), (1,)), ((), ())), preferred_element_type=F32)


def first_times(left, right):
    return lax.dot_general(left, right, (((0,), (0,)), ((), ())), preferred_element_type=F32)


def row_sum(values):
    return jnp.sum(values, axis=-1, keepdims=True)


def column_sum(values):
    return jnp.sum(values, axis=0, keepdims=True)


def call(body, outs, args, scratch=(), flops=0, nbytes=0, limit=VMEM_BYTES):
    near_in = [number for number, (_, spec) in enumerate(args) if spec in (VMEM, SMEM)]
    near_out = [number for number, (_, _, spec) in enumerate(outs) if spec in (VMEM, SMEM)]
    copies = [args[number][1](args[number][0].shape, args[number][0].dtype) for number in near_in]
    copies += [outs[number][2](outs[number][0], outs[number][1]) for number in near_out]

    def kernel(*refs):
        ins, refs = list(refs[: len(args)]), refs[len(args) :]
        results, refs = list(refs[: len(outs)]), refs[len(outs) :]
        own, refs = refs[: len(scratch)], refs[len(scratch) :]
        held, sems = refs[:-1], refs[-1]
        moving = []
        for place, number in enumerate(near_in):
            moving.append(pltpu.make_async_copy(ins[number], held[place], sems.at[place]))
            ins[number] = held[place]
        for copy in moving:
            copy.start()

        def ready():
            while moving:
                moving.pop(0).wait()

        far = {}
        for place, number in enumerate(near_out, len(near_in)):
            far[place] = results[number]
            results[number] = held[place]
        mover = body(ready, *ins, *results, *own)
        ready()
        leaving = [
            pltpu.make_async_copy(held[place], target, sems.at[place]) for place, target in far.items()
        ]
        for copy in leaving:
            copy.start()
        if mover is not None:
            mover.finish()
        for copy in leaving:
            copy.wait()

    return pl.pallas_call(
        kernel,
        out_shape=tuple(jax.ShapeDtypeStruct(shape, kind) for shape, kind, _ in outs),
        in_specs=[NEAR if spec is NEAR else FAR for _, spec in args],
        out_specs=tuple([NEAR if spec is NEAR else FAR for _, _, spec in outs]),
        scratch_shapes=list(scratch)
        + copies
        + [pltpu.SemaphoreType.DMA((max(1, len(near_in) + len(near_out)),))],
        compiler_params=pltpu.CompilerParams(vmem_limit_bytes=limit),
        cost_estimate=pl.CostEstimate(flops=flops, bytes_accessed=nbytes, transcendentals=0),
    )(*[array for array, _ in args])


class Mover:
    def __init__(self, sems):
        self.sems = sems
        self.used = 0
        self.open = []

    def start(self, source, target):
        copy = pltpu.make_async_copy(source, target, self.sems.at[self.used])
        self.used += 1
        copy.start()
        return copy

    def out(self, source, target):
        self.open.append(self.start(source, target))

    def finish(self):
        for copy in self.open:
            copy.wait()


class Feed:
    def __init__(self, mover, pairs, depth):
        self.mover = mover
        self.pairs = pairs
        self.running = []
        self.done = 0
        for _ in range(depth):
            self.more()

    def more(self):
        if len(self.running) < len(self.pairs):
            self.running.append(self.mover.start(*self.pairs[len(self.running)]))

    def ahead(self):
        while len(self.running) < len(self.pairs):
            self.more()

    def need(self, count):
        while self.done < count:
            self.running[self.done].wait()
            self.done += 1
            self.more()


X, Y, NEAR_Z, FAR_Z = 1, 2, 4, 8
STEPS = 4
OUTER_WAYS = ((X, Y, NEAR_Z, FAR_Z), (NEAR_Z, Y, X, FAR_Z))
INNER_WAYS = OUTER_WAYS
QKV_WAYS = ((X, Y, NEAR_Z, FAR_Z), (NEAR_Z, X, Y, FAR_Z))


class Place:
    def __init__(self, dp, rows):
        self.dp = dp
        self.fast = dp == 1 << STEPS and rows % (16 * dp) == 0
        self.count = 4 if self.fast else 1

    def flip(self, position, ways, core):
        flips = []
        for way in ways:
            flips.append(sum(way[step] for step in range(STEPS) if not position >> (STEPS - 1 - step) & 1))
        return jnp.where(core == 0, flips[0], flips[1])

    def out(self, mover, source, columns, fars, core, size, ways, start=0):
        width = columns.size if isinstance(columns, pl.Slice) else columns.stop - columns.start
        target = slice(start, start + width)
        if not self.fast:
            there = slice(0, source.shape[0])
            if mover is None:
                fars[0][there, target] = source[:, columns]
            else:
                mover.out(source.at[:, columns], fars[0].at[there, target])
            return
        each = self.dp // len(fars)
        for position in range(self.dp):
            block = lax.axis_index("dp") ^ self.flip(position, ways, core)
            here = pl.ds(pl.multiple_of(block * size, 16), size)
            inside = position % each
            there = slice(inside * size, (inside + 1) * size)
            far = fars[position // each]
            if mover is None:
                far[there, target] = source[here, columns]
            else:
                mover.out(source.at[here, columns], far.at[there, target])

    def out_part(self, mover, source, columns, far, core, first, size, ways):
        if not self.fast:
            rows = slice(first * size, first * size + source.shape[0])
            mover.out(source.at[:, columns], far.at[rows, :])
            return
        for step in range(source.shape[0] // size):
            diff = lax.axis_index("dp") ^ (first + step)
            place = 0
            for number in range(STEPS):
                mask = jnp.where(core == 0, ways[0][number], ways[1][number])
                place = place * 2 + ((diff & mask) == 0).astype(jnp.int32)
            offset = pl.multiple_of(place * size, 16)
            mover.out(
                source.at[step * size : (step + 1) * size, columns], far.at[pl.ds(offset, size), :]
            )


def half_of(which, half):
    return pl.ds(pl.multiple_of(which * half, LANES), half)


def head_masks(rows):
    lane = lax.broadcasted_iota(jnp.int32, (rows, LANES), 1)
    left = (lane < LANES // 2).astype(F32).astype(LOW)
    right = (lane >= LANES // 2).astype(F32).astype(LOW)
    return left, right


def gelu_both(inner):
    density = jnp.exp(inner * inner * (-0.5)) * 0.3989422804014327
    below = 0.5 + 0.5 * lax.erf(inner * 0.7071067811865476)
    return inner * below, below + inner * density


def forward(
    place, length, ramp_count, ready,
    x_far, qkv_far, query_bias_ref, value_bias_ref, output_far, output_bias_ref,
    first_scale_ref, first_shift_ref, inner_far, inner_bias_ref, outer_far,
    outer_bias_ref, second_scale_ref, second_shift_ref, cot_far, pool_own_far, pool_other_far,
    pool_bias_own_ref, pool_bias_other_ref, class_own_ref, class_other_ref,
    class_bias_own_ref, class_bias_other_ref, labels_ref, ramps_ref,
    mixed_far, probs_far, context_far, normal_far, low_far, spread_ref,
    final_far, logits_ref, slope_far, resid_far, full_far, vector_ref, *refs,
):
    sends, owns, refs = refs[: place.count], refs[place.count : place.count + 1], refs[place.count + 1 :]
    (
    x_ref, qkv_ref, output_ref, mixed_ref, probs_ref, context_ref, normal_ref,
    inner_ref, outer_ref, cot_ref, pool_own_ref, pool_other_ref,
    final_ref, acted_ref, slope_ref, resid_ref, full_ref,
    low_ref, sum_ref, second_spread_ref, pair_own_ref, pair_send_ref, sems,
    ) = refs
    rows, features = x_ref.shape
    hidden_units = inner_ref.shape[1]
    seqs = rows // length
    pairs = features // LANES
    factor = (features // HEADS) ** (-0.5)
    core = lax.axis_index("ramp")
    mover = Mover(sems)
    parts = [slice(part * features, (part + 1) * features) for part in range(3)]
    steps = [
        slice(one * features, (one + 1) * features) for one in range(hidden_units // features)
    ]
    wanted = [(x_far, x_ref)]
    wanted += [(qkv_far.at[:, one], qkv_ref.at[:, one]) for one in parts]
    wanted += [(output_far, output_ref)]
    for one in steps:
        wanted += [(inner_far.at[:, one], inner_ref.at[:, one])]
        wanted += [(outer_far.at[one], outer_ref.at[one])]
    wanted += [(pool_own_far, pool_own_ref), (pool_other_far, pool_other_ref), (cot_far, cot_ref)]
    feed = Feed(mover, wanted, 3)
    ready()
    for part, columns in enumerate(parts):
        feed.need(2 + part)
        mixed = times(x_ref[...], qkv_ref[:, columns])
        if part == 0:
            mixed = mixed + query_bias_ref[...][None, :]
        if part == 2:
            mixed = mixed + value_bias_ref[...][None, :]
        mixed_ref[:, columns] = mixed.astype(LOW)
    feed.ahead()
    left, right = head_masks(length)
    left_t, right_t = left.T, right.T

    def one_sequence(seq, carry):
        here = pl.ds(pl.multiple_of(seq * length, length), length)
        for pair in range(pairs):
            start = pair * LANES
            query = mixed_ref[here, start : start + LANES]
            key = mixed_ref[here, features + start : features + start + LANES]
            value = mixed_ref[here, 2 * features + start : 2 * features + start + LANES]
            stacked = jnp.concatenate([query * left, query * right], axis=0)
            scores = times_transposed(key, stacked)
            top = jnp.max(scores, axis=0, keepdims=True)
            raised = jnp.exp((scores - top) * factor)
            probs = (raised * (1.0 / column_sum(raised))).astype(LOW)
            probs_ref[pl.ds(seq * pairs + pair, 1)] = probs[None]
            value_t = value.T
            both = jnp.concatenate([value_t * left_t, value_t * right_t], axis=1)
            tall = jnp.concatenate([probs[:, :length], probs[:, length:]], axis=0)
            context_t = times(both, tall).astype(LOW)
            context_ref[here, start : start + LANES] = context_t.T
        return carry

    lax.fori_loop(0, seqs, one_sequence, 0, unroll=2)
    feed.need(5)
    mover.out(mixed_ref, mixed_far)
    mover.out(probs_ref, probs_far)
    mover.out(context_ref, context_far)
    normal_ref[...] = times(context_ref[...], output_ref[...]) + output_bias_ref[...][None, :]
    hidden_square = jnp.zeros((1, features), F32)
    attended_square = jnp.zeros((1, features), F32)
    first_scale = first_scale_ref[...][None, :]
    first_shift = first_shift_ref[...][None, :]
    outer_bias = outer_bias_ref[...][None, :]
    for seq in range(seqs):
        here = slice(seq * length, (seq + 1) * length)
        hidden = x_ref[here, :].astype(F32)
        attended = normal_ref[here, :]
        residual = hidden + attended
        centred = residual - row_sum(residual) * (1.0 / features)
        spread = lax.rsqrt(row_sum(centred * centred) * (1.0 / features) + EPS)
        normal = centred * spread
        normal_ref[here, :] = normal
        spread_ref[here, :] = spread
        first = normal * first_scale + first_shift
        low_ref[here, :] = first.astype(LOW)
        sum_ref[here, :] = first + outer_bias
        hidden_square = hidden_square + column_sum(hidden * hidden)
        attended_square = attended_square + column_sum(attended * attended)
    mover.out(normal_ref, normal_far)
    mover.out(low_ref, low_far)

    feed.need(5 + 2 * len(steps))

    def inner_of(columns):
        return times(low_ref[...], inner_ref[:, columns]) + inner_bias_ref[columns][None, :]

    inner = inner_of(steps[0])
    for step, columns in enumerate(steps):
        following = inner_of(steps[step + 1]) if step + 1 < len(steps) else None
        acted, slope = gelu_both(inner)
        acted = acted.astype(LOW)
        acted_ref[:, columns] = acted
        slope_ref[:, columns] = slope.astype(LOW)
        sum_ref[...] += times(acted, outer_ref[columns, :])
        inner = following
    mover.out(slope_ref, slope_far)

    scale = second_scale_ref[...][None, :]
    shift = second_shift_ref[...][None, :]
    square = jnp.zeros((1, features), F32)
    leading = []
    for seq in range(seqs):
        here = slice(seq * length, (seq + 1) * length)
        residual = sum_ref[here, :]
        outer = residual - (normal_ref[here, :] * first_scale + first_shift)
        square = square + column_sum(outer * outer)
        centred = residual - row_sum(residual) * (1.0 / features)
        spread = lax.rsqrt(row_sum(centred * centred) * (1.0 / features) + EPS)
        normal = centred * spread
        sum_ref[here, :] = normal
        second_spread_ref[here, :] = spread
        final = (normal * scale + shift).astype(LOW)
        final_ref[here, :] = final
        leading.append(final[0:1, :].astype(F32))
    mover.out(final_ref, final_far)

    feed.need(len(wanted) - 1)
    leading = jnp.concatenate(leading + [jnp.zeros((8 - seqs, features), F32)], axis=0)
    states = leading.astype(LOW)
    row = lax.broadcasted_iota(jnp.int32, (8, 1), 0)
    ramp_of = jnp.full((8, 1), -1, jnp.int32)
    label_of = jnp.full((8, 1), -1, jnp.int32)
    for seq in range(seqs):
        ramp_of = jnp.where(row == seq, ramps_ref[seq], ramp_of)
        label_of = jnp.where(row == seq, labels_ref[seq], label_of)
    own = ramp_of == core
    pre_own = times(states, pool_own_ref[0]) + pool_bias_own_ref[...]
    pre_other = times(states, pool_other_ref[0]) + pool_bias_other_ref[...]
    pooled = jnp.tanh(jnp.where(own, pre_own, pre_other))
    pooled_low = pooled.astype(LOW)
    logits = jnp.where(
        own,
        times_transposed(pooled_low, class_own_ref[0]) + class_bias_own_ref[...],
        times_transposed(pooled_low, class_other_ref[0]) + class_bias_other_ref[...],
    )
    logits_ref[...] = logits[:seqs, :]
    raised = jnp.exp(logits - jnp.max(logits, axis=-1, keepdims=True))
    kind = lax.broadcasted_iota(jnp.int32, (8, CLASSES), 1)
    grads = raised / row_sum(raised) - (kind == label_of).astype(F32)
    grads = jnp.where(ramp_of >= 0, grads, 0.0)
    grads_high = grads.astype(LOW)
    grads_rest = (grads - grads_high.astype(F32)).astype(LOW)

    def from_logits(weight):
        return times(grads_high, weight) + times(grads_rest, weight)

    pooled_grad = jnp.where(own, from_logits(class_own_ref[0]), from_logits(class_other_ref[0]))
    pre_low = (pooled_grad * (1.0 - pooled * pooled)).astype(LOW).astype(F32)
    pre_own_low = jnp.where(own, pre_low, 0.0).astype(LOW)
    pre_other_low = jnp.where(own, 0.0, pre_low).astype(LOW)
    state_grad = times_transposed(pre_own_low, pool_own_ref[0])
    state_grad = state_grad + times_transposed(pre_other_low, pool_other_ref[0])
    chosen_row = lax.broadcasted_iota(jnp.int32, (8, 8), 0)
    chosen_seq = lax.broadcasted_iota(jnp.int32, (8, 8), 1)
    per_ramp = seqs // ramp_count
    for ref, which, top in ((pair_own_ref, core, 0), (pair_send_ref, 1 - core, 2 * per_ramp)):
        pick_states = jnp.zeros((8, 8), jnp.bool_)
        pick_grads = jnp.zeros((8, 8), jnp.bool_)
        for seq in range(seqs):
            rank = jnp.int32(0)
            for other in range(seq):
                rank = rank + (ramps_ref[other] == which).astype(jnp.int32)
            here = (chosen_seq == seq) & (ramps_ref[seq] == which)
            pick_states = pick_states | (here & (chosen_row == top + rank))
            pick_grads = pick_grads | (here & (chosen_row == top + per_ramp + rank))
        rows_of_pair = times(pick_states.astype(F32).astype(LOW), states)
        rows_of_pair = rows_of_pair + times(pick_grads.astype(F32).astype(LOW), pre_low.astype(LOW))
        folded = jnp.concatenate([rows_of_pair[:, : features // 2], rows_of_pair[:, features // 2 :]], axis=0)
        ref[...] = folded.astype(LOW)

    vector_ref[...] = jnp.zeros(vector_ref.shape, F32)
    for ramp in range(ramp_count):
        mask = ramp_of == ramp
        base = 8 * (ramp + 1)
        vector_ref[base : base + 1, :] = column_sum(jnp.where(mask, pre_low, 0.0))
        high = jnp.where(mask, grads_high.astype(F32), 0.0).astype(LOW)
        rest = jnp.where(mask, grads_rest.astype(F32), 0.0).astype(LOW)
        vector_ref[base + 1 : base + 1 + CLASSES, :] = first_times(high, pooled_low) + first_times(
            rest, pooled_low
        )
        vector_ref[base + 4 : base + 5, 0:CLASSES] = column_sum(jnp.where(mask, grads, 0.0))

    feed.need(len(wanted))
    scale_grad = jnp.zeros((1, features), F32)
    shift_grad = jnp.zeros((1, features), F32)
    bias_grad = jnp.zeros((1, features), F32)
    at_first = lax.broadcasted_iota(jnp.int32, (length, 1), 0) == 0
    for seq in range(seqs):
        here = slice(seq * length, (seq + 1) * length)
        final_grad = cot_ref[here, :].astype(F32)
        final_grad = final_grad + jnp.where(at_first, state_grad[seq : seq + 1, :], 0.0)
        normal = sum_ref[here, :]
        scale_grad = scale_grad + column_sum(final_grad * normal)
        shift_grad = shift_grad + column_sum(final_grad)
        scaled = final_grad * scale
        resid = second_spread_ref[here, :] * (
            scaled
            - row_sum(scaled) * (1.0 / features)
            - normal * (row_sum(scaled * normal) * (1.0 / features))
        )
        resid_ref[here, :] = resid
        low = resid.astype(LOW)
        full_ref[here, :] = low
        bias_grad = bias_grad + column_sum(low.astype(F32))
    mover.out(full_ref, full_far)
    mover.out(resid_ref, resid_far)
    below = pl.ds(hidden_units, 16)
    mover.out(pair_own_ref, owns[0].at[below])
    mover.out(pair_send_ref, sends[0].at[pl.ds(hidden_units // place.count, 16)])
    size = hidden_units // place.dp
    half = features // 2
    for step, columns in enumerate(steps):
        outer_ref[columns, :] = first_times(acted_ref[:, columns], full_ref[...]).astype(LOW)
        place.out_part(
            mover, outer_ref.at[columns], half_of(core, half), owns[0], core, step * features // size, size, OUTER_WAYS
        )
    place.out(mover, outer_ref, half_of(1 - core, half), sends, 1 - core, size, OUTER_WAYS)
    vector_ref[0:1, :] = bias_grad
    vector_ref[1:2, :] = scale_grad
    vector_ref[2:3, :] = shift_grad
    vector_ref[3:4, 0:1] = row_sum(hidden_square)
    vector_ref[3:4, 1:2] = row_sum(attended_square)
    vector_ref[3:4, 2:3] = row_sum(square)
    return mover


def feed_backward(
    place, length, ready,
    full_far, slope_far, outer_far, inner_far, resid_far, first_far, after_far,
    first_grad_far, vector_ref, *refs,
):
    sends, owns, refs = refs[: place.count], refs[place.count : place.count + 1], refs[place.count + 1 :]
    full_ref, slope_ref, outer_ref, inner_ref, sum_ref, weight_ref, first_ref, sems = refs
    rows, features = first_ref.shape
    core = lax.axis_index("ramp")
    hidden_units = slope_ref.shape[1]
    half = hidden_units // 2
    mover = Mover(sems)
    order = []
    for fars, who in ((sends, 1 - core), (owns, core)):
        for start in range(0, half, features):
            number = who * (half // features) + start // features
            columns = pl.ds(pl.multiple_of(number * features, LANES), features)
            order.append((fars, who, start, number, columns))
    wanted = [(full_far, full_ref)]
    for _, _, _, _, columns in order:
        wanted.append((outer_far.at[columns], outer_ref.at[columns]))
        wanted.append((slope_far.at[:, columns], slope_ref.at[:, columns]))
        if len(wanted) == 3:
            wanted.append((first_far, first_ref))
        wanted.append((inner_far.at[:, columns], inner_ref.at[:, columns]))
        if len(wanted) == 5:
            wanted.append((resid_far, sum_ref))
    feed = Feed(mover, wanted, 7)
    ready()
    vector_ref[...] = jnp.zeros(vector_ref.shape, F32)
    size = features // place.dp

    def acted_grad_of(step):
        return times_transposed(full_ref[...], outer_ref[order[step][4], :])

    feed.need(2)
    acted_grad = acted_grad_of(0)
    for step, (fars, who, start, number, columns) in enumerate(order):
        feed.need(min(6 + 3 * step + 1, len(wanted)))
        following = acted_grad_of(step + 1) if step + 1 < len(order) else None
        inner_grad = (slope_ref[:, columns].astype(F32) * acted_grad).astype(LOW)
        vector_ref[pl.ds(number, 1), :] = column_sum(inner_grad.astype(F32))
        sum_ref[...] += times_transposed(inner_grad, inner_ref[:, columns])
        here = slice(step * features, (step + 1) * features)
        weight_ref[:, here] = first_times(first_ref[...], inner_grad).astype(LOW)
        place.out(None, weight_ref, here, fars, who, size, INNER_WAYS, start)
        acted_grad = following
    mover.out(sum_ref, first_grad_far)
    return mover


def attention_backward(
    place, length, ready,
    first_grad_far, normal_far, spread_ref, first_scale_ref, output_far, context_far,
    mixed_far, probs_far, x_far, after_far,
    grad_far, first_resid_far, vector_ref, *refs,
):
    sends, owns, refs = refs[: place.count], refs[place.count : place.count + 1], refs[place.count + 1 :]
    (
        first_grad_ref, normal_ref, output_ref, context_ref, low_ref, first_resid_ref,
        mixed_ref, probs_ref, context_grad_ref, x_ref, grad_ref, weight_ref, sems, out_sems,
    ) = refs
    rows, features = context_grad_ref.shape
    seqs = rows // length
    core = lax.axis_index("ramp")
    pairs = features // LANES
    factor = (features // HEADS) ** (-0.5)
    half = features // 2
    size = features // place.dp
    left, right = head_masks(length)
    mover = Mover(out_sems)
    wanted = [
        (first_grad_far, first_grad_ref),
        (normal_far, normal_ref),
        (output_far, output_ref),
        (context_far, context_ref),
    ]
    feed = Feed(mover, wanted, len(wanted))

    def copies(seq):
        here = pl.ds(pl.multiple_of(seq * length, length), length)
        heads = pl.ds(seq * pairs, pairs)
        return (
            pltpu.make_async_copy(mixed_far.at[here], mixed_ref.at[here], sems.at[0, seq]),
            pltpu.make_async_copy(probs_far.at[heads], probs_ref.at[heads], sems.at[1, seq]),
        )

    for seq in range(seqs):
        for copy in copies(seq):
            copy.start()
    got_x = mover.start(x_far, x_ref)
    ready()
    feed.need(2)
    scale = first_scale_ref[...][None, :]
    zero = jnp.zeros((1, features), F32)
    sums = [zero, zero, zero]
    for seq in range(seqs):
        here = slice(seq * length, (seq + 1) * length)
        first_grad = first_grad_ref[here, :]
        normal = normal_ref[here, :]
        scaled = first_grad * scale
        resid = spread_ref[here, :] * (
            scaled
            - row_sum(scaled) * (1.0 / features)
            - normal * (row_sum(scaled * normal) * (1.0 / features))
        )
        first_resid_ref[here, :] = resid
        low = resid.astype(LOW)
        low_ref[here, :] = low
        sums[0] = sums[0] + column_sum(low.astype(F32))
        sums[1] = sums[1] + column_sum(first_grad * normal)
        sums[2] = sums[2] + column_sum(first_grad)
    mover.out(first_resid_ref, first_resid_far)
    feed.need(len(wanted))
    context_grad_ref[...] = times_transposed(low_ref[...], output_ref[...]).astype(LOW)
    columns = slice(3 * features, 4 * features)
    weight_ref[:, columns] = first_times(context_ref[...], low_ref[...]).astype(LOW)
    for fars, who in ((sends, 1 - core), (owns, core)):
        columns = pl.ds(pl.multiple_of(3 * features + who * half, LANES), half)
        place.out(None, weight_ref, columns, fars, who, size, QKV_WAYS, 3 * half)

    def one_sequence(seq, carry):
        here = pl.ds(pl.multiple_of(seq * length, length), length)
        for copy in copies(seq):
            copy.wait()
        for pair in range(pairs):
            start = pair * LANES
            query = mixed_ref[here, start : start + LANES]
            key = mixed_ref[here, features + start : features + start + LANES]
            value = mixed_ref[here, 2 * features + start : 2 * features + start + LANES]
            context_grad = context_grad_ref[here, start : start + LANES]
            queries = jnp.concatenate([query * left, query * right], axis=0)
            keys = jnp.concatenate([key * left, key * right], axis=0)
            grads = jnp.concatenate([context_grad * left, context_grad * right], axis=0)
            probs = probs_ref[pl.ds(seq * pairs + pair, 1)][0]
            probs_grad = times_transposed(value, grads)
            wide = probs.astype(F32)
            score_grad = wide * (probs_grad - column_sum(wide * probs_grad))
            score_grad = score_grad.astype(LOW)
            value_grad = times(probs, grads).astype(LOW)
            key_grad = (times(score_grad, queries) * factor).astype(LOW)
            turned = jnp.concatenate(
                [score_grad[:, :length].T, score_grad[:, length:].T], axis=1
            )
            query_grad = (times(turned, keys) * factor).astype(LOW)
            grad_ref[here, start : start + LANES] = query_grad
            grad_ref[here, features + start : features + start + LANES] = key_grad
            grad_ref[here, 2 * features + start : 2 * features + start + LANES] = value_grad
        return carry

    lax.fori_loop(0, seqs, one_sequence, 0, unroll=2)
    mover.out(grad_ref, grad_far)
    got_x.wait()
    for fars, who in ((sends, 1 - core), (owns, core)):
        for start, width in ((0, features), (features, half)):
            columns = pl.ds(pl.multiple_of(who * 3 * half + start, LANES), width)
            weight_ref[:, columns] = first_times(x_ref[...], grad_ref[:, columns]).astype(LOW)
            place.out(None, weight_ref, columns, fars, who, size, QKV_WAYS, start)
    vector_ref[...] = jnp.zeros(vector_ref.shape, F32)
    vector_ref[0:1, :] = column_sum(grad_ref[:, :features].astype(F32))
    vector_ref[1:2, :] = column_sum(grad_ref[:, 2 * features :].astype(F32))
    for number, one in enumerate(sums):
        vector_ref[2 + number : 3 + number, :] = one
    return mover


def input_gradient(
    ready,
    grad_far, qkv_far, resid_far, after_far,
    result_far, token_far,
    grad_ref, qkv_ref, resid_ref, result_ref, sems,
):
    mover = Mover(sems)
    features = resid_ref.shape[1]
    parts = [slice(part * features, (part + 1) * features) for part in range(3)]
    got = []
    for one in parts:
        got.append(
            (
                mover.start(grad_far.at[:, one], grad_ref.at[:, one]),
                mover.start(qkv_far.at[:, one], qkv_ref.at[:, one]),
            )
        )
    got_resid = mover.start(resid_far, resid_ref)
    total = None
    for columns, copies in zip(parts, got):
        for copy in copies:
            copy.wait()
        product = times_transposed(grad_ref[:, columns], qkv_ref[:, columns])
        total = product if total is None else total + product
    got_resid.wait()
    result_ref[...] = (resid_ref[...] + total).astype(LOW)
    mover.out(result_ref, result_far)
    return mover


def swap_core(values):
    return lax.ppermute(values, "ramp", [(0, 1), (1, 0)])


def shift(values, even, odd):
    dp = lax.axis_size("dp")
    pairs = []
    for one in range(dp):
        pairs.append((2 * one, 2 * (one ^ even)))
        pairs.append((2 * one + 1, 2 * (one ^ odd) + 1))
    return lax.ppermute(values, ("dp", "ramp"), pairs)


RIDERS = 16


def pack(ref, total, top, beside):
    high = total.astype(LOW)
    rest = (total - high.astype(F32)).astype(LOW)
    count = total.shape[0] // RIDERS
    if beside is not None:
        spots = rider_spots(ref.shape[0], total.shape[0])
        ref[:, beside:] = jnp.zeros((ref.shape[0], ref.shape[1] - beside), LOW)
        for values, number, row, start in spots:
            part = (high, rest)[values][number * RIDERS : (number + 1) * RIDERS, :]
            ref[row : row + RIDERS, beside + start : beside + start + LANES] = part
        return
    ref[top : top + RIDERS, :] = jnp.zeros((RIDERS, ref.shape[1]), LOW)
    for number in range(count):
        rows = slice(number * RIDERS, (number + 1) * RIDERS)
        for part, values in enumerate((high, rest)):
            start = (part * count + number) * LANES
            ref[top : top + RIDERS, start : start + LANES] = values[rows, :]


def rider_spots(height, rows):
    spots = []
    for number in range(rows // RIDERS):
        below, beside = number % (height // RIDERS), number // (height // RIDERS)
        spots.append((0, number, below * RIDERS, beside * LANES))
    return spots


def rider_width(height, rows):
    return rider_spots(height, rows)[-1][3] + LANES


def unpack(ref, count, top, beside):
    parts = [None] * count
    if beside is not None:
        for _, number, row, start in rider_spots(ref.shape[0], count * RIDERS):
            term = ref[row : row + RIDERS, beside + start : beside + start + LANES].astype(F32)
            parts[number] = term if parts[number] is None else parts[number] + term
    else:
        for number in range(count):
            start, rest = number * LANES, (count + number) * LANES
            high = ref[top : top + RIDERS, start : start + LANES].astype(F32)
            parts[number] = high + ref[top : top + RIDERS, rest : rest + LANES].astype(F32)
    return parts[0] if count == 1 else jnp.concatenate(parts, axis=0)


def combine(plan, count, rider, carried, ready, *refs):
    arrays, results = refs[:count], refs[count:]
    if rider is not None:
        plain, packed, into, beside = rider
        out_ref = results[len(plan)]
        total = None
        for number in plain:
            total = arrays[number][...] if total is None else total + arrays[number][...]
        for number, top, side in packed:
            total = total + unpack(arrays[number], total.shape[0] // RIDERS, top, side)
        out_ref[...] = total
    for number, (parts, result) in enumerate(zip(plan, results)):
        top = 0
        for rows, width, terms in parts:
            total_rows = None
            wide = len(terms) > 2 or result.dtype == F32
            for array, row, column in terms:
                term = arrays[array][row : row + rows, column : column + width]
                term = term.astype(F32) if wide else term
                total_rows = term if total_rows is None else total_rows + term
            result[top : top + rows, :width] = total_rows.astype(result.dtype)
            top += rows
        if rider is not None and number in into:
            pack(result, total, top, parts[0][1] if beside else None)
        if number in carried:
            sums, side = carried[number]
            pack(result, arrays[sums][...], top, parts[0][1] if side else None)


def combined(results, after=(), rider=None, riders=()):
    arrays = []

    def number(array):
        for place, one in enumerate(arrays):
            if one is array:
                return place
        arrays.append(array)
        return len(arrays) - 1

    plan = [
        [(rows, width, [(number(array), row, column) for array, row, column in terms]) for rows, terms in parts]
        for width, _, parts in results
    ]
    ride, extra, into, beside = None, [], (), False
    if rider is not None:
        plain, packed, into, *rest = rider
        beside = bool(rest)
        ride = ([number(one) for one in plain], [(number(one), *where) for one, *where in packed], into, beside)
        extra = [(plain[0].shape, F32, NEAR)]
    shapes = []
    carried = {}
    for place, sums, *rest in riders:
        carried[place] = (number(sums), bool(rest))
    for place, (width, kind, parts) in enumerate(results):
        height = sum(part[0] for part in parts)
        if place in carried and carried[place][1]:
            width = width + rider_width(height, arrays[carried[place][0]].shape[0])
        elif place in carried:
            height = height + RIDERS
        if place in into and beside:
            width = width + rider_width(height, plain[0].shape[0])
        elif place in into:
            height = height + RIDERS
        shapes.append(((height, width), kind))
    return call(
        partial(combine, plan, len(arrays) + len(after), ride, carried),
        [(shape, kind, NEAR) for shape, kind in shapes] + extra + [((8, LANES), F32, FAR)],
        [(array, NEAR) for array in arrays] + [(array, FAR) for array in after],
        nbytes=sum(8 * shape[0] * shape[1] for shape, _ in shapes),
        limit=SMALL_BYTES,
    )


class Chain:
    def __init__(self, sends, own, ways, spare=0):
        self.own = own
        self.ways = ways
        self.step = 0
        self.count = own.shape[0] - spare
        self.got = [swap_core(one) for one in sends]
        self.heights = [self.count // len(sends)] * len(sends)
        self.width = own.shape[1]

    def come(self, start, count):
        spans = []
        top = 0
        for one, height in zip(self.got, self.heights):
            low, high = max(start, top), min(start + count, top + height)
            if low < high:
                spans.append((high - low, (one, low - top, 0)))
            top += height
        return spans

    def parts(self, start, count):
        result = []
        for rows, place in self.come(start, count):
            result.append((rows, [(self.own, start, 0), place]))
            start += rows
        return result

    def add(self):
        rows = self.count // 2
        return [(self.width, LOW, self.parts(start, rows)) for start in (0, rows)]

    def send(self, array, keep):
        self.got, self.own = [shift(array, self.ways[0][self.step], self.ways[1][self.step])], keep
        self.step += 1
        self.count = keep.shape[0]
        self.heights = [self.count]

    def rider(self, beside=False):
        return (self.got[0], 0, self.width) if beside else (self.got[0], self.count, None)

    def gather(self, results, number, *terms):
        width, kind, parts = results[number]
        results[number] = (width, kind, parts + list(terms))
        return results

    def add_last(self, widths):
        results = []
        start = 0
        for width in widths:
            terms = [(array, 0, start) for array in (self.own, self.got[0])]
            results.append((width, F32, [(self.count, terms)]))
            start += width
        return results

    def plain(self, widths):
        total = (self.own[: self.count].astype(F32) + self.got[0][: self.count].astype(F32)).astype(LOW)
        rows = lax.psum_scatter(total, "dp", scatter_dimension=0, tiled=True).astype(F32)
        ends = [sum(widths[: one + 1]) for one in range(len(widths))]
        return [rows[:, end - width : end] for width, end in zip(widths, ends)]


EARLY_ROWS, LATE_ROWS = 96, 32


def put_rows(out_ref, place, row):
    for start in range(0, row.shape[1], LANES):
        out_ref[place : place + 1, :] = row[:, start : start + LANES]
        place += 1
    return place


def collect_late(ready, mixed_ref, after_far, out_ref):
    ready()
    out_ref[...] = jnp.zeros(out_ref.shape, F32)
    place = 0
    for number in range(5):
        place = put_rows(out_ref, place, mixed_ref[number : number + 1, :])


def collect_early(ready, first_ref, second_ref, after_far, out_ref):
    ready()
    out_ref[...] = jnp.zeros(out_ref.shape, F32)
    place = 0
    for number in range(first_ref.shape[0] // 2):
        place = put_rows(out_ref, place, first_ref[number : number + 1, :])
    for number in range(3):
        place = put_rows(out_ref, place, second_ref[number : number + 1, :])
    for base in (8, 16):
        for number in range(1 + CLASSES):
            place = put_rows(out_ref, place, second_ref[base + number : base + number + 1, :])
    for number in (3, 12, 20):
        place = put_rows(out_ref, place, second_ref[number : number + 1, :LANES])


def add_all(ready, *refs):
    ready()
    *refs, after_far, out_ref = refs
    total = refs[0][...]
    for ref in refs[1:]:
        total = total + ref[...]
    out_ref[...] = total


def add_over(values, masks, after=None):
    got = [shift(values, mask, mask) for mask in masks]
    (total,) = call(
        add_all,
        [(values.shape, values.dtype, VMEM)],
        [(one, VMEM) for one in [values] + got] + [((after or [values])[0], FAR)],
        limit=SMALL_BYTES,
    )
    return total


def take_rows(all_ref, place, ref, start, width):
    for column in range(0, width, LANES):
        ref[pl.ds(start + column, LANES)] = all_ref[place, :]
        place += 1
    return place


def hand_out(features, entries, ready, all_ref, other_ref, late_ref, *outs):
    ready()
    all_ref[...] += other_ref[...]
    place = 0
    for ref in outs[8:]:
        place = take_rows(late_ref, place, ref, 0, features)
    outs = outs[:8]
    core = lax.axis_index("ramp")
    rms_ref, inner_ref, outer_ref, second_scale_ref, second_shift_ref = outs[:5]
    pool_ref, class_ref, class_bias_ref = outs[5:]
    place = 0
    for ref in (inner_ref, outer_ref, second_scale_ref, second_shift_ref):
        place = take_rows(all_ref, place, ref, 0, ref.shape[0])
    step = features // LANES
    size = step * (1 + CLASSES)
    for column in range(step):
        at = column * LANES
        first = all_ref[place + column : place + column + 1, :]
        second = all_ref[place + size + column : place + size + column + 1, :]
        pool_ref[:, at : at + LANES] = jnp.where(core == 0, first, second)
        for kind in range(CLASSES):
            row = place + (1 + kind) * step + column
            first = all_ref[row : row + 1, :]
            second = all_ref[row + size : row + size + 1, :]
            class_ref[kind, :, at : at + LANES] = jnp.where(core == 0, first, second)
    place += 2 * size
    rms_ref[...] = jnp.sqrt(all_ref[place, :] * (1.0 / entries))[: rms_ref.shape[0]]
    first = all_ref[place + 1 : place + 2, :CLASSES]
    second = all_ref[place + 2 : place + 3, :CLASSES]
    class_bias_ref[...] = jnp.where(core == 0, first, second)


def pool_gradient(ready, pair_ref, after_far, out_ref, token_far, all_ref):
    ready()
    height, half = pair_ref.shape
    blocks = pair_ref[...].astype(F32).reshape(height // 16, 16, half)
    rows = jnp.concatenate([blocks[:, 0:8, :], blocks[:, 8:16, :]], axis=2)
    rows = rows.reshape(height // 2, 2 * half).astype(LOW)
    at = lax.broadcasted_iota(jnp.int32, (height // 2, height // 2), 0)
    beyond = lax.broadcasted_iota(jnp.int32, (height // 2, height // 2), 1)
    moved = ((beyond == at + 2) & (at % 4 < 2)).astype(F32).astype(LOW)
    all_ref[...] = first_times(rows, times(moved, rows).astype(LOW))
    count = out_ref.shape[0]
    out_ref[...] = all_ref[pl.ds(pl.multiple_of(lax.axis_index("dp") * count, 8), count), :]


def on_device(
    hidden_in, cotangent, qkv_weight, query_bias, value_bias, output_weight, output_bias,
    first_scale, first_shift, inner_weight, inner_bias, outer_weight, outer_bias,
    second_scale, second_shift, pool_weight, pool_bias, class_weight, class_bias,
    labels, ramp_index,
):
    rows, features = hidden_in.shape
    seqs = labels.shape[0]
    length = rows // seqs
    units = inner_weight.shape[1]
    dp = lax.axis_size("dp")
    ramps = lax.axis_size("ramp")
    pairs = features // LANES
    place = Place(dp, features)
    half = features // 2

    pool_other = swap_core(pool_weight)
    pool_bias_other = swap_core(pool_bias)
    class_weight = jnp.swapaxes(class_weight, 1, 2)
    class_other = swap_core(class_weight)
    class_bias_other = swap_core(class_bias)
    (
        mixed, probs, context, normal, first_low, spread, output, logits, slope, second_resid, outer_full,
        second_vector, *outer_parts,
    ) = call(
        partial(forward, place, length, ramps),
        [
            ((rows, 3 * features), LOW, FAR),
            ((seqs * pairs, length, 2 * length), LOW, FAR),
            ((rows, features), LOW, FAR),
            ((rows, features), F32, FAR),
            ((rows, features), LOW, FAR),
            ((rows, 1), F32, VMEM),
            ((rows, features), LOW, FAR),
            ((seqs, CLASSES), F32, VMEM),
            ((rows, units), LOW, FAR),
            ((rows, features), F32, FAR),
            ((rows, features), LOW, FAR),
            ((8 * (ramps + 1), features), F32, VMEM),
        ]
        + [((units // place.count + 16, half), LOW, FAR)]
        + [((units // place.count, half), LOW, FAR)] * (place.count - 1)
        + [((units + 16, half), LOW, FAR)],
        [
            (hidden_in, FAR),
            (qkv_weight, FAR),
            (query_bias, VMEM),
            (value_bias, VMEM),
            (output_weight, FAR),
            (output_bias, VMEM),
            (first_scale, VMEM),
            (first_shift, VMEM),
            (inner_weight, FAR),
            (inner_bias, VMEM),
            (outer_weight, FAR),
            (outer_bias, VMEM),
            (second_scale, VMEM),
            (second_shift, VMEM),
            (cotangent, FAR),
            (pool_weight, FAR),
            (pool_other, FAR),
            (pool_bias, VMEM),
            (pool_bias_other, VMEM),
            (class_weight, VMEM),
            (class_other, VMEM),
            (class_bias, VMEM),
            (class_bias_other, VMEM),
            (labels, SMEM),
            (ramp_index, SMEM),
        ],
        scratch=[
            pltpu.VMEM((rows, features), LOW),
            pltpu.VMEM((features, 3 * features), LOW),
            pltpu.VMEM((features, features), LOW),
            pltpu.VMEM((rows, 3 * features), LOW),
            pltpu.VMEM((seqs * pairs, length, 2 * length), LOW),
            pltpu.VMEM((rows, features), LOW),
            pltpu.VMEM((rows, features), F32),
            pltpu.VMEM((features, units), LOW),
            pltpu.VMEM((units, features), LOW),
            pltpu.VMEM((rows, features), LOW),
            pltpu.VMEM((1, features, features), LOW),
            pltpu.VMEM((1, features, features), LOW),
            pltpu.VMEM((rows, features), LOW),
            pltpu.VMEM((rows, units), LOW),
            pltpu.VMEM((rows, units), LOW),
            pltpu.VMEM((rows, features), F32),
            pltpu.VMEM((rows, features), LOW),
            pltpu.VMEM((rows, features), LOW),
            pltpu.VMEM((rows, features), F32),
            pltpu.VMEM((rows, 1), F32),
            pltpu.VMEM((16, half), LOW),
            pltpu.VMEM((16, half), LOW),
            pltpu.SemaphoreType.DMA((20 + 3 * (units // features) + 2 * dp,)),
        ],
        flops=2 * rows * features * (4 * features + 3 * units) + 8 * rows * features * length,
        nbytes=40 << 20,
        limit=VMEM_BYTES,
    )
    outer_chain = Chain(outer_parts[: place.count], outer_parts[place.count], OUTER_WAYS, 16)
    token = second_vector
    if place.fast:
        shared = [(outer_chain.own, units, 0), (outer_chain.got[0], units // place.count, 0)]
        results = outer_chain.gather(outer_chain.add(), 0, (16, shared))
        send, pair, token = combined(results[:1] + [(half, LOW, [(16, shared)])])
        keep, token = combined(results[1:], after=[token])
        outer_chain.send(send, keep)

    first_grad, first_vector, *inner_parts = call(
        partial(feed_backward, place, length),
        [((rows, features), F32, FAR), ((8, features), F32, VMEM)]
        + [((features // place.count, units // 2), LOW, NEAR)] * place.count
        + [((features, units // 2), LOW, NEAR)],
        [
            (outer_full, FAR),
            (slope, FAR),
            (outer_weight, FAR),
            (inner_weight, FAR),
            (second_resid, FAR),
            (first_low, FAR),
            (token, FAR),
        ],
        scratch=[
            pltpu.VMEM((rows, features), LOW),
            pltpu.VMEM((rows, units), LOW),
            pltpu.VMEM((units, features), LOW),
            pltpu.VMEM((features, units), LOW),
            pltpu.VMEM((rows, features), F32),
            pltpu.VMEM((features, units), LOW),
            pltpu.VMEM((rows, features), LOW),
            pltpu.SemaphoreType.DMA((8 + 3 * (units // features),)),
        ],
        flops=6 * rows * features * units,
        nbytes=25 << 20,
        limit=44 << 20,
    )
    inner_chain = Chain(inner_parts[: place.count], inner_parts[place.count], INNER_WAYS)
    token = first_vector

    def with_pair():
        height = pair.shape[0]
        shared = [(height, [(pair, 0, 0)]), (height, [(outer_chain.got[0], outer_chain.count, 0)])]
        return outer_chain.gather(outer_chain.add(), 0, *shared) + [(half, LOW, shared)]

    if place.fast:
        send, keep, pair, token = combined(with_pair(), after=[first_vector])
        outer_chain.send(send, keep)
    (early,) = call(
        collect_early,
        [((EARLY_ROWS, LANES), F32, VMEM)],
        [(first_vector, VMEM), (second_vector, VMEM), (token, FAR)],
        limit=SMALL_BYTES,
    )
    if place.fast:
        results = inner_chain.add()
        send, early, token = combined(results[:1], after=[token], rider=([early], [], (0,)))
        keep, token = combined(results[1:], after=[token])
        inner_chain.send(send, keep)

    mixed_grad, first_resid, mixed_vector, *qkv_parts = call(
        partial(attention_backward, place, length),
        [((rows, 3 * features), LOW, FAR), ((rows, features), F32, FAR), ((8, features), F32, VMEM)]
        + [((features // place.count, 4 * half), LOW, NEAR)] * place.count
        + [((features, 4 * half), LOW, NEAR)],
        [
            (first_grad, FAR),
            (normal, FAR),
            (spread, VMEM),
            (first_scale, VMEM),
            (output_weight, FAR),
            (context, FAR),
            (mixed, FAR),
            (probs, FAR),
            (hidden_in, FAR),
            (token, FAR),
        ],
        scratch=[
            pltpu.VMEM((rows, features), F32),
            pltpu.VMEM((rows, features), F32),
            pltpu.VMEM((features, features), LOW),
            pltpu.VMEM((rows, features), LOW),
            pltpu.VMEM((rows, features), LOW),
            pltpu.VMEM((rows, features), F32),
            pltpu.VMEM((rows, 3 * features), LOW),
            pltpu.VMEM((seqs * pairs, length, 2 * length), LOW),
            pltpu.VMEM((rows, features), LOW),
            pltpu.VMEM((rows, features), LOW),
            pltpu.VMEM((rows, 3 * features), LOW),
            pltpu.VMEM((features, 4 * features), LOW),
            pltpu.SemaphoreType.DMA((2, seqs)),
            pltpu.SemaphoreType.DMA((8,)),
        ],
        flops=20 * rows * features * length + 10 * rows * features * features,
        nbytes=12 << 20,
        limit=36 << 20,
    )
    qkv_chain = Chain(qkv_parts[: place.count], qkv_parts[place.count], QKV_WAYS)
    token = mixed_vector
    if place.fast:
        *sends, pair, early, token = combined(
            inner_chain.add() + with_pair(),
            after=[mixed_vector],
            rider=([early], [inner_chain.rider()], (0,)),
        )
        inner_chain.send(*sends[:2])
        outer_chain.send(*sends[2:])
    (late,) = call(
        collect_late,
        [((LATE_ROWS, LANES), F32, VMEM)],
        [(mixed_vector, VMEM), (mixed_vector, FAR)],
        limit=SMALL_BYTES,
    )
    late_other = swap_core(late)

    if place.fast:
        send, keep, late, token = combined(
            qkv_chain.add(), after=[token], rider=([late, late_other], [], (0,))
        )
        qkv_chain.send(send, keep)
    input_grad, token = call(
        input_gradient,
        [((rows, features), LOW, FAR), ((8, LANES), F32, FAR)],
        [(mixed_grad, FAR), (qkv_weight, FAR), (first_resid, FAR), (token, FAR)],
        scratch=[
            pltpu.VMEM((rows, 3 * features), LOW),
            pltpu.VMEM((features, 3 * features), LOW),
            pltpu.VMEM((rows, features), F32),
            pltpu.VMEM((rows, features), LOW),
            pltpu.SemaphoreType.DMA((8,)),
        ],
        flops=6 * rows * features * features,
        nbytes=10 << 20,
        limit=20 << 20,
    )

    if place.fast:
        early, token = combined([], after=[token], rider=([early], [inner_chain.rider()], ()))
        late, token = combined([], after=[token], rider=([late], [qkv_chain.rider()], ()))
        *sends, pair, token = combined(
            inner_chain.add() + qkv_chain.add() + with_pair(), after=[token], riders=[(0, early), (2, late)]
        )
        inner_chain.send(*sends[:2])
        qkv_chain.send(*sends[2:4])
        outer_chain.send(*sends[4:])
        early, token = combined([], after=[token], rider=([early], [inner_chain.rider()], ()))
        late, token = combined([], after=[token], rider=([late], [qkv_chain.rider()], ()))
        height = pair.shape[0]
        shared = [(height, [(pair, 0, 0)]), (height, [(outer_chain.got[0], outer_chain.count, 0)])]
        *sends, outer_sum, pair, token = combined(
            inner_chain.add() + qkv_chain.add() + outer_chain.add_last([half]) + [(half, LOW, shared)],
            after=[token],
            riders=[(0, early, True), (2, late)],
        )
        inner_chain.send(*sends[:2])
        qkv_chain.send(*sends[2:])
        pool_sum, token = call(
            pool_gradient,
            [((features // dp, features), F32, VMEM), ((8, LANES), F32, FAR)],
            [(pair, VMEM), (token, FAR)],
            scratch=[pltpu.VMEM((features, features), F32)],
            limit=SMALL_BYTES,
        )
        late, token = combined([], after=[token], rider=([late], [qkv_chain.rider()], ()))
        *sends, inner_sum, token = combined(
            qkv_chain.add() + inner_chain.add_last([units // 2]), after=[token], riders=[(0, late, True)]
        )
        early, token = combined([], after=[token], rider=([early], [inner_chain.rider(True)], ()))
        qkv_chain.send(*sends)
        qkv_sum, output_sum, late, token = combined(
            qkv_chain.add_last([3 * half, half]),
            rider=([late], [qkv_chain.rider(True)], ()),
        )
    else:
        early = add_over(early, list(range(1, dp)))
        late = add_over(late + late_other, list(range(1, dp)))
    if not place.fast:
        pair = outer_chain.own[units:] + outer_chain.got[0][units:]
        pair = lax.all_gather(pair, "dp")
        pair = pair.reshape(dp, 2, 2, 2, seqs // ramps, half)
        pair = jnp.moveaxis(pair, 1, 4).reshape(dp, 2, 2, seqs // ramps, features)
        states = pair[:, :, 0].reshape(-1, features)
        pre_grads = pair[:, :, 1].reshape(-1, features)
        own_rows = features // dp
        states = lax.dynamic_slice_in_dim(
            states, lax.axis_index("dp") * own_rows, own_rows, axis=1
        )
        pool_sum = first_times(states, pre_grads)
        (outer_sum,) = outer_chain.plain([half])
        (inner_sum,) = inner_chain.plain([units // 2])
        qkv_sum, output_sum = qkv_chain.plain([3 * half, half])
    early_other = swap_core(early)
    (
        rms, inner_bias_sum, outer_bias_sum, second_scale_sum, second_shift_sum,
        pool_bias_sum, class_sum, class_bias_sum,
        query_bias_sum, value_bias_sum, output_bias_sum, first_scale_sum, first_shift_sum,
    ) = call(
        partial(hand_out, features, rows * features * dp * ramps),
        [((3,), F32, VMEM), ((units,), F32, VMEM)]
        + [((features,), F32, VMEM)] * 3
        + [((1, features), F32, VMEM), ((CLASSES, 1, features), F32, VMEM), ((1, CLASSES), F32, VMEM)]
        + [((features,), F32, VMEM)] * 5,
        [(early, VMEM), (early_other, VMEM), (late, VMEM)],
        limit=SMALL_BYTES,
    )
    return (
        output,
        logits,
        rms,
        input_grad,
        qkv_sum,
        query_bias_sum,
        value_bias_sum,
        output_sum,
        output_bias_sum,
        first_scale_sum,
        first_shift_sum,
        inner_sum,
        inner_bias_sum,
        outer_sum,
        outer_bias_sum,
        second_scale_sum,
        second_shift_sum,
        pool_sum[None],
        pool_bias_sum,
        jnp.transpose(class_sum, (1, 2, 0)),
        class_bias_sum,
    )


def solution(mesh):
    whole = P(("dp", "ramp"), None)
    return jax.shard_map(
        on_device,
        mesh=mesh,
        in_specs=(whole, whole)
        + (P(),) * 13
        + (
            P("ramp", None, None),
            P("ramp", None),
            P("ramp", None, None),
            P("ramp", None),
            P(("dp", "ramp")),
            P(("dp", "ramp")),
        ),
        out_specs=(
            whole,
            whole,
            P(),
            whole,
            P("dp", "ramp"),
            P(),
            P(),
            P("dp", "ramp"),
            P(),
            P(),
            P(),
            P("dp", "ramp"),
            P(),
            P("dp", "ramp"),
            P(),
            P(),
            P(),
            P("ramp", "dp", None),
            P("ramp", None),
            P("ramp", None, None),
            P("ramp", None),
        ),
        check_vma=False,
    )
```

```python
from functools import partial

import jax
import jax.numpy as jnp
from jax import lax
from jax.experimental import pallas as pl
from jax.experimental.pallas import tpu as pltpu
from jax.sharding import PartitionSpec as P

HEADS = 12
CLASSES = 3
LANES = 128
EPS = 1e-06
F32 = jnp.float32
LOW = jnp.bfloat16
NEAR = pl.BlockSpec(memory_space=pltpu.VMEM)
VMEM = pltpu.VMEM
SMEM = pltpu.SMEM
FAR = pl.BlockSpec(memory_space=pl.ANY)
VMEM_BYTES = 60 * 1024 * 1024
SMALL_BYTES = 16 * 1024 * 1024


def times(left, right):
    return lax.dot_general(left, right, (((1,), (0,)), ((), ())), preferred_element_type=F32)


def times_transposed(left, right):
    return lax.dot_general(left, right, (((1,), (1,)), ((), ())), preferred_element_type=F32)


def first_times(left, right):
    return lax.dot_general(left, right, (((0,), (0,)), ((), ())), preferred_element_type=F32)


def row_sum(values):
    return jnp.sum(values, axis=-1, keepdims=True)


def column_sum(values):
    return jnp.sum(values, axis=0, keepdims=True)


def call(body, outs, args, scratch=(), flops=0, nbytes=0, limit=VMEM_BYTES):
    near_in = [number for number, (_, spec) in enumerate(args) if spec in (VMEM, SMEM)]
    near_out = [number for number, (_, _, spec) in enumerate(outs) if spec in (VMEM, SMEM)]
    copies = [args[number][1](args[number][0].shape, args[number][0].dtype) for number in near_in]
    copies += [outs[number][2](outs[number][0], outs[number][1]) for number in near_out]

    def kernel(*refs):
        ins, refs = list(refs[: len(args)]), refs[len(args) :]
        results, refs = list(refs[: len(outs)]), refs[len(outs) :]
        own, refs = refs[: len(scratch)], refs[len(scratch) :]
        held, sems = refs[:-1], refs[-1]
        moving = []
        for place, number in enumerate(near_in):
            moving.append(pltpu.make_async_copy(ins[number], held[place], sems.at[place]))
            ins[number] = held[place]
        for copy in moving:
            copy.start()

        def ready():
            while moving:
                moving.pop(0).wait()

        far = {}
        for place, number in enumerate(near_out, len(near_in)):
            far[place] = results[number]
            results[number] = held[place]
        mover = body(ready, *ins, *results, *own)
        ready()
        leaving = [
            pltpu.make_async_copy(held[place], target, sems.at[place]) for place, target in far.items()
        ]
        for copy in leaving:
            copy.start()
        if mover is not None:
            mover.finish()
        for copy in leaving:
            copy.wait()

    return pl.pallas_call(
        kernel,
        out_shape=tuple(jax.ShapeDtypeStruct(shape, kind) for shape, kind, _ in outs),
        in_specs=[NEAR if spec is NEAR else FAR for _, spec in args],
        out_specs=tuple([NEAR if spec is NEAR else FAR for _, _, spec in outs]),
        scratch_shapes=list(scratch)
        + copies
        + [pltpu.SemaphoreType.DMA((max(1, len(near_in) + len(near_out)),))],
        compiler_params=pltpu.CompilerParams(vmem_limit_bytes=limit),
        cost_estimate=pl.CostEstimate(flops=flops, bytes_accessed=nbytes, transcendentals=0),
    )(*[array for array, _ in args])


class Mover:
    def __init__(self, sems):
        self.sems = sems
        self.used = 0
        self.open = []

    def start(self, source, target):
        copy = pltpu.make_async_copy(source, target, self.sems.at[self.used])
        self.used += 1
        copy.start()
        return copy

    def out(self, source, target):
        self.open.append(self.start(source, target))

    def finish(self):
        for copy in self.open:
            copy.wait()


class Feed:
    def __init__(self, mover, pairs, depth):
        self.mover = mover
        self.pairs = pairs
        self.running = []
        self.done = 0
        for _ in range(depth):
            self.more()

    def more(self):
        if len(self.running) < len(self.pairs):
            self.running.append(self.mover.start(*self.pairs[len(self.running)]))

    def ahead(self):
        while len(self.running) < len(self.pairs):
            self.more()

    def need(self, count):
        while self.done < count:
            self.running[self.done].wait()
            self.done += 1
            self.more()


X, Y, NEAR_Z, FAR_Z = 1, 2, 4, 8
STEPS = 4
OUTER_WAYS = ((X, Y, NEAR_Z, FAR_Z), (NEAR_Z, Y, X, FAR_Z))
INNER_WAYS = OUTER_WAYS
QKV_WAYS = ((X, Y, NEAR_Z, FAR_Z), (NEAR_Z, X, Y, FAR_Z))


class Place:
    def __init__(self, dp, rows):
        self.dp = dp
        self.fast = dp == 1 << STEPS and rows % (16 * dp) == 0
        self.count = 4 if self.fast else 1

    def flip(self, position, ways, core):
        flips = []
        for way in ways:
            flips.append(sum(way[step] for step in range(STEPS) if not position >> (STEPS - 1 - step) & 1))
        return jnp.where(core == 0, flips[0], flips[1])

    def out(self, mover, source, columns, fars, core, size, ways, start=0):
        width = columns.size if isinstance(columns, pl.Slice) else columns.stop - columns.start
        target = slice(start, start + width)
        if not self.fast:
            there = slice(0, source.shape[0])
            if mover is None:
                fars[0][there, target] = source[:, columns]
            else:
                mover.out(source.at[:, columns], fars[0].at[there, target])
            return
        each = self.dp // len(fars)
        for position in range(self.dp):
            block = lax.axis_index("dp") ^ self.flip(position, ways, core)
            here = pl.ds(pl.multiple_of(block * size, 16), size)
            inside = position % each
            there = slice(inside * size, (inside + 1) * size)
            far = fars[position // each]
            if mover is None:
                far[there, target] = source[here, columns]
            else:
                mover.out(source.at[here, columns], far.at[there, target])

    def out_part(self, mover, source, columns, far, core, first, size, ways):
        if not self.fast:
            rows = slice(first * size, first * size + source.shape[0])
            mover.out(source.at[:, columns], far.at[rows, :])
            return
        for step in range(source.shape[0] // size):
            diff = lax.axis_index("dp") ^ (first + step)
            place = 0
            for number in range(STEPS):
                mask = jnp.where(core == 0, ways[0][number], ways[1][number])
                place = place * 2 + ((diff & mask) == 0).astype(jnp.int32)
            offset = pl.multiple_of(place * size, 16)
            mover.out(
                source.at[step * size : (step + 1) * size, columns], far.at[pl.ds(offset, size), :]
            )


def half_of(which, half):
    return pl.ds(pl.multiple_of(which * half, LANES), half)


def head_masks(rows):
    lane = lax.broadcasted_iota(jnp.int32, (rows, LANES), 1)
    left = (lane < LANES // 2).astype(F32).astype(LOW)
    right = (lane >= LANES // 2).astype(F32).astype(LOW)
    return left, right


def gelu_both(inner):
    density = jnp.exp(inner * inner * (-0.5)) * 0.3989422804014327
    below = 0.5 + 0.5 * lax.erf(inner * 0.7071067811865476)
    return inner * below, below + inner * density


def forward(
    place, length, ramp_count, ready,
    x_far, qkv_far, query_bias_ref, value_bias_ref, output_far, output_bias_ref,
    first_scale_ref, first_shift_ref, inner_far, inner_bias_ref, outer_far,
    outer_bias_ref, second_scale_ref, second_shift_ref, cot_far, pool_own_far, pool_other_far,
    pool_bias_own_ref, pool_bias_other_ref, class_own_ref, class_other_ref,
    class_bias_own_ref, class_bias_other_ref, labels_ref, ramps_ref,
    mixed_far, probs_far, context_far, normal_far, low_far, spread_ref,
    final_far, logits_ref, slope_far, resid_far, full_far, vector_ref, *refs,
):
    sends, owns, refs = refs[: place.count], refs[place.count : place.count + 1], refs[place.count + 1 :]
    (
    x_ref, qkv_ref, output_ref, mixed_ref, probs_ref, context_ref, normal_ref,
    inner_ref, outer_ref, cot_ref, pool_own_ref, pool_other_ref,
    final_ref, acted_ref, slope_ref, resid_ref, full_ref,
    low_ref, sum_ref, second_spread_ref, pair_own_ref, pair_send_ref, sems,
    ) = refs
    rows, features = x_ref.shape
    hidden_units = inner_ref.shape[1]
    seqs = rows // length
    pairs = features // LANES
    factor = (features // HEADS) ** (-0.5)
    core = lax.axis_index("ramp")
    mover = Mover(sems)
    parts = [slice(part * features, (part + 1) * features) for part in range(3)]
    steps = [
        slice(one * features, (one + 1) * features) for one in range(hidden_units // features)
    ]
    wanted = [(x_far, x_ref)]
    wanted += [(qkv_far.at[:, one], qkv_ref.at[:, one]) for one in parts]
    wanted += [(output_far, output_ref)]
    for one in steps:
        wanted += [(inner_far.at[:, one], inner_ref.at[:, one])]
        wanted += [(outer_far.at[one], outer_ref.at[one])]
    wanted += [(pool_own_far, pool_own_ref), (pool_other_far, pool_other_ref), (cot_far, cot_ref)]
    feed = Feed(mover, wanted, 3)
    ready()
    for part, columns in enumerate(parts):
        feed.need(2 + part)
        mixed = times(x_ref[...], qkv_ref[:, columns])
        if part == 0:
            mixed = mixed + query_bias_ref[...][None, :]
        if part == 2:
            mixed = mixed + value_bias_ref[...][None, :]
        mixed_ref[:, columns] = mixed.astype(LOW)
    feed.ahead()
    left, right = head_masks(length)
    left_t, right_t = left.T, right.T

    def one_sequence(seq, carry):
        here = pl.ds(pl.multiple_of(seq * length, length), length)
        for pair in range(pairs):
            start = pair * LANES
            query = mixed_ref[here, start : start + LANES]
            key = mixed_ref[here, features + start : features + start + LANES]
            value = mixed_ref[here, 2 * features + start : 2 * features + start + LANES]
            stacked = jnp.concatenate([query * left, query * right], axis=0)
            scores = times_transposed(key, stacked)
            top = jnp.max(scores, axis=0, keepdims=True)
            raised = jnp.exp((scores - top) * factor)
            probs = (raised * (1.0 / column_sum(raised))).astype(LOW)
            probs_ref[pl.ds(seq * pairs + pair, 1)] = probs[None]
            value_t = value.T
            both = jnp.concatenate([value_t * left_t, value_t * right_t], axis=1)
            tall = jnp.concatenate([probs[:, :length], probs[:, length:]], axis=0)
            context_t = times(both, tall).astype(LOW)
            context_ref[here, start : start + LANES] = context_t.T
        return carry

    lax.fori_loop(0, seqs, one_sequence, 0, unroll=2)
    feed.need(5)
    mover.out(mixed_ref, mixed_far)
    mover.out(probs_ref, probs_far)
    mover.out(context_ref, context_far)
    normal_ref[...] = times(context_ref[...], output_ref[...]) + output_bias_ref[...][None, :]
    hidden_square = jnp.zeros((1, features), F32)
    attended_square = jnp.zeros((1, features), F32)
    first_scale = first_scale_ref[...][None, :]
    first_shift = first_shift_ref[...][None, :]
    outer_bias = outer_bias_ref[...][None, :]
    for seq in range(seqs):
        here = slice(seq * length, (seq + 1) * length)
        hidden = x_ref[here, :].astype(F32)
        attended = normal_ref[here, :]
        residual = hidden + attended
        centred = residual - row_sum(residual) * (1.0 / features)
        spread = lax.rsqrt(row_sum(centred * centred) * (1.0 / features) + EPS)
        normal = centred * spread
        normal_ref[here, :] = normal
        spread_ref[here, :] = spread
        first = normal * first_scale + first_shift
        low_ref[here, :] = first.astype(LOW)
        sum_ref[here, :] = first + outer_bias
        hidden_square = hidden_square + column_sum(hidden * hidden)
        attended_square = attended_square + column_sum(attended * attended)
    mover.out(normal_ref, normal_far)
    mover.out(low_ref, low_far)

    feed.need(5 + 2 * len(steps))

    def inner_of(columns):
        return times(low_ref[...], inner_ref[:, columns]) + inner_bias_ref[columns][None, :]

    inner = inner_of(steps[0])
    for step, columns in enumerate(steps):
        following = inner_of(steps[step + 1]) if step + 1 < len(steps) else None
        acted, slope = gelu_both(inner)
        acted = acted.astype(LOW)
        acted_ref[:, columns] = acted
        slope_ref[:, columns] = slope.astype(LOW)
        sum_ref[...] += times(acted, outer_ref[columns, :])
        inner = following
    mover.out(slope_ref, slope_far)

    scale = second_scale_ref[...][None, :]
    shift = second_shift_ref[...][None, :]
    square = jnp.zeros((1, features), F32)
    leading = []
    for seq in range(seqs):
        here = slice(seq * length, (seq + 1) * length)
        residual = sum_ref[here, :]
        outer = residual - (normal_ref[here, :] * first_scale + first_shift)
        square = square + column_sum(outer * outer)
        centred = residual - row_sum(residual) * (1.0 / features)
        spread = lax.rsqrt(row_sum(centred * centred) * (1.0 / features) + EPS)
        normal = centred * spread
        sum_ref[here, :] = normal
        second_spread_ref[here, :] = spread
        final = (normal * scale + shift).astype(LOW)
        final_ref[here, :] = final
        leading.append(final[0:1, :].astype(F32))
    mover.out(final_ref, final_far)

    feed.need(len(wanted) - 1)
    leading = jnp.concatenate(leading + [jnp.zeros((8 - seqs, features), F32)], axis=0)
    states = leading.astype(LOW)
    row = lax.broadcasted_iota(jnp.int32, (8, 1), 0)
    ramp_of = jnp.full((8, 1), -1, jnp.int32)
    label_of = jnp.full((8, 1), -1, jnp.int32)
    for seq in range(seqs):
        ramp_of = jnp.where(row == seq, ramps_ref[seq], ramp_of)
        label_of = jnp.where(row == seq, labels_ref[seq], label_of)
    own = ramp_of == core
    pre_own = times(states, pool_own_ref[0]) + pool_bias_own_ref[...]
    pre_other = times(states, pool_other_ref[0]) + pool_bias_other_ref[...]
    pooled = jnp.tanh(jnp.where(own, pre_own, pre_other))
    pooled_low = pooled.astype(LOW)
    logits = jnp.where(
        own,
        times_transposed(pooled_low, class_own_ref[0]) + class_bias_own_ref[...],
        times_transposed(pooled_low, class_other_ref[0]) + class_bias_other_ref[...],
    )
    logits_ref[...] = logits[:seqs, :]
    raised = jnp.exp(logits - jnp.max(logits, axis=-1, keepdims=True))
    kind = lax.broadcasted_iota(jnp.int32, (8, CLASSES), 1)
    grads = raised / row_sum(raised) - (kind == label_of).astype(F32)
    grads = jnp.where(ramp_of >= 0, grads, 0.0)
    grads_high = grads.astype(LOW)
    grads_rest = (grads - grads_high.astype(F32)).astype(LOW)

    def from_logits(weight):
        return times(grads_high, weight) + times(grads_rest, weight)

    pooled_grad = jnp.where(own, from_logits(class_own_ref[0]), from_logits(class_other_ref[0]))
    pre_low = (pooled_grad * (1.0 - pooled * pooled)).astype(LOW).astype(F32)
    pre_own_low = jnp.where(own, pre_low, 0.0).astype(LOW)
    pre_other_low = jnp.where(own, 0.0, pre_low).astype(LOW)
    state_grad = times_transposed(pre_own_low, pool_own_ref[0])
    state_grad = state_grad + times_transposed(pre_other_low, pool_other_ref[0])
    chosen_row = lax.broadcasted_iota(jnp.int32, (8, 8), 0)
    chosen_seq = lax.broadcasted_iota(jnp.int32, (8, 8), 1)
    per_ramp = seqs // ramp_count
    for ref, which, top in ((pair_own_ref, core, 0), (pair_send_ref, 1 - core, 2 * per_ramp)):
        pick_states = jnp.zeros((8, 8), jnp.bool_)
        pick_grads = jnp.zeros((8, 8), jnp.bool_)
        for seq in range(seqs):
            rank = jnp.int32(0)
            for other in range(seq):
                rank = rank + (ramps_ref[other] == which).astype(jnp.int32)
            here = (chosen_seq == seq) & (ramps_ref[seq] == which)
            pick_states = pick_states | (here & (chosen_row == top + rank))
            pick_grads = pick_grads | (here & (chosen_row == top + per_ramp + rank))
        rows_of_pair = times(pick_states.astype(F32).astype(LOW), states)
        rows_of_pair = rows_of_pair + times(pick_grads.astype(F32).astype(LOW), pre_low.astype(LOW))
        folded = jnp.concatenate([rows_of_pair[:, : features // 2], rows_of_pair[:, features // 2 :]], axis=0)
        ref[...] = folded.astype(LOW)

    vector_ref[...] = jnp.zeros(vector_ref.shape, F32)
    for ramp in range(ramp_count):
        mask = ramp_of == ramp
        base = 8 * (ramp + 1)
        vector_ref[base : base + 1, :] = column_sum(jnp.where(mask, pre_low, 0.0))
        high = jnp.where(mask, grads_high.astype(F32), 0.0).astype(LOW)
        rest = jnp.where(mask, grads_rest.astype(F32), 0.0).astype(LOW)
        vector_ref[base + 1 : base + 1 + CLASSES, :] = first_times(high, pooled_low) + first_times(
            rest, pooled_low
        )
        vector_ref[base + 4 : base + 5, 0:CLASSES] = column_sum(jnp.where(mask, grads, 0.0))

    feed.need(len(wanted))
    scale_grad = jnp.zeros((1, features), F32)
    shift_grad = jnp.zeros((1, features), F32)
    bias_grad = jnp.zeros((1, features), F32)
    at_first = lax.broadcasted_iota(jnp.int32, (length, 1), 0) == 0
    for seq in range(seqs):
        here = slice(seq * length, (seq + 1) * length)
        final_grad = cot_ref[here, :].astype(F32)
        final_grad = final_grad + jnp.where(at_first, state_grad[seq : seq + 1, :], 0.0)
        normal = sum_ref[here, :]
        scale_grad = scale_grad + column_sum(final_grad * normal)
        shift_grad = shift_grad + column_sum(final_grad)
        scaled = final_grad * scale
        resid = second_spread_ref[here, :] * (
            scaled
            - row_sum(scaled) * (1.0 / features)
            - normal * (row_sum(scaled * normal) * (1.0 / features))
        )
        resid_ref[here, :] = resid
        low = resid.astype(LOW)
        full_ref[here, :] = low
        bias_grad = bias_grad + column_sum(low.astype(F32))
    mover.out(full_ref, full_far)
    mover.out(resid_ref, resid_far)
    below = pl.ds(hidden_units, 16)
    mover.out(pair_own_ref, owns[0].at[below])
    mover.out(pair_send_ref, sends[0].at[pl.ds(hidden_units // place.count, 16)])
    size = hidden_units // place.dp
    half = features // 2
    for step, columns in enumerate(steps):
        outer_ref[columns, :] = first_times(acted_ref[:, columns], full_ref[...]).astype(LOW)
        place.out_part(
            mover, outer_ref.at[columns], half_of(core, half), owns[0], core, step * features // size, size, OUTER_WAYS
        )
    place.out(mover, outer_ref, half_of(1 - core, half), sends, 1 - core, size, OUTER_WAYS)
    vector_ref[0:1, :] = bias_grad
    vector_ref[1:2, :] = scale_grad
    vector_ref[2:3, :] = shift_grad
    vector_ref[3:4, 0:1] = row_sum(hidden_square)
    vector_ref[3:4, 1:2] = row_sum(attended_square)
    vector_ref[3:4, 2:3] = row_sum(square)
    return mover


def feed_backward(
    place, length, ready,
    full_far, slope_far, outer_far, inner_far, resid_far, first_far, after_far,
    first_grad_far, vector_ref, *refs,
):
    sends, owns, refs = refs[: place.count], refs[place.count : place.count + 1], refs[place.count + 1 :]
    full_ref, slope_ref, outer_ref, inner_ref, sum_ref, weight_ref, first_ref, sems = refs
    rows, features = first_ref.shape
    core = lax.axis_index("ramp")
    hidden_units = slope_ref.shape[1]
    half = hidden_units // 2
    mover = Mover(sems)
    order = []
    for fars, who in ((sends, 1 - core), (owns, core)):
        for start in range(0, half, features):
            number = who * (half // features) + start // features
            columns = pl.ds(pl.multiple_of(number * features, LANES), features)
            order.append((fars, who, start, number, columns))
    wanted = [(full_far, full_ref)]
    for _, _, _, _, columns in order:
        wanted.append((outer_far.at[columns], outer_ref.at[columns]))
        wanted.append((slope_far.at[:, columns], slope_ref.at[:, columns]))
        if len(wanted) == 3:
            wanted.append((first_far, first_ref))
        wanted.append((inner_far.at[:, columns], inner_ref.at[:, columns]))
        if len(wanted) == 5:
            wanted.append((resid_far, sum_ref))
    feed = Feed(mover, wanted, 7)
    ready()
    vector_ref[...] = jnp.zeros(vector_ref.shape, F32)
    size = features // place.dp

    def acted_grad_of(step):
        return times_transposed(full_ref[...], outer_ref[order[step][4], :])

    feed.need(2)
    acted_grad = acted_grad_of(0)
    for step, (fars, who, start, number, columns) in enumerate(order):
        feed.need(min(6 + 3 * step + 1, len(wanted)))
        following = acted_grad_of(step + 1) if step + 1 < len(order) else None
        inner_grad = (slope_ref[:, columns].astype(F32) * acted_grad).astype(LOW)
        vector_ref[pl.ds(number, 1), :] = column_sum(inner_grad.astype(F32))
        sum_ref[...] += times_transposed(inner_grad, inner_ref[:, columns])
        here = slice(step * features, (step + 1) * features)
        weight_ref[:, here] = first_times(first_ref[...], inner_grad).astype(LOW)
        place.out(None, weight_ref, here, fars, who, size, INNER_WAYS, start)
        acted_grad = following
    mover.out(sum_ref, first_grad_far)
    return mover


def attention_backward(
    place, length, ready,
    first_grad_far, normal_far, spread_ref, first_scale_ref, output_far, context_far,
    mixed_far, probs_far, x_far, after_far,
    grad_far, first_resid_far, vector_ref, *refs,
):
    sends, owns, refs = refs[: place.count], refs[place.count : place.count + 1], refs[place.count + 1 :]
    (
        first_grad_ref, normal_ref, output_ref, context_ref, low_ref, first_resid_ref,
        mixed_ref, probs_ref, context_grad_ref, x_ref, grad_ref, weight_ref, sems, out_sems,
    ) = refs
    rows, features = context_grad_ref.shape
    seqs = rows // length
    core = lax.axis_index("ramp")
    pairs = features // LANES
    factor = (features // HEADS) ** (-0.5)
    half = features // 2
    size = features // place.dp
    left, right = head_masks(length)
    mover = Mover(out_sems)
    wanted = [
        (first_grad_far, first_grad_ref),
        (normal_far, normal_ref),
        (output_far, output_ref),
        (context_far, context_ref),
    ]
    feed = Feed(mover, wanted, len(wanted))

    def copies(seq):
        here = pl.ds(pl.multiple_of(seq * length, length), length)
        heads = pl.ds(seq * pairs, pairs)
        return (
            pltpu.make_async_copy(mixed_far.at[here], mixed_ref.at[here], sems.at[0, seq]),
            pltpu.make_async_copy(probs_far.at[heads], probs_ref.at[heads], sems.at[1, seq]),
        )

    for seq in range(seqs):
        for copy in copies(seq):
            copy.start()
    got_x = mover.start(x_far, x_ref)
    ready()
    feed.need(2)
    scale = first_scale_ref[...][None, :]
    zero = jnp.zeros((1, features), F32)
    sums = [zero, zero, zero]
    for seq in range(seqs):
        here = slice(seq * length, (seq + 1) * length)
        first_grad = first_grad_ref[here, :]
        normal = normal_ref[here, :]
        scaled = first_grad * scale
        resid = spread_ref[here, :] * (
            scaled
            - row_sum(scaled) * (1.0 / features)
            - normal * (row_sum(scaled * normal) * (1.0 / features))
        )
        first_resid_ref[here, :] = resid
        low = resid.astype(LOW)
        low_ref[here, :] = low
        sums[0] = sums[0] + column_sum(low.astype(F32))
        sums[1] = sums[1] + column_sum(first_grad * normal)
        sums[2] = sums[2] + column_sum(first_grad)
    mover.out(first_resid_ref, first_resid_far)
    feed.need(len(wanted))
    context_grad_ref[...] = times_transposed(low_ref[...], output_ref[...]).astype(LOW)
    columns = slice(3 * features, 4 * features)
    weight_ref[:, columns] = first_times(context_ref[...], low_ref[...]).astype(LOW)
    for fars, who in ((sends, 1 - core), (owns, core)):
        columns = pl.ds(pl.multiple_of(3 * features + who * half, LANES), half)
        place.out(None, weight_ref, columns, fars, who, size, QKV_WAYS, 3 * half)

    def one_sequence(seq, carry):
        here = pl.ds(pl.multiple_of(seq * length, length), length)
        for copy in copies(seq):
            copy.wait()
        for pair in range(pairs):
            start = pair * LANES
            query = mixed_ref[here, start : start + LANES]
            key = mixed_ref[here, features + start : features + start + LANES]
            value = mixed_ref[here, 2 * features + start : 2 * features + start + LANES]
            context_grad = context_grad_ref[here, start : start + LANES]
            queries = jnp.concatenate([query * left, query * right], axis=0)
            keys = jnp.concatenate([key * left, key * right], axis=0)
            grads = jnp.concatenate([context_grad * left, context_grad * right], axis=0)
            probs = probs_ref[pl.ds(seq * pairs + pair, 1)][0]
            probs_grad = times_transposed(value, grads)
            wide = probs.astype(F32)
            score_grad = wide * (probs_grad - column_sum(wide * probs_grad))
            score_grad = score_grad.astype(LOW)
            value_grad = times(probs, grads).astype(LOW)
            key_grad = (times(score_grad, queries) * factor).astype(LOW)
            turned = jnp.concatenate(
                [score_grad[:, :length].T, score_grad[:, length:].T], axis=1
            )
            query_grad = (times(turned, keys) * factor).astype(LOW)
            grad_ref[here, start : start + LANES] = query_grad
            grad_ref[here, features + start : features + start + LANES] = key_grad
            grad_ref[here, 2 * features + start : 2 * features + start + LANES] = value_grad
        return carry

    lax.fori_loop(0, seqs, one_sequence, 0, unroll=2)
    mover.out(grad_ref, grad_far)
    got_x.wait()
    for fars, who in ((sends, 1 - core), (owns, core)):
        for start, width in ((0, features), (features, half)):
            columns = pl.ds(pl.multiple_of(who * 3 * half + start, LANES), width)
            weight_ref[:, columns] = first_times(x_ref[...], grad_ref[:, columns]).astype(LOW)
            place.out(None, weight_ref, columns, fars, who, size, QKV_WAYS, start)
    vector_ref[...] = jnp.zeros(vector_ref.shape, F32)
    vector_ref[0:1, :] = column_sum(grad_ref[:, :features].astype(F32))
    vector_ref[1:2, :] = column_sum(grad_ref[:, 2 * features :].astype(F32))
    for number, one in enumerate(sums):
        vector_ref[2 + number : 3 + number, :] = one
    return mover


def input_gradient(
    ready,
    grad_far, qkv_far, resid_far, after_far,
    result_far, token_far,
    grad_ref, qkv_ref, resid_ref, result_ref, sems,
):
    mover = Mover(sems)
    features = resid_ref.shape[1]
    parts = [slice(part * features, (part + 1) * features) for part in range(3)]
    got = []
    for one in parts:
        got.append(
            (
                mover.start(grad_far.at[:, one], grad_ref.at[:, one]),
                mover.start(qkv_far.at[:, one], qkv_ref.at[:, one]),
            )
        )
    got_resid = mover.start(resid_far, resid_ref)
    total = None
    for columns, copies in zip(parts, got):
        for copy in copies:
            copy.wait()
        product = times_transposed(grad_ref[:, columns], qkv_ref[:, columns])
        total = product if total is None else total + product
    got_resid.wait()
    result_ref[...] = (resid_ref[...] + total).astype(LOW)
    mover.out(result_ref, result_far)
    return mover


def swap_core(values):
    return lax.ppermute(values, "ramp", [(0, 1), (1, 0)])


def shift(values, even, odd):
    dp = lax.axis_size("dp")
    pairs = []
    for one in range(dp):
        pairs.append((2 * one, 2 * (one ^ even)))
        pairs.append((2 * one + 1, 2 * (one ^ odd) + 1))
    return lax.ppermute(values, ("dp", "ramp"), pairs)


RIDERS = 16


def pack(ref, total, top, beside):
    high = total.astype(LOW)
    rest = (total - high.astype(F32)).astype(LOW)
    count = total.shape[0] // RIDERS
    if beside is not None:
        spots = rider_spots(ref.shape[0], total.shape[0])
        ref[:, beside:] = jnp.zeros((ref.shape[0], ref.shape[1] - beside), LOW)
        for values, number, row, start in spots:
            part = (high, rest)[values][number * RIDERS : (number + 1) * RIDERS, :]
            ref[row : row + RIDERS, beside + start : beside + start + LANES] = part
        return
    ref[top : top + RIDERS, :] = jnp.zeros((RIDERS, ref.shape[1]), LOW)
    for number in range(count):
        rows = slice(number * RIDERS, (number + 1) * RIDERS)
        for part, values in enumerate((high, rest)):
            start = (part * count + number) * LANES
            ref[top : top + RIDERS, start : start + LANES] = values[rows, :]


def rider_spots(height, rows):
    spots = []
    for number in range(rows // RIDERS):
        below, beside = number % (height // RIDERS), number // (height // RIDERS)
        spots.append((0, number, below * RIDERS, beside * LANES))
    return spots


def rider_width(height, rows):
    return rider_spots(height, rows)[-1][3] + LANES


def unpack(ref, count, top, beside):
    parts = [None] * count
    if beside is not None:
        for _, number, row, start in rider_spots(ref.shape[0], count * RIDERS):
            term = ref[row : row + RIDERS, beside + start : beside + start + LANES].astype(F32)
            parts[number] = term if parts[number] is None else parts[number] + term
    else:
        for number in range(count):
            start, rest = number * LANES, (count + number) * LANES
            high = ref[top : top + RIDERS, start : start + LANES].astype(F32)
            parts[number] = high + ref[top : top + RIDERS, rest : rest + LANES].astype(F32)
    return parts[0] if count == 1 else jnp.concatenate(parts, axis=0)


def combine(plan, count, rider, carried, ready, *refs):
    arrays, results = refs[:count], refs[count:]
    if rider is not None:
        plain, packed, into, beside = rider
        out_ref = results[len(plan)]
        total = None
        for number in plain:
            total = arrays[number][...] if total is None else total + arrays[number][...]
        for number, top, side in packed:
            total = total + unpack(arrays[number], total.shape[0] // RIDERS, top, side)
        out_ref[...] = total
    for number, (parts, result) in enumerate(zip(plan, results)):
        top = 0
        for rows, width, terms in parts:
            total_rows = None
            wide = len(terms) > 2 or result.dtype == F32
            for array, row, column in terms:
                term = arrays[array][row : row + rows, column : column + width]
                term = term.astype(F32) if wide else term
                total_rows = term if total_rows is None else total_rows + term
            result[top : top + rows, :width] = total_rows.astype(result.dtype)
            top += rows
        if rider is not None and number in into:
            pack(result, total, top, parts[0][1] if beside else None)
        if number in carried:
            sums, side = carried[number]
            pack(result, arrays[sums][...], top, parts[0][1] if side else None)


def combined(results, after=(), rider=None, riders=()):
    arrays = []

    def number(array):
        for place, one in enumerate(arrays):
            if one is array:
                return place
        arrays.append(array)
        return len(arrays) - 1

    plan = [
        [(rows, width, [(number(array), row, column) for array, row, column in terms]) for rows, terms in parts]
        for width, _, parts in results
    ]
    ride, extra, into, beside = None, [], (), False
    if rider is not None:
        plain, packed, into, *rest = rider
        beside = bool(rest)
        ride = ([number(one) for one in plain], [(number(one), *where) for one, *where in packed], into, beside)
        extra = [(plain[0].shape, F32, NEAR)]
    shapes = []
    carried = {}
    for place, sums, *rest in riders:
        carried[place] = (number(sums), bool(rest))
    for place, (width, kind, parts) in enumerate(results):
        height = sum(part[0] for part in parts)
        if place in carried and carried[place][1]:
            width = width + rider_width(height, arrays[carried[place][0]].shape[0])
        elif place in carried:
            height = height + RIDERS
        if place in into and beside:
            width = width + rider_width(height, plain[0].shape[0])
        elif place in into:
            height = height + RIDERS
        shapes.append(((height, width), kind))
    return call(
        partial(combine, plan, len(arrays) + len(after), ride, carried),
        [(shape, kind, NEAR) for shape, kind in shapes] + extra + [((8, LANES), F32, FAR)],
        [(array, NEAR) for array in arrays] + [(array, FAR) for array in after],
        nbytes=sum(8 * shape[0] * shape[1] for shape, _ in shapes),
        limit=SMALL_BYTES,
    )


class Chain:
    def __init__(self, sends, own, ways, spare=0):
        self.own = own
        self.ways = ways
        self.step = 0
        self.count = own.shape[0] - spare
        self.got = [swap_core(one) for one in sends]
        self.heights = [self.count // len(sends)] * len(sends)
        self.width = own.shape[1]

    def come(self, start, count):
        spans = []
        top = 0
        for one, height in zip(self.got, self.heights):
            low, high = max(start, top), min(start + count, top + height)
            if low < high:
                spans.append((high - low, (one, low - top, 0)))
            top += height
        return spans

    def parts(self, start, count):
        result = []
        for rows, place in self.come(start, count):
            result.append((rows, [(self.own, start, 0), place]))
            start += rows
        return result

    def add(self):
        rows = self.count // 2
        return [(self.width, LOW, self.parts(start, rows)) for start in (0, rows)]

    def send(self, array, keep):
        self.got, self.own = [shift(array, self.ways[0][self.step], self.ways[1][self.step])], keep
        self.step += 1
        self.count = keep.shape[0]
        self.heights = [self.count]

    def rider(self, beside=False):
        return (self.got[0], 0, self.width) if beside else (self.got[0], self.count, None)

    def gather(self, results, number, *terms):
        width, kind, parts = results[number]
        results[number] = (width, kind, parts + list(terms))
        return results

    def add_last(self, widths):
        results = []
        start = 0
        for width in widths:
            terms = [(array, 0, start) for array in (self.own, self.got[0])]
            results.append((width, F32, [(self.count, terms)]))
            start += width
        return results

    def plain(self, widths):
        total = (self.own[: self.count].astype(F32) + self.got[0][: self.count].astype(F32)).astype(LOW)
        rows = lax.psum_scatter(total, "dp", scatter_dimension=0, tiled=True).astype(F32)
        ends = [sum(widths[: one + 1]) for one in range(len(widths))]
        return [rows[:, end - width : end] for width, end in zip(widths, ends)]


EARLY_ROWS, LATE_ROWS = 96, 32


def put_rows(out_ref, place, row):
    for start in range(0, row.shape[1], LANES):
        out_ref[place : place + 1, :] = row[:, start : start + LANES]
        place += 1
    return place


def collect_late(ready, mixed_ref, after_far, out_ref):
    ready()
    out_ref[...] = jnp.zeros(out_ref.shape, F32)
    place = 0
    for number in range(5):
        place = put_rows(out_ref, place, mixed_ref[number : number + 1, :])


def collect_early(ready, first_ref, second_ref, after_far, out_ref):
    ready()
    out_ref[...] = jnp.zeros(out_ref.shape, F32)
    place = 0
    for number in range(first_ref.shape[0] // 2):
        place = put_rows(out_ref, place, first_ref[number : number + 1, :])
    for number in range(3):
        place = put_rows(out_ref, place, second_ref[number : number + 1, :])
    for base in (8, 16):
        for number in range(1 + CLASSES):
            place = put_rows(out_ref, place, second_ref[base + number : base + number + 1, :])
    for number in (3, 12, 20):
        place = put_rows(out_ref, place, second_ref[number : number + 1, :LANES])


def add_all(ready, *refs):
    ready()
    *refs, after_far, out_ref = refs
    total = refs[0][...]
    for ref in refs[1:]:
        total = total + ref[...]
    out_ref[...] = total


def add_over(values, masks, after=None):
    got = [shift(values, mask, mask) for mask in masks]
    (total,) = call(
        add_all,
        [(values.shape, values.dtype, VMEM)],
        [(one, VMEM) for one in [values] + got] + [((after or [values])[0], FAR)],
        limit=SMALL_BYTES,
    )
    return total


def take_rows(all_ref, place, ref, start, width):
    for column in range(0, width, LANES):
        ref[pl.ds(start + column, LANES)] = all_ref[place, :]
        place += 1
    return place


def hand_out(features, entries, ready, all_ref, other_ref, late_ref, late_other_ref, *outs):
    ready()
    all_ref[...] += other_ref[...]
    late_ref[...] += late_other_ref[...]
    place = 0
    for ref in outs[8:]:
        place = take_rows(late_ref, place, ref, 0, features)
    outs = outs[:8]
    core = lax.axis_index("ramp")
    rms_ref, inner_ref, outer_ref, second_scale_ref, second_shift_ref = outs[:5]
    pool_ref, class_ref, class_bias_ref = outs[5:]
    place = 0
    for ref in (inner_ref, outer_ref, second_scale_ref, second_shift_ref):
        place = take_rows(all_ref, place, ref, 0, ref.shape[0])
    step = features // LANES
    size = step * (1 + CLASSES)
    for column in range(step):
        at = column * LANES
        first = all_ref[place + column : place + column + 1, :]
        second = all_ref[place + size + column : place + size + column + 1, :]
        pool_ref[:, at : at + LANES] = jnp.where(core == 0, first, second)
        for kind in range(CLASSES):
            row = place + (1 + kind) * step + column
            first = all_ref[row : row + 1, :]
            second = all_ref[row + size : row + size + 1, :]
            class_ref[kind, :, at : at + LANES] = jnp.where(core == 0, first, second)
    place += 2 * size
    rms_ref[...] = jnp.sqrt(all_ref[place, :] * (1.0 / entries))[: rms_ref.shape[0]]
    first = all_ref[place + 1 : place + 2, :CLASSES]
    second = all_ref[place + 2 : place + 3, :CLASSES]
    class_bias_ref[...] = jnp.where(core == 0, first, second)


def pool_gradient(ready, pair_ref, after_far, out_ref, token_far, all_ref):
    ready()
    height, half = pair_ref.shape
    blocks = pair_ref[...].astype(F32).reshape(height // 16, 16, half)
    rows = jnp.concatenate([blocks[:, 0:8, :], blocks[:, 8:16, :]], axis=2)
    rows = rows.reshape(height // 2, 2 * half).astype(LOW)
    at = lax.broadcasted_iota(jnp.int32, (height // 2, height // 2), 0)
    beyond = lax.broadcasted_iota(jnp.int32, (height // 2, height // 2), 1)
    moved = ((beyond == at + 2) & (at % 4 < 2)).astype(F32).astype(LOW)
    all_ref[...] = first_times(rows, times(moved, rows).astype(LOW))
    count = out_ref.shape[0]
    out_ref[...] = all_ref[pl.ds(pl.multiple_of(lax.axis_index("dp") * count, 8), count), :]


def on_device(
    hidden_in, cotangent, qkv_weight, query_bias, value_bias, output_weight, output_bias,
    first_scale, first_shift, inner_weight, inner_bias, outer_weight, outer_bias,
    second_scale, second_shift, pool_weight, pool_bias, class_weight, class_bias,
    labels, ramp_index,
):
    rows, features = hidden_in.shape
    seqs = labels.shape[0]
    length = rows // seqs
    units = inner_weight.shape[1]
    dp = lax.axis_size("dp")
    ramps = lax.axis_size("ramp")
    pairs = features // LANES
    place = Place(dp, features)
    half = features // 2

    pool_other = swap_core(pool_weight)
    pool_bias_other = swap_core(pool_bias)
    class_weight = jnp.swapaxes(class_weight, 1, 2)
    class_other = swap_core(class_weight)
    class_bias_other = swap_core(class_bias)
    (
        mixed, probs, context, normal, first_low, spread, output, logits, slope, second_resid, outer_full,
        second_vector, *outer_parts,
    ) = call(
        partial(forward, place, length, ramps),
        [
            ((rows, 3 * features), LOW, FAR),
            ((seqs * pairs, length, 2 * length), LOW, FAR),
            ((rows, features), LOW, FAR),
            ((rows, features), F32, FAR),
            ((rows, features), LOW, FAR),
            ((rows, 1), F32, VMEM),
            ((rows, features), LOW, FAR),
            ((seqs, CLASSES), F32, VMEM),
            ((rows, units), LOW, FAR),
            ((rows, features), F32, FAR),
            ((rows, features), LOW, FAR),
            ((8 * (ramps + 1), features), F32, VMEM),
        ]
        + [((units // place.count + 16, half), LOW, FAR)]
        + [((units // place.count, half), LOW, FAR)] * (place.count - 1)
        + [((units + 16, half), LOW, FAR)],
        [
            (hidden_in, FAR),
            (qkv_weight, FAR),
            (query_bias, VMEM),
            (value_bias, VMEM),
            (output_weight, FAR),
            (output_bias, VMEM),
            (first_scale, VMEM),
            (first_shift, VMEM),
            (inner_weight, FAR),
            (inner_bias, VMEM),
            (outer_weight, FAR),
            (outer_bias, VMEM),
            (second_scale, VMEM),
            (second_shift, VMEM),
            (cotangent, FAR),
            (pool_weight, FAR),
            (pool_other, FAR),
            (pool_bias, VMEM),
            (pool_bias_other, VMEM),
            (class_weight, VMEM),
            (class_other, VMEM),
            (class_bias, VMEM),
            (class_bias_other, VMEM),
            (labels, SMEM),
            (ramp_index, SMEM),
        ],
        scratch=[
            pltpu.VMEM((rows, features), LOW),
            pltpu.VMEM((features, 3 * features), LOW),
            pltpu.VMEM((features, features), LOW),
            pltpu.VMEM((rows, 3 * features), LOW),
            pltpu.VMEM((seqs * pairs, length, 2 * length), LOW),
            pltpu.VMEM((rows, features), LOW),
            pltpu.VMEM((rows, features), F32),
            pltpu.VMEM((features, units), LOW),
            pltpu.VMEM((units, features), LOW),
            pltpu.VMEM((rows, features), LOW),
            pltpu.VMEM((1, features, features), LOW),
            pltpu.VMEM((1, features, features), LOW),
            pltpu.VMEM((rows, features), LOW),
            pltpu.VMEM((rows, units), LOW),
            pltpu.VMEM((rows, units), LOW),
            pltpu.VMEM((rows, features), F32),
            pltpu.VMEM((rows, features), LOW),
            pltpu.VMEM((rows, features), LOW),
            pltpu.VMEM((rows, features), F32),
            pltpu.VMEM((rows, 1), F32),
            pltpu.VMEM((16, half), LOW),
            pltpu.VMEM((16, half), LOW),
            pltpu.SemaphoreType.DMA((20 + 3 * (units // features) + 2 * dp,)),
        ],
        flops=2 * rows * features * (4 * features + 3 * units) + 8 * rows * features * length,
        nbytes=40 << 20,
        limit=VMEM_BYTES,
    )
    outer_chain = Chain(outer_parts[: place.count], outer_parts[place.count], OUTER_WAYS, 16)
    token = second_vector
    if place.fast:
        shared = [(outer_chain.own, units, 0), (outer_chain.got[0], units // place.count, 0)]
        results = outer_chain.gather(outer_chain.add(), 0, (16, shared))
        send, pair, token = combined(results[:1] + [(half, LOW, [(16, shared)])])
        keep, token = combined(results[1:], after=[token])
        outer_chain.send(send, keep)

    first_grad, first_vector, *inner_parts = call(
        partial(feed_backward, place, length),
        [((rows, features), F32, FAR), ((8, features), F32, VMEM)]
        + [((features // place.count, units // 2), LOW, NEAR)] * place.count
        + [((features, units // 2), LOW, NEAR)],
        [
            (outer_full, FAR),
            (slope, FAR),
            (outer_weight, FAR),
            (inner_weight, FAR),
            (second_resid, FAR),
            (first_low, FAR),
            (token, FAR),
        ],
        scratch=[
            pltpu.VMEM((rows, features), LOW),
            pltpu.VMEM((rows, units), LOW),
            pltpu.VMEM((units, features), LOW),
            pltpu.VMEM((features, units), LOW),
            pltpu.VMEM((rows, features), F32),
            pltpu.VMEM((features, units), LOW),
            pltpu.VMEM((rows, features), LOW),
            pltpu.SemaphoreType.DMA((8 + 3 * (units // features),)),
        ],
        flops=6 * rows * features * units,
        nbytes=25 << 20,
        limit=44 << 20,
    )
    inner_chain = Chain(inner_parts[: place.count], inner_parts[place.count], INNER_WAYS)
    token = first_vector

    def with_pair():
        height = pair.shape[0]
        shared = [(height, [(pair, 0, 0)]), (height, [(outer_chain.got[0], outer_chain.count, 0)])]
        return outer_chain.gather(outer_chain.add(), 0, *shared) + [(half, LOW, shared)]

    if place.fast:
        send, keep, pair, token = combined(with_pair(), after=[first_vector])
        outer_chain.send(send, keep)
    (early,) = call(
        collect_early,
        [((EARLY_ROWS, LANES), F32, VMEM)],
        [(first_vector, VMEM), (second_vector, VMEM), (token, FAR)],
        limit=SMALL_BYTES,
    )
    if place.fast:
        results = inner_chain.add()
        send, early, token = combined(results[:1], after=[token], rider=([early], [], (0,)))
        keep, token = combined(results[1:], after=[token])
        inner_chain.send(send, keep)

    mixed_grad, first_resid, mixed_vector, *qkv_parts = call(
        partial(attention_backward, place, length),
        [((rows, 3 * features), LOW, FAR), ((rows, features), F32, FAR), ((8, features), F32, VMEM)]
        + [((features // place.count, 4 * half), LOW, NEAR)] * place.count
        + [((features, 4 * half), LOW, NEAR)],
        [
            (first_grad, FAR),
            (normal, FAR),
            (spread, VMEM),
            (first_scale, VMEM),
            (output_weight, FAR),
            (context, FAR),
            (mixed, FAR),
            (probs, FAR),
            (hidden_in, FAR),
            (token, FAR),
        ],
        scratch=[
            pltpu.VMEM((rows, features), F32),
            pltpu.VMEM((rows, features), F32),
            pltpu.VMEM((features, features), LOW),
            pltpu.VMEM((rows, features), LOW),
            pltpu.VMEM((rows, features), LOW),
            pltpu.VMEM((rows, features), F32),
            pltpu.VMEM((rows, 3 * features), LOW),
            pltpu.VMEM((seqs * pairs, length, 2 * length), LOW),
            pltpu.VMEM((rows, features), LOW),
            pltpu.VMEM((rows, features), LOW),
            pltpu.VMEM((rows, 3 * features), LOW),
            pltpu.VMEM((features, 4 * features), LOW),
            pltpu.SemaphoreType.DMA((2, seqs)),
            pltpu.SemaphoreType.DMA((8,)),
        ],
        flops=20 * rows * features * length + 10 * rows * features * features,
        nbytes=12 << 20,
        limit=36 << 20,
    )
    qkv_chain = Chain(qkv_parts[: place.count], qkv_parts[place.count], QKV_WAYS)
    token = mixed_vector
    if place.fast:
        *sends, pair, early, token = combined(
            inner_chain.add() + with_pair(),
            after=[mixed_vector],
            rider=([early], [inner_chain.rider()], (0,)),
        )
        inner_chain.send(*sends[:2])
        outer_chain.send(*sends[2:])
    (late,) = call(
        collect_late,
        [((LATE_ROWS, LANES), F32, VMEM)],
        [(mixed_vector, VMEM), (mixed_vector, FAR)],
        limit=SMALL_BYTES,
    )

    if place.fast:
        results = qkv_chain.add()
        send, late, token = combined(results[:1], after=[token], rider=([late], [], (0,)))
        keep, token = combined(results[1:], after=[token])
        qkv_chain.send(send, keep)
    input_grad, token = call(
        input_gradient,
        [((rows, features), LOW, FAR), ((8, LANES), F32, FAR)],
        [(mixed_grad, FAR), (qkv_weight, FAR), (first_resid, FAR), (token, FAR)],
        scratch=[
            pltpu.VMEM((rows, 3 * features), LOW),
            pltpu.VMEM((features, 3 * features), LOW),
            pltpu.VMEM((rows, features), F32),
            pltpu.VMEM((rows, features), LOW),
            pltpu.SemaphoreType.DMA((8,)),
        ],
        flops=6 * rows * features * features,
        nbytes=10 << 20,
        limit=20 << 20,
    )

    if place.fast:
        early, token = combined([], after=[token], rider=([early], [inner_chain.rider()], ()))
        late, token = combined([], after=[token], rider=([late], [qkv_chain.rider()], ()))
        *sends, pair, token = combined(
            inner_chain.add() + qkv_chain.add() + with_pair(), after=[token], riders=[(0, early), (2, late)]
        )
        inner_chain.send(*sends[:2])
        qkv_chain.send(*sends[2:4])
        outer_chain.send(*sends[4:])
        early, token = combined([], after=[token], rider=([early], [inner_chain.rider()], ()))
        late, token = combined([], after=[token], rider=([late], [qkv_chain.rider()], ()))
        height = pair.shape[0]
        shared = [(height, [(pair, 0, 0)]), (height, [(outer_chain.got[0], outer_chain.count, 0)])]
        *sends, outer_sum, pair, token = combined(
            inner_chain.add() + qkv_chain.add() + outer_chain.add_last([half]) + [(half, LOW, shared)],
            after=[token],
            riders=[(0, early, True), (2, late)],
        )
        inner_chain.send(*sends[:2])
        qkv_chain.send(*sends[2:])
        pool_sum, token = call(
            pool_gradient,
            [((features // dp, features), F32, VMEM), ((8, LANES), F32, FAR)],
            [(pair, VMEM), (token, FAR)],
            scratch=[pltpu.VMEM((features, features), F32)],
            limit=SMALL_BYTES,
        )
        late, token = combined([], after=[token], rider=([late], [qkv_chain.rider()], ()))
        *sends, inner_sum, token = combined(
            qkv_chain.add() + inner_chain.add_last([units // 2]), after=[token], riders=[(0, late, True)]
        )
        early, token = combined([], after=[token], rider=([early], [inner_chain.rider(True)], ()))
        qkv_chain.send(*sends)
        qkv_sum, output_sum, late, token = combined(
            qkv_chain.add_last([3 * half, half]),
            rider=([late], [qkv_chain.rider(True)], ()),
        )
    else:
        early = add_over(early, list(range(1, dp)))
        late = add_over(late, list(range(1, dp)))
    if not place.fast:
        pair = outer_chain.own[units:] + outer_chain.got[0][units:]
        pair = lax.all_gather(pair, "dp")
        pair = pair.reshape(dp, 2, 2, 2, seqs // ramps, half)
        pair = jnp.moveaxis(pair, 1, 4).reshape(dp, 2, 2, seqs // ramps, features)
        states = pair[:, :, 0].reshape(-1, features)
        pre_grads = pair[:, :, 1].reshape(-1, features)
        own_rows = features // dp
        states = lax.dynamic_slice_in_dim(
            states, lax.axis_index("dp") * own_rows, own_rows, axis=1
        )
        pool_sum = first_times(states, pre_grads)
        (outer_sum,) = outer_chain.plain([half])
        (inner_sum,) = inner_chain.plain([units // 2])
        qkv_sum, output_sum = qkv_chain.plain([3 * half, half])
    early_other = swap_core(early)
    late_other = swap_core(late)
    (
        rms, inner_bias_sum, outer_bias_sum, second_scale_sum, second_shift_sum,
        pool_bias_sum, class_sum, class_bias_sum,
        query_bias_sum, value_bias_sum, output_bias_sum, first_scale_sum, first_shift_sum,
    ) = call(
        partial(hand_out, features, rows * features * dp * ramps),
        [((3,), F32, VMEM), ((units,), F32, VMEM)]
        + [((features,), F32, VMEM)] * 3
        + [((1, features), F32, VMEM), ((CLASSES, 1, features), F32, VMEM), ((1, CLASSES), F32, VMEM)]
        + [((features,), F32, VMEM)] * 5,
        [(early, VMEM), (early_other, VMEM), (late, VMEM), (late_other, VMEM)],
        limit=SMALL_BYTES,
    )
    return (
        output,
        logits,
        rms,
        input_grad,
        qkv_sum,
        query_bias_sum,
        value_bias_sum,
        output_sum,
        output_bias_sum,
        first_scale_sum,
        first_shift_sum,
        inner_sum,
        inner_bias_sum,
        outer_sum,
        outer_bias_sum,
        second_scale_sum,
        second_shift_sum,
        pool_sum[None],
        pool_bias_sum,
        jnp.transpose(class_sum, (1, 2, 0)),
        class_bias_sum,
    )


def solution(mesh):
    whole = P(("dp", "ramp"), None)
    return jax.shard_map(
        on_device,
        mesh=mesh,
        in_specs=(whole, whole)
        + (P(),) * 13
        + (
            P("ramp", None, None),
            P("ramp", None),
            P("ramp", None, None),
            P("ramp", None),
            P(("dp", "ramp")),
            P(("dp", "ramp")),
        ),
        out_specs=(
            whole,
            whole,
            P(),
            whole,
            P("dp", "ramp"),
            P(),
            P(),
            P("dp", "ramp"),
            P(),
            P(),
            P(),
            P("dp", "ramp"),
            P(),
            P("dp", "ramp"),
            P(),
            P(),
            P(),
            P("ramp", "dp", None),
            P("ramp", None),
            P("ramp", None, None),
            P("ramp", None),
        ),
        check_vma=False,
    )
```
